32 devices in a mesh: grp: 4 (over x, core), ctx: 2 (over y), wsh: 4 (over z).
Axes of the slice: x: 2, y: 2, z: 4, core: 2. Of those that a mesh axis runs over, the one named last changes fastest.
Arguments:
- tokens: bfloat16 [16, 256, 1024], P(('grp', 'wsh'), 'ctx'), may hold values from -6 to 6
- cotangent: bfloat16 [16, 256, 1024], P(('grp', 'wsh'), 'ctx'), may hold values from -6 to 6
- norm_gain: bfloat16 [1024], P(('grp', 'ctx', 'wsh')), may hold values from 0.5 to 1.5
- project_weight: bfloat16 [1024, 3072], P(('grp', 'ctx', 'wsh')), may hold values from -0.1875 to 0.1875
- output_weight: bfloat16 [1024, 1024], P(('grp', 'ctx', 'wsh')), may hold values from -1 to 1
- centroids: bfloat16 [2, 1024], P(None, ('grp', 'ctx', 'wsh')), may hold values from -0.125 to 0.125
- expert_up: bfloat16 [2, 2, 1024, 4096], P('ctx', None, 'grp', 'wsh'), may hold values from -0.1875 to 0.1875
- expert_down: bfloat16 [2, 2, 4096, 1024], P('ctx', None, 'wsh', 'grp'), may hold values from -0.09375 to 0.09375
- sequence_lengths: int32 [16, 3], P(('grp', 'wsh')), may hold values from 1 to 128, 256 in all within a row
- block_order: int32 [16, 2], P(('grp', 'wsh')), may hold values from 0 to 1, each once within a row
- routes: int32 [16, 256, 1], P(('grp', 'wsh'), 'ctx'), may hold values from 0 to 1; in each aligned block of 128 rows (0 to 127, 128 to 255, ..., all dimensions but the last counted through in order) at most 80 rows name the same one
Outputs:
- output: bfloat16 [16, 256, 1024], P(('grp', 'wsh'), 'ctx')
- tokens_grad: float32 [16, 256, 1024], P(('grp', 'wsh'), 'ctx')
- norm_gain_grad: float32 [1024], P(('grp', 'ctx', 'wsh'))
- project_weight_grad: float32 [1024, 3072], P(('grp', 'ctx', 'wsh'))
- output_weight_grad: float32 [1024, 1024], P(('grp', 'ctx', 'wsh'))
- centroids_grad: float32 [2, 1024], P(None, ('grp', 'ctx', 'wsh'))
- expert_up_grad: float32 [2, 2, 1024, 4096], P('ctx', None, 'grp', 'wsh')
- expert_down_grad: float32 [2, 2, 4096, 1024], P('ctx', None, 'wsh', 'grp')
The draws below stay inside these ranges and needn't reach their ends.
Inputs may be any that keep to these rules, and one draw needn't show every extreme that they name: `routes`: within the rows of one device no expert is named by more than 80 rows, and in some device's rows one expert is named by exactly 80. `sequence_lengths`: each group's lengths sum to 256; each group's longest sequence has exactly 128 tokens. `block_order`: each group's row is a permutation of the 2 block numbers.
All inputs are finite; a program needn't handle non-finite values.
Results may differ from the reference program's by a relative error of at most 0.02.
Values may be sent and summed in bfloat16 or wider, within the bound.
A program may use at most 192 MiB of HBM per device.

```python
import math
import jax
import jax.numpy as jnp
import numpy as np
from jax import lax

D = 1024
HEADS = 16
HDIM = 64
FF = 4096
TOK_DEV = 128
BLK = 128
GROUPS = 16
GTOK = 256
NBLK = 2
MAXLEN = 128
NSEQ = 3
EXPERTS = 2
CAP = 80
N_CTX = 2


def block_scale(rng, extent, shards, low, high):
    gain, own = 1.0, jax.random.fold_in(rng, 6)
    for dim, blocks in shards:
        steps = jnp.exp(jax.random.uniform(jax.random.fold_in(own, dim), (blocks,), jnp.float32, low / len(shards), high / len(shards)))
        gain = gain * jnp.repeat(steps, extent[dim] // blocks).reshape([-1 if axis == dim else 1 for axis in range(len(extent))])
    return gain


def profile(amount, total, limit, skew):
    loads = [(1 << 20) // math.isqrt(rank ** skew) + 1 for rank in range(2, amount + 1)]
    surplus, holding = total - limit - (amount - 1), [1] * (amount - 1)
    while surplus > 0:
        movable = [i for i in range(amount - 1) if holding[i] < limit]
        pool, left = sum([loads[i] for i in movable]), surplus
        for i in movable:
            more = min(limit - holding[i], max(1, left * loads[i] // pool), surplus)
            holding[i] = holding[i] + more
            surplus = surplus - more
    return np.array([limit] + holding)


def uneven_parts(key, number_of, total, reach, lean):
    if number_of == 2:
        one = jax.random.randint(key, (), max(1, total - reach), min(reach, total - 1) + 1)
        return jnp.stack([one, total - one])
    sizes = jnp.asarray(profile(number_of, total, reach, lean), jnp.int32)
    couples = (number_of - 1) // 2
    donor, receiver = sizes[1:1 + 2 * couples:2], sizes[2:2 + 2 * couples:2]
    margin = jnp.minimum(donor - 1, reach - receiver)
    passed = jax.random.randint(jax.random.fold_in(key, 1), (couples,), 0, 1 << 20) % (margin + 1)
    sizes = sizes.at[1:1 + 2 * couples:2].set(donor - passed).at[2:2 + 2 * couples:2].set(receiver + passed)
    return sizes[jax.random.permutation(jax.random.fold_in(key, 2), number_of)]


def deal_out(key, own, number, rows, count, top, reach, skew):
    order = jax.random.permutation(key, count)
    heavy_load, ordinary = shares(count, rows * top, reach, skew, True), shares(count, rows * top, reach, skew, False)
    places = jnp.arange(count)

    def named(tallies, offset_by):
        used = int((tallies > 0).sum())
        fixed = max(1, used // 4)
        moved = fixed + (places - fixed + offset_by * (used - fixed)) % max(1, count - fixed)
        return jnp.zeros((count,), jnp.int32).at[order[jnp.where(places < fixed, places, moved)]].set(jnp.asarray(tallies, jnp.int32))

    tallies = jnp.where(number % 4 == 0, named(heavy_load, number // 4), named(ordinary, number - number // 4 - 1))
    mixed = jax.random.permutation(jax.random.fold_in(own, 3), count)
    source_of, sink = mixed[0:count // 2 * 2:2], mixed[1:count // 2 * 2:2]
    room = jnp.minimum(tallies[source_of] - 1, reach - tallies[sink]) // 2
    room = jnp.where((source_of == order[0]) | (sink == order[0]) | (tallies[sink] == 0), 0, jnp.maximum(room, 0))
    moved = jax.random.randint(jax.random.fold_in(own, 4), (count // 2,), 0, 1 << 20) % (room + 1)
    tallies = tallies.at[source_of].add(-moved).at[sink].add(moved)
    items = jnp.searchsorted(jnp.cumsum(tallies), jnp.arange(rows * top), side="right").astype(jnp.int32)
    listing = items.reshape(top, rows).T
    listing = listing[jax.random.permutation(jax.random.fold_in(own, 1), rows)]
    offset_by = jax.random.randint(jax.random.fold_in(own, 2), (rows, 1), 0, top)
    return jnp.take_along_axis(listing, (jnp.arange(top)[None, :] + offset_by) % top, axis=1)


def shares(count, total, bound, skew, full):
    loads = [(1 << 20) // math.isqrt(standing ** skew) + 1 for standing in range(1, count + 1)]
    largest = bound if full else min(bound, max(-(-total // count), total * loads[0] // sum(loads)))
    least = 1 if total - largest >= count - 1 else 0
    given, surplus = [largest] + [least] * (count - 1), total - largest - least * (count - 1)
    while surplus > 0:
        movable = [i for i in range(1, count) if given[i] < largest] or [i for i in range(1, count) if given[i] < bound]
        whole, remaining = sum([loads[i] for i in movable]), surplus
        for i in movable:
            extra = min(bound - given[i], max(1, remaining * loads[i] // whole), surplus)
            given[i] = given[i] + extra
            surplus = surplus - extra
    return np.array(given)


def noise(rng, extent, spread, limit, pieces=(), kind=jnp.bfloat16):
    level = block_scale(rng, extent, pieces, -0.22, 0.18) if pieces else 1.0
    values = jax.random.normal(rng, extent, jnp.float32) * spread * level
    return jnp.minimum(jnp.maximum(values, -limit), limit).astype(kind)


def setup_inputs(seed: int = 0) -> dict:
    keys = jax.random.split(jax.random.key(seed), 12)
    tokens = noise(keys[0], (GROUPS, GTOK, D), 1.0, 6.0, ((0, 16), (1, 2)))
    cotangent = noise(keys[1], (GROUPS, GTOK, D), 1.0, 6.0, ((0, 16), (1, 2)))
    norm_gain = jnp.clip(1.0 + 0.1 * jax.random.normal(keys[2], (D,), jnp.float32), 0.5, 1.5).astype(jnp.bfloat16)
    project_weight = noise(keys[3], (D, 3 * D), D ** -0.5, 0.1875, ((0, 32),))
    output_weight = noise(keys[4], (D, D), (D // 32) ** -0.5, 1.0, ((0, 32),))
    centroids = noise(keys[5], (EXPERTS, D), (2 * D) ** -0.5, 0.125, ((1, 32),))
    expert_up = noise(keys[6], (EXPERTS, 2, D, FF), D ** -0.5, 0.1875, ((0, 2), (2, 4), (3, 4)))
    expert_down = noise(keys[7], (EXPERTS, 2, FF, D), FF ** -0.5, 0.09375, ((0, 2), (2, 4), (3, 4)))
    sequence_lengths = jax.vmap(lambda own: uneven_parts(own, NSEQ, GTOK, MAXLEN, 2))(jax.random.split(keys[8], GROUPS)).reshape((GROUPS, NSEQ)).astype(jnp.int32)
    block_order = jax.vmap(lambda own: jax.random.permutation(own, NBLK))(jax.random.split(keys[9], GROUPS)).reshape((GROUPS, NBLK)).astype(jnp.int32)
    routes_keys = jax.random.split(jax.random.fold_in(keys[10], 1), GROUPS * GTOK // TOK_DEV)
    routes_turns = jax.random.permutation(jax.random.fold_in(keys[10], 3), GROUPS * GTOK // TOK_DEV)
    routes = jax.vmap(lambda own, number: deal_out(jax.random.fold_in(keys[10], 2), own, number, TOK_DEV, EXPERTS, 1, CAP, 1))(routes_keys, routes_turns).reshape((GROUPS, GTOK, 1))
    return dict(tokens=tokens, cotangent=cotangent, norm_gain=norm_gain, project_weight=project_weight, output_weight=output_weight, centroids=centroids, expert_up=expert_up, expert_down=expert_down, sequence_lengths=sequence_lengths, block_order=block_order, routes=routes)


@jax.custom_vjp
def low(v):
    return lax.optimization_barrier(v.astype(jnp.bfloat16)).astype(jnp.float32)

@jax.custom_vjp
def low_back(v):
    return v

def low_keep(v):
    return (low(v), None)

def low_pass(kept, grad):
    return (grad,)

def back_keep(v):
    return (v, None)

def back_low(kept, grad):
    return (low(grad),)
low.defvjp(low_keep, low_pass)
low_back.defvjp(back_keep, back_low)
precise = lax.Precision.HIGHEST

def place_rows(block_order, lengths_row):
    row_index = jnp.arange(GTOK, dtype=jnp.int32)
    picked = (row_index // BLK)[:, None] == jnp.arange(NBLK, dtype=jnp.int32)[None, :]
    blocks = lax.optimization_barrier(jnp.sum(jnp.where(picked, block_order[None, :], 0), axis=1)).astype(jnp.int32)
    token_place = (blocks * BLK + row_index % BLK).astype(jnp.int32)
    bounds = jnp.cumsum(lengths_row).astype(jnp.int32)
    sequence = lax.optimization_barrier(jnp.sum((token_place[:, None] >= bounds[None, :]).astype(jnp.int32), axis=1))
    return (token_place, sequence)

def attend_block(inputs, keys_all, values_all, key_place, key_sequence):
    query_block, query_place, query_sequence = inputs
    score_scale = 1.0 / math.sqrt(HDIM)
    heads_query = query_block.reshape(-1, HEADS, HDIM)
    heads_key = keys_all.reshape(-1, HEADS, HDIM)
    heads_value = values_all.reshape(-1, HEADS, HDIM)
    scores = jnp.einsum('thd,shd->hts', heads_query, heads_key, precision=precise) * score_scale
    allowed = (query_sequence[:, None] == key_sequence[None, :]) & (key_place[None, :] <= query_place[:, None])
    scores = low_back(jnp.where(allowed[None], scores, -1000000000.0))
    weights = low(jax.nn.softmax(scores, axis=-1))
    mixed_block = jnp.einsum('hts,shd->thd', weights, heads_value, precision=precise)
    return mixed_block.reshape(-1, D)

def expert_branch(inputs):
    routed, up_pair, down_pair = inputs
    hidden_one = low_back(jnp.dot(routed, up_pair[0], precision=precise))
    branch_one = low_back(jnp.dot(low(jax.nn.gelu(hidden_one)), down_pair[0], precision=precise))
    middle = low(routed + branch_one)
    hidden_two = low_back(jnp.dot(middle, up_pair[1], precision=precise))
    branch_two = jnp.dot(low(jax.nn.gelu(hidden_two)), down_pair[1], precision=precise)
    return branch_one + branch_two

def group_forward(inputs, gain_values, project_full, output_full, centroid_table, up_weight, down_weight):
    tokens_group, order_row, lengths_row, route_group = inputs
    token_place, sequence = place_rows(order_row, lengths_row)
    average = lax.optimization_barrier(jnp.mean(tokens_group, axis=-1, keepdims=True))
    centred = tokens_group - average
    inverse = lax.rsqrt(lax.optimization_barrier(jnp.mean(centred * centred, axis=-1, keepdims=True)) + 1e-05)
    normed = low(centred * inverse * gain_values)
    projected = jnp.dot(normed, project_full, precision=precise)
    queries = low_back(low(projected[:, :D]))
    keys_all = low_back(low(projected[:, D:2 * D]))
    values_all = low_back(low(projected[:, 2 * D:]))
    block_rows = min(512, GTOK)
    block_count = GTOK // block_rows

    def one_block(block_inputs):
        return attend_block(block_inputs, keys_all, values_all, token_place, sequence)
    mixed_all = lax.map(jax.checkpoint(one_block), (queries.reshape(block_count, block_rows, D), token_place.reshape(block_count, block_rows), sequence.reshape(block_count, block_rows))).reshape(GTOK, D)
    mixed_all = low_back(low(mixed_all))
    after_attention = tokens_group + low_back(jnp.dot(mixed_all, output_full, precision=precise))
    route_ids = route_group[:, 0].astype(jnp.int32)
    gate_value = jax.nn.sigmoid(lax.optimization_barrier(jnp.sum(after_attention * centroid_table[route_ids], axis=-1)))
    sent_rows = low_back(low(after_attention))
    member = (route_ids[:, None] == jnp.arange(EXPERTS, dtype=jnp.int32)[None, :]).astype(jnp.int32)
    member = member.reshape(N_CTX, TOK_DEV, EXPERTS)
    ranking = lax.optimization_barrier(jnp.sum((jnp.cumsum(member, axis=1).astype(jnp.int32) - 1) * member, axis=2)).reshape(GTOK).astype(jnp.int32)
    device_of = jnp.arange(GTOK, dtype=jnp.int32) // TOK_DEV
    slot_index = (route_ids * (N_CTX * CAP) + device_of * CAP + ranking).astype(jnp.int32)
    total_slots = EXPERTS * N_CTX * CAP
    filler = jnp.full((total_slots,), GTOK, dtype=jnp.int32).at[slot_index].set(jnp.arange(GTOK, dtype=jnp.int32))
    padded = jnp.concatenate([sent_rows, jnp.zeros((1, D), jnp.float32)], axis=0)
    dispatched = padded[filler].reshape(EXPERTS, N_CTX * CAP, D)
    expert_out = lax.map(jax.checkpoint(expert_branch), (dispatched, up_weight, down_weight))
    returned = low_back(low(expert_out)).reshape(total_slots, D)[slot_index]
    return after_attention + gate_value[:, None] * returned

def reference(tokens, cotangent, norm_gain, project_weight, output_weight, centroids, expert_up, expert_down, sequence_lengths, block_order, routes):
    floats = (tokens.astype(jnp.float32), norm_gain.astype(jnp.float32), project_weight.astype(jnp.float32), output_weight.astype(jnp.float32), centroids.astype(jnp.float32), expert_up.astype(jnp.float32), expert_down.astype(jnp.float32))

    def forward(tokens_f, gain_values, project_full, output_full, centroid_table, up_weight, down_weight):

        def one_group(inputs):
            return group_forward(inputs, gain_values, project_full, output_full, centroid_table, up_weight, down_weight)
        return lax.map(jax.checkpoint(one_group), (tokens_f, block_order, sequence_lengths, routes))
    result, pullback = jax.vjp(forward, *floats)
    gradients = pullback(cotangent.astype(jnp.float32))
    return (result.astype(jnp.bfloat16), gradients[0], gradients[1], gradients[2], gradients[3], gradients[4], gradients[5], gradients[6])
```

```python
import math

import jax
import jax.numpy as jnp
from jax import lax
from jax.experimental import pallas as pl
from jax.experimental.pallas import tpu as pltpu
from jax.sharding import PartitionSpec as P

HEADS = 16
HDIM = 64
BLK = 128


precise = lax.Precision.HIGHEST


def place_rows(order_row, lengths_row, total_rows):
    row_index = jnp.arange(total_rows, dtype=jnp.int32)
    picked = (row_index // BLK)[:, None] == jnp.arange(order_row.shape[0], dtype=jnp.int32)[None, :]
    blocks = jnp.sum(jnp.where(picked, order_row[None, :], 0), axis=1)
    token_place = blocks * BLK + row_index % BLK
    bounds = jnp.cumsum(lengths_row)
    sequence = jnp.sum((token_place[:, None] >= bounds[None, :]).astype(jnp.int32), axis=1)
    return (token_place, sequence)


def normalize(values):
    average = jnp.mean(values, axis=-1, keepdims=True)
    centred = values - average
    inverse = lax.rsqrt(jnp.mean(centred * centred, axis=-1, keepdims=True) + 1e-05)
    return (centred * inverse, inverse)


def head_slice(matrix, section, offset, heads_per):
    width_part = heads_per * HDIM
    first_col = offset + section * width_part
    return matrix[:, first_col : first_col + width_part].reshape(matrix.shape[0], heads_per, HDIM)


def spread_rows(local_rows):
    return lax.all_gather(local_rows, "wsh", axis=0, tiled=True)


def collect_rows(partial_term):
    return lax.psum_scatter(
        partial_term.astype(jnp.bfloat16), "wsh", scatter_dimension=0, tiled=True
    ).astype(jnp.float32)


def trade_rows(slots_rows, peer_count, capacity):
    shaped = slots_rows.reshape(peer_count, capacity, slots_rows.shape[-1])
    moved = lax.all_to_all(shaped, "ctx", split_axis=0, concat_axis=0, tiled=True)
    return moved.reshape(peer_count * capacity, slots_rows.shape[-1])


def gelu_pullback(hidden, incoming):
    value_out, pullback = jax.vjp(jax.nn.gelu, hidden)
    return pullback(incoming)[0]


def shards(
    tokens,
    cotangent,
    norm_gain,
    project_weight,
    output_weight,
    centroids,
    expert_up,
    expert_down,
    sequence_lengths,
    block_order,
    routes,
):
    local_rows = tokens.shape[1]
    model_width = tokens.shape[2]
    peer_count = lax.axis_size("ctx")
    position = lax.axis_index("ctx")
    total_rows = local_rows * peer_count
    capacity = max(2, (5 * local_rows + 4 * peer_count - 1) // (4 * peer_count))
    slot_count = peer_count * capacity
    score_scale = 1.0 / math.sqrt(HDIM)
    heads_per = 4
    sections = HEADS // heads_per
    inputs_f = tokens[0].astype(jnp.float32)
    upstream = cotangent[0].astype(jnp.float32)
    project_full, output_full, gain_full, centroid_full = (
        lax.all_gather(project_weight, ("grp", "ctx", "wsh"), axis=0, tiled=True),
        lax.all_gather(output_weight, ("grp", "ctx", "wsh"), axis=0, tiled=True),
        lax.all_gather(norm_gain, ("grp", "ctx", "wsh"), axis=0, tiled=True),
        lax.all_gather(centroids, ("grp", "ctx", "wsh"), axis=1, tiled=True),
    )
    up_full, down_full = (
        lax.all_gather(expert_up, "grp", axis=2, tiled=True),
        lax.all_gather(expert_down, "grp", axis=3, tiled=True),
    )
    place_all, sequence_all = place_rows(block_order[0], sequence_lengths[0], total_rows)
    place_own = lax.dynamic_slice_in_dim(place_all, position * local_rows, local_rows)
    sequence_own = lax.dynamic_slice_in_dim(sequence_all, position * local_rows, local_rows)
    allowed = (sequence_own[:, None] == sequence_all[None, :]) & (
        place_all[None, :] <= place_own[:, None]
    )
    normed, inverse = normalize(inputs_f)
    gain_values = gain_full.astype(jnp.float32)
    normed_low = (normed * gain_values).astype(jnp.bfloat16)
    projected = jnp.dot(normed_low, project_full, preferred_element_type=jnp.float32)
    queries = projected[:, :model_width].astype(jnp.bfloat16)
    keyvalue = projected[:, model_width:].astype(jnp.bfloat16)
    keyvalue_all = lax.all_gather(keyvalue, "ctx", axis=0, tiled=True)
    mixed_parts = []
    logsum_parts = []
    for section in range(sections):
        head_query = head_slice(queries, section, 0, heads_per)
        head_key = head_slice(keyvalue_all, section, 0, heads_per)
        head_value = head_slice(keyvalue_all, section, model_width, heads_per)
        scores = (
            jnp.einsum("tgd,sgd->gts", head_query, head_key, preferred_element_type=jnp.float32)
            * score_scale
        )
        scores = jnp.where(allowed[None], scores, -1000000000.0)
        largest = jnp.max(scores, axis=-1, keepdims=True)
        exponent = jnp.exp(scores - largest)
        totals = jnp.sum(exponent, axis=-1, keepdims=True)
        weights = (exponent / totals).astype(jnp.bfloat16)
        mixed_part = jnp.einsum(
            "gts,sgd->tgd", weights, head_value, preferred_element_type=jnp.float32
        )
        mixed_parts.append(mixed_part.reshape(local_rows, heads_per * HDIM))
        logsum_parts.append((largest + jnp.log(totals))[:, :, 0])
    mixed_all = jnp.concatenate(mixed_parts, axis=1).astype(jnp.bfloat16)
    logsum = jnp.concatenate(logsum_parts, axis=0)
    after_attention = inputs_f + jnp.dot(mixed_all, output_full, preferred_element_type=jnp.float32)
    route_ids = routes[0, :, 0]
    member = route_ids[:, None] == jnp.arange(peer_count, dtype=jnp.int32)[None, :]
    member_f = member.astype(jnp.float32)
    picked_centroid = jnp.dot(member_f, centroid_full.astype(jnp.float32), precision=precise)
    gate_value = jax.nn.sigmoid(jnp.sum(after_attention * picked_centroid, axis=-1))
    member_int = member.astype(jnp.int32)
    ranking = jnp.sum((jnp.cumsum(member_int, axis=0) - 1) * member_int, axis=1)
    slot_index = route_ids * capacity + ranking
    dispatch = (slot_index[None, :] == jnp.arange(slot_count, dtype=jnp.int32)[:, None]).astype(
        jnp.bfloat16
    )
    sent_rows = jnp.dot(
        dispatch, after_attention.astype(jnp.bfloat16), preferred_element_type=jnp.float32
    ).astype(jnp.bfloat16)
    arrived = trade_rows(sent_rows, peer_count, capacity)
    up_first = up_full[0, 0]
    up_second = up_full[0, 1]
    down_first = down_full[0, 0]
    down_second = down_full[0, 1]
    gathered_one = spread_rows(arrived)
    hidden_one = jnp.dot(gathered_one, up_first, preferred_element_type=jnp.float32)
    active_one = jax.nn.gelu(hidden_one).astype(jnp.bfloat16)
    branch_one = collect_rows(jnp.dot(active_one, down_first, preferred_element_type=jnp.float32))
    middle = (arrived.astype(jnp.float32) + branch_one).astype(jnp.bfloat16)
    gathered_two = spread_rows(middle)
    hidden_two = jnp.dot(gathered_two, up_second, preferred_element_type=jnp.float32)
    active_two = jax.nn.gelu(hidden_two).astype(jnp.bfloat16)
    branch_two = collect_rows(jnp.dot(active_two, down_second, preferred_element_type=jnp.float32))
    expert_out = (branch_one + branch_two).astype(jnp.bfloat16)
    returned = trade_rows(expert_out, peer_count, capacity)
    returned_tok = jnp.einsum("st,sd->td", dispatch, returned, preferred_element_type=jnp.float32)
    output = after_attention + gate_value[:, None] * returned_tok
    gate_grad = jnp.sum(upstream * returned_tok, axis=-1)
    score_grad = gate_grad * gate_value * (1.0 - gate_value)
    centroid_term = jnp.dot(member_f.T, score_grad[:, None] * after_attention, precision=precise)
    branch_grad = (gate_value[:, None] * upstream).astype(jnp.bfloat16)
    branch_sent = jnp.dot(dispatch, branch_grad, preferred_element_type=jnp.float32).astype(
        jnp.bfloat16
    )
    branch_arrived = trade_rows(branch_sent, peer_count, capacity)
    grad_two = spread_rows(branch_arrived)
    hidden_two_grad = gelu_pullback(
        hidden_two, jnp.dot(grad_two, down_second.T, preferred_element_type=jnp.float32)
    ).astype(jnp.bfloat16)
    down_second_grad = jnp.dot(active_two.T, grad_two, preferred_element_type=jnp.float32)
    up_second_grad = jnp.dot(gathered_two.T, hidden_two_grad, preferred_element_type=jnp.float32)
    middle_grad = collect_rows(
        jnp.dot(hidden_two_grad, up_second.T, preferred_element_type=jnp.float32)
    )
    first_branch_grad = (branch_arrived.astype(jnp.float32) + middle_grad).astype(jnp.bfloat16)
    grad_one = spread_rows(first_branch_grad)
    hidden_one_grad = gelu_pullback(
        hidden_one, jnp.dot(grad_one, down_first.T, preferred_element_type=jnp.float32)
    ).astype(jnp.bfloat16)
    down_first_grad = jnp.dot(active_one.T, grad_one, preferred_element_type=jnp.float32)
    up_first_grad = jnp.dot(gathered_one.T, hidden_one_grad, preferred_element_type=jnp.float32)
    arrived_grad = (
        collect_rows(jnp.dot(hidden_one_grad, up_first.T, preferred_element_type=jnp.float32))
        + middle_grad
    ).astype(jnp.bfloat16)
    home_grad = trade_rows(arrived_grad, peer_count, capacity)
    home_grad_tok = jnp.einsum("st,sd->td", dispatch, home_grad, preferred_element_type=jnp.float32)
    up_terms = jnp.stack([up_first_grad, up_second_grad])[None]
    down_terms = jnp.stack([down_first_grad, down_second_grad])[None]
    up_grad_out, down_grad_out = (
        lax.psum_scatter(
            up_terms.astype(jnp.bfloat16), "grp", scatter_dimension=2, tiled=True
        ).astype(jnp.float32),
        lax.psum_scatter(
            down_terms.astype(jnp.bfloat16), "grp", scatter_dimension=3, tiled=True
        ).astype(jnp.float32),
    )
    residual_grad = upstream + score_grad[:, None] * picked_centroid + home_grad_tok
    residual_low = residual_grad.astype(jnp.bfloat16)
    output_term = jnp.dot(mixed_all.T, residual_low, preferred_element_type=jnp.float32)
    mixed_grad = jnp.dot(residual_low, output_full.T, preferred_element_type=jnp.float32).astype(
        jnp.bfloat16
    )
    query_grads = []
    key_grads = []
    value_grads = []
    delta_parts = []
    for section in range(sections):
        head_query = head_slice(queries, section, 0, heads_per)
        head_key = head_slice(keyvalue_all, section, 0, heads_per)
        head_value = head_slice(keyvalue_all, section, model_width, heads_per)
        head_grad = head_slice(mixed_grad, section, 0, heads_per)
        scores = (
            jnp.einsum("tgd,sgd->gts", head_query, head_key, preferred_element_type=jnp.float32)
            * score_scale
        )
        scores = jnp.where(allowed[None], scores, -1000000000.0)
        probs = jnp.exp(
            scores - logsum[section * heads_per : (section + 1) * heads_per][:, :, None]
        )
        probs_grad = jnp.einsum(
            "tgd,sgd->gts", head_grad, head_value, preferred_element_type=jnp.float32
        )
        row_delta = jnp.sum(probs_grad * probs, axis=-1)
        scores_grad = (probs * (probs_grad - row_delta[:, :, None])).astype(jnp.bfloat16)
        query_part = (
            jnp.einsum("gts,sgd->tgd", scores_grad, head_key, preferred_element_type=jnp.float32)
            * score_scale
        )
        query_grads.append(query_part.reshape(local_rows, heads_per * HDIM))
        delta_parts.append(row_delta)
        key_part = (
            jnp.einsum("gts,tgd->sgd", scores_grad, head_query, preferred_element_type=jnp.float32)
            * score_scale
        )
        value_part = jnp.einsum(
            "gts,tgd->sgd",
            probs.astype(jnp.bfloat16),
            head_grad,
            preferred_element_type=jnp.float32,
        )
        key_grads.append(key_part.reshape(total_rows, heads_per * HDIM))
        value_grads.append(value_part.reshape(total_rows, heads_per * HDIM))
    query_grad = jnp.concatenate(query_grads, axis=1).astype(jnp.bfloat16)
    keyvalue_terms = jnp.concatenate(key_grads + value_grads, axis=1)
    keyvalue_grad = lax.psum_scatter(
        keyvalue_terms.astype(jnp.bfloat16), "ctx", scatter_dimension=0, tiled=True
    )
    projected_grad = jnp.concatenate([query_grad, keyvalue_grad], axis=1)
    project_term = jnp.dot(normed_low.T, projected_grad, preferred_element_type=jnp.float32)
    normed_grad = jnp.dot(projected_grad, project_full.T, preferred_element_type=jnp.float32)
    gain_term = jnp.sum(normed_grad * normed, axis=0)
    scaled_grad = normed_grad * gain_values
    input_grad = residual_grad + inverse * (
        scaled_grad
        - jnp.mean(scaled_grad, axis=-1, keepdims=True)
        - normed * jnp.mean(scaled_grad * normed, axis=-1, keepdims=True)
    )
    project_grad, output_grad, gain_grad, centroid_grad = (
        lax.psum_scatter(project_term, ("grp", "ctx", "wsh"), scatter_dimension=0, tiled=True),
        lax.psum_scatter(output_term, ("grp", "ctx", "wsh"), scatter_dimension=0, tiled=True),
        lax.psum_scatter(gain_term, ("grp", "ctx", "wsh"), scatter_dimension=0, tiled=True),
        lax.psum_scatter(centroid_term, ("grp", "ctx", "wsh"), scatter_dimension=1, tiled=True),
    )
    return (
        output.astype(jnp.bfloat16)[None],
        input_grad[None],
        gain_grad,
        project_grad,
        output_grad,
        centroid_grad,
        up_grad_out,
        down_grad_out,
    )


VMEM_LIMIT = 60 * 2**20

IN_SPECS = (
    P(("grp", "wsh"), "ctx", None),
    P(("grp", "wsh"), "ctx", None),
    P(("grp", "ctx", "wsh")),
    P(("grp", "ctx", "wsh"), None),
    P(("grp", "ctx", "wsh"), None),
    P(None, ("grp", "ctx", "wsh")),
    P("ctx", None, "grp", "wsh"),
    P("ctx", None, "wsh", "grp"),
    P(("grp", "wsh"), None),
    P(("grp", "wsh"), None),
    P(("grp", "wsh"), "ctx", None),
)
OUT_SPECS = (
    P(("grp", "wsh"), "ctx", None),
    P(("grp", "wsh"), "ctx", None),
    P(("grp", "ctx", "wsh")),
    P(("grp", "ctx", "wsh"), None),
    P(("grp", "ctx", "wsh"), None),
    P(None, ("grp", "ctx", "wsh")),
    P("ctx", None, "grp", "wsh"),
    P("ctx", None, "wsh", "grp"),
)

BF = jnp.bfloat16
F32 = jnp.float32
NN = ((1,), (0,))
NT = ((1,), (1,))
TN = ((0,), (0,))
MESH = pl.DeviceIdType.MESH
GELU_C = 0.7978845608028654
EXTRA = 128
CAP = 80


def dot(a, b, dims=NN):
    return lax.dot_general(a, b, (dims, ((), ())), preferred_element_type=F32)


def gelu_both(h):
    sq = h * h
    t = jnp.tanh(GELU_C * h * (1.0 + 0.044715 * sq))
    half = 0.5 * (1.0 + t)
    slope = half + 0.5 * h * (1.0 - t * t) * (GELU_C * (1.0 + 3.0 * 0.044715 * sq))
    return h * half, slope


def copy_in(src, dst, sem):
    return pltpu.make_async_copy(src, dst, sem)


class Copies:
    def __init__(self, send, recv):
        self.send, self.recv, self.used = send, recv, 0

    def block(self, count):
        first = self.used
        self.used += count
        return first

    def at(self, index, src, dst, device):
        return pltpu.make_async_remote_copy(
            src_ref=src,
            dst_ref=dst,
            send_sem=self.send.at[index],
            recv_sem=self.recv.at[index],
            device_id=device,
            device_id_type=MESH,
        )

    def new(self, src, dst, device):
        return self.at(self.block(1), src, dst, device)


class Place:
    def __init__(self):
        g, y, w = lax.axis_index("grp"), lax.axis_index("ctx"), lax.axis_index("wsh")
        self.g, self.y, self.w = g, y, w
        self.x = lax.div(g, 2)
        self.c = g - 2 * self.x
        self.gx = 2 * (1 - self.x) + self.c
        self.gc = 2 * self.x + 1 - self.c
        self.gd = 2 * (1 - self.x) + 1 - self.c
        self.wb = lax.rem(w, 2)
        self.w1 = w + 1 - 2 * self.wb
        self.w2 = lax.rem(w + 2, 4)
        self.dev_x = (self.gx, y, w)
        self.dev_c = (self.gc, y, w)
        self.dev_y = (g, 1 - y, w)
        self.dev_z = lambda k: (g, y, lax.rem(w + k, 4))

    def team(self, j):
        jx, jz = lax.rem(j, 2), lax.div(j, 2)
        tx = self.x + jx - 2 * self.x * jx
        tz = self.wb + jz - 2 * self.wb * jz
        return 2 * tx + tz, (2 * tx + self.c, self.y, (1 - jz) * self.w + jz * self.w1)


def greet(devices):
    barrier = pltpu.get_barrier_semaphore()
    for device in devices:
        pl.semaphore_signal(barrier, inc=1, device_id=device, device_id_type=MESH)
    pl.semaphore_wait(barrier, len(devices))


def dispatch_block(route_rows, expert):
    member = (route_rows == expert.astype(F32)).astype(F32)
    earlier = lax.broadcasted_iota(jnp.int32, (128, 128), 0) < lax.broadcasted_iota(jnp.int32, (128, 128), 1)
    rank = dot(member.astype(BF), earlier.astype(F32).astype(BF))
    slot = lax.broadcasted_iota(jnp.int32, (CAP, 128), 0).astype(F32)
    hit = (jnp.broadcast_to(rank[0:1, :], (CAP, 128)) == slot) & (
        jnp.broadcast_to(member[0:1, :], (CAP, 128)) > 0.5
    )
    return hit.astype(F32).astype(BF)


def place_of(meta, index):
    place = jnp.where(index < 128, meta[3], meta[4]) * 128 + lax.rem(index, 128)
    bound = meta[0]
    sequence = jnp.where(place >= bound, 1, 0)
    for part in (1, 2):
        bound = bound + meta[part]
        sequence = sequence + jnp.where(place >= bound, 1, 0)
    return place, sequence


def forward_kernel(
    meta, tok, cot, rts, wq_in, wo_in, up_in, dn_in,
    XG, QKV, PR, MXH, WQ, WO, RT, OUTS, RESS, CGR, GU1, GD1, S2U, S2D,
    TQ, CG, XH, NRM, UP, DN, DSP, XS, GS, MS, AA,
    R1, R2, R3, R4, RB, PS, OWN, GP1, A1, A2, DH, SUMS,
    GU2, GD2, CRU, CRD, ZSU, ZSD, ZRU, ZRD,
    send, recv, local,
):
    p = Place()
    g, y, w, x = p.g, p.y, p.w, p.x
    cp = Copies(send, recv)
    greet([p.dev_x, p.dev_c, p.dev_y, p.dev_z(1), p.dev_z(2), p.dev_z(3), p.team(3)[1]])
    nlocal = [0]

    def here(src, dst):
        nlocal[0] += 1
        return copy_in(src, dst, local.at[nlocal[0] - 1])

    def go(*items):
        for item in items:
            item.start()
        return items

    def wait(*items):
        for item in items:
            item.wait()

    mine = pl.ds(y * 128, 128)
    row = pl.ds(pl.multiple_of(g * 256 + y * 128 + w * 32, 32), 32)
    row_o = pl.ds(pl.multiple_of(g * 128 + w * 32, 32), 32)
    row_t = pl.ds(pl.multiple_of(w * 32, 32), 32)
    zq = []
    zo = []
    for k in (1, 3, 2):
        zq += go(
            cp.new(wq_in.at[y], WQ.at[row, :], p.dev_z(k)),
            cp.new(wq_in.at[1 - y], TQ.at[row_t, :], p.dev_z(k)),
        )
    own = go(
        here(wq_in.at[y], WQ.at[row, :]),
        here(wq_in.at[1 - y], TQ.at[row_t, :]),
        here(wo_in, WO.at[y, row_o, :]),
        here(tok, XG.at[mine, :]),
        here(cot, CG.at[mine, :]),
        here(rts, RT.at[y]),
    )
    ty = go(
        cp.new(tok, XG.at[mine, :], p.dev_y),
        cp.new(rts, RT.at[y], p.dev_y),
    )
    for k in (1, 3, 2):
        zo += go(cp.new(wo_in, WO.at[y, row_o, :], p.dev_z(k)))

    def dq(q):
        return pl.ds(pl.multiple_of(q * 256, 256), 256)

    half = pl.ds(pl.multiple_of(x * 512, 512), 512)
    other = pl.ds(pl.multiple_of((1 - x) * 512, 512), 512)

    def e_first(s):
        return go(
            cp.new(up_in.at[s, :, other], UP.at[s, 0, dq(g), :], p.dev_x),
            cp.new(dn_in.at[s, other, :], DN.at[s, 0, :, dq(g)], p.dev_x),
        )

    def e_core0(s):
        return go(
            cp.new(up_in.at[s, :, half], UP.at[s, 0, dq(g), :], p.dev_c),
            cp.new(dn_in.at[s, half, :], DN.at[s, 0, :, dq(g)], p.dev_c),
        )

    def e_local(s):
        return go(
            here(up_in.at[s, :, half], UP.at[s, 0, dq(g), :]),
            here(dn_in.at[s, half, :], DN.at[s, 0, :, dq(g)]),
        )

    def e_z(s):
        return go(
            cp.new(up_in.at[s, :, half], UP.at[s, 1, dq(g), :], p.dev_z(2)),
            cp.new(dn_in.at[s, half, :], DN.at[s, 1, :, dq(g)], p.dev_z(2)),
        )

    def e_relay(s):
        return go(
            cp.new(UP.at[s, 0, dq(p.gx), :], UP.at[s, 1, dq(p.gx), :], p.dev_z(2)),
            cp.new(DN.at[s, 0, :, dq(p.gx)], DN.at[s, 1, :, dq(p.gx)], p.dev_z(2)),
        )

    def e_core(s, q, which):
        return go(
            cp.new(UP.at[s, q, dq(which), :], UP.at[s, q, dq(which), :], p.dev_c),
            cp.new(DN.at[s, q, :, dq(which)], DN.at[s, q, :, dq(which)], p.dev_c),
        )

    e1 = [e_first(0)]
    el = e_local(0) + e_local(1)
    ec0 = [e_core0(0), e_core0(1)]

    wait(*own)
    wait(*ty)
    cy = go(cp.new(cot, CG.at[mine, :], p.dev_y))
    values = XG[...].astype(F32)
    centred = values - jnp.mean(values, axis=1, keepdims=True)
    inverse = lax.rsqrt(jnp.mean(centred * centred, axis=1, keepdims=True) + 1e-05)
    XH[...] = centred * inverse
    for b in (0, 1):
        DSP[b] = dispatch_block(RT[b], y)
        XS[b * CAP : (b + 1) * CAP, :] = dot(DSP[b], XG[b * 128 : (b + 1) * 128, :])

    wait(*zq)
    yq = go(cp.new(TQ, WQ.at[pl.ds(pl.multiple_of(g * 256 + y * 128, 128), 128), :], p.dev_y))
    wait(*e1[0])
    ez = [e_z(0)]
    er = [e_relay(0)]
    ec = [e_core(0, 0, p.gx)]
    wait(*zo)
    block_y = pl.ds(pl.multiple_of(g * 128, 128), 128)
    yo = go(cp.new(WO.at[y, block_y, :], WO.at[y, block_y, :], p.dev_y))
    wait(*yq)
    xq = go(
        cp.new(WQ.at[dq(g), :], WQ.at[dq(g), :], p.dev_x),
        cp.new(WQ.at[dq(g), :], WQ.at[dq(g), :], p.dev_c),
    )
    wait(*yo)
    xo = go(
        cp.new(WO.at[:, block_y, :], WO.at[:, block_y, :], p.dev_x),
        cp.new(WO.at[:, block_y, :], WO.at[:, block_y, :], p.dev_c),
    )
    e1.append(e_first(1))
    wait(*xq)
    fq = go(cp.new(WQ.at[dq(p.gx), :], WQ.at[dq(p.gx), :], p.dev_c))
    wait(*cy)
    for b in (0, 1):
        GS[b * CAP : (b + 1) * CAP, :] = dot(DSP[b], CG[b * 128 : (b + 1) * 128, :]).astype(BF)
    wait(*fq)

    pick = (
        lax.broadcasted_iota(jnp.int32, (8, EXTRA), 0) == lax.broadcasted_iota(jnp.int32, (8, EXTRA), 1)
    ).astype(F32).astype(BF)
    extra = dot(pick, WQ[:, 1536:], NT)
    gain = extra[0:1, :]
    centroid = jnp.where(y == 0, extra[1:2, :], extra[2:3, :])
    NRM[...] = (XH[...] * gain).astype(BF)

    def project(t, carry):
        cols = pl.ds(pl.multiple_of(t * 512, 512), 512)
        QKV[:, cols] = dot(NRM[...], WQ[:, cols]).astype(BF)
        return carry

    lax.fori_loop(0, 3, project, 0)
    wait(*xo)
    far = pl.ds(pl.multiple_of(p.gx * 128, 128), 128)
    fo = go(cp.new(WO.at[:, far, :], WO.at[:, far, :], p.dev_c))

    place_q, seq_q = place_of(meta, lax.broadcasted_iota(jnp.int32, (256, 256), 0))
    place_k, seq_k = place_of(meta, lax.broadcasted_iota(jnp.int32, (256, 256), 1))
    allowed = (seq_q == seq_k) & (place_k <= place_q)
    low_half = lax.broadcasted_iota(jnp.int32, (256, 128), 1) < 64
    mixed_first = cp.block(4)

    def mixed_copy(t):
        cols = pl.ds(pl.multiple_of(t * 128, 128), 128)
        return cp.at(mixed_first + t, MXH.at[y, :, cols], MXH.at[y, :, cols], p.dev_y)

    def heads(t, carry):
        cols = pl.ds(pl.multiple_of(t * 128, 128), 128)
        q2 = QKV[:, cols]
        k2 = QKV[:, pl.ds(pl.multiple_of(512 + t * 128, 128), 128)]
        v2 = QKV[:, pl.ds(pl.multiple_of(1024 + t * 128, 128), 128)]
        parts = []
        for i in (0, 1):
            keep = low_half if i == 0 else ~low_half
            scores = dot(jnp.where(keep, q2, jnp.zeros_like(q2)), k2, NT) * 0.125
            scores = jnp.where(allowed, scores, -1000000000.0)
            exponent = jnp.exp(scores - jnp.max(scores, axis=1, keepdims=True))
            probs = exponent / jnp.sum(exponent, axis=1, keepdims=True)
            PR[2 * t + i] = probs
            parts.append(dot(probs.astype(BF), v2))
        MXH[y, :, cols] = jnp.where(low_half, parts[0], parts[1]).astype(BF)
        mixed_copy(t).start()
        return carry

    lax.fori_loop(0, 4, heads, 0)

    def mixed_pick(yy):
        for b in (0, 1):
            MS[yy, b * CAP : (b + 1) * CAP, :] = dot(DSP[b], MXH[yy, b * 128 : (b + 1) * 128, :]).astype(BF)

    mixed_pick(y)
    wait(*fo)
    AA[...] = XS[...] + dot(MS[y], WO[y])
    lax.fori_loop(0, 4, lambda t, carry: (mixed_copy(t).wait(), carry)[1], 0)
    mixed_pick(1 - y)
    AA[...] += dot(MS[1 - y], WO[1 - y])
    gate = jax.nn.sigmoid(jnp.sum(AA[...] * centroid, axis=1, keepdims=True))

    wait(*el)
    me = pl.ds(pl.multiple_of(p.team(0)[0] * 160, 160), 160)

    def spread(first, R):
        def one(j):
            device = p.team(j)[1]
            return cp.at(first + j - 1, R.at[me, :], R.at[me, :], device)

        return one

    def each(fn):
        def body(j, carry):
            fn(j)
            return carry

        lax.fori_loop(1, 4, body, 0)

    def reduce_copy(first, k, b):
        def one(j):
            device = p.team(j)[1]
            return cp.at(first + j - 1, PS.at[k, j - 1], RB.at[b, j - 1], device)

        return one

    firsts = [cp.block(3) for _ in range(8)]
    g1, g2, g3, g4 = (spread(f, R) for f, R in zip(firsts[:4], (R1, R2, R3, R4)))
    r1, r3, r2, r4 = (reduce_copy(f, k, b) for f, k, b in zip(firsts[4:], (0, 1, 2, 0), (0, 1, 2, 3)))

    def rows_of(j):
        return pl.ds(pl.multiple_of(p.team(j)[0] * 160, 160), 160)

    R1[me, :] = AA[...].astype(BF)
    each(lambda j: g1(j).start())
    R3[me, :] = (gate * GS[...].astype(F32)).astype(BF)
    each(lambda j: g3(j).start())

    wait(*ec0[0])
    wait(*ec[0])
    wait(*ez[0])
    ec1 = e_core(0, 1, g)
    wait(*er[0])
    ec2 = e_core(0, 1, p.gx)
    wait(*e1[1])
    ez.append(e_z(1))
    er.append(e_relay(1))
    ec.append(e_core(1, 0, p.gx))
    wait(*ec1)
    wait(*ec2)

    def cols_of(q):
        return slice(q * 512, (q + 1) * 512)

    def first_forward(j):
        at = rows_of(j)
        total = None
        for q in (0, 1):
            active, slope = gelu_both(dot(R1[at, :], UP[0, q]))
            GP1[at, cols_of(q)] = slope
            A1[at, cols_of(q)] = active.astype(BF)
            term = dot(active.astype(BF), DN[0, q])
            total = term if total is None else total + term
        return total

    OWN[0] = first_forward(0)

    def step_one(j):
        g1(j).wait()
        PS[0, j - 1] = first_forward(j).astype(BF)
        r1(j).start()

    each(step_one)
    each(lambda j: r1(j).wait())
    branch_one = OWN[0] + RB[0, 0].astype(F32) + RB[0, 1].astype(F32) + RB[0, 2].astype(F32)
    SUMS[0] = branch_one
    R2[me, :] = (AA[...].astype(BF).astype(F32) + branch_one).astype(BF)
    each(lambda j: g2(j).start())
    each(lambda j: g3(j).wait())

    wait(*ec0[1])
    wait(*ec[1])
    wait(*ez[1])
    ec1 = e_core(1, 1, g)
    wait(*er[1])
    ec2 = e_core(1, 1, p.gx)
    wait(*ec1)
    wait(*ec2)

    def second_both(j):
        at = rows_of(j)
        total, total_grad = None, None
        for q in (0, 1):
            active, slope = gelu_both(dot(R2[at, :], UP[1, q]))
            A2[at, cols_of(q)] = active.astype(BF)
            grad = (slope * dot(R3[at, :], DN[1, q], NT)).astype(BF)
            DH[at, cols_of(q)] = grad
            term = dot(grad, UP[1, q], NT)
            total_grad = term if total_grad is None else total_grad + term
        for q in (0, 1):
            term = dot(A2[at, cols_of(q)], DN[1, q])
            total = term if total is None else total + term
        return total, total_grad

    OWN[1], OWN[2] = second_both(0)

    def step_two(j):
        g2(j).wait()
        total, total_grad = second_both(j)
        PS[1, j - 1] = total_grad.astype(BF)
        r3(j).start()
        PS[2, j - 1] = total.astype(BF)
        r2(j).start()

    each(step_two)

    def weight_grads(A, R, RG, GU, GD):
        def one(q, d):
            qcols = pl.ds(pl.multiple_of(q * 512, 512), 512)
            GU[q, d] = dot(R[:, dq(d)], DH[:, qcols], TN).astype(BF)
            GD[q, d] = dot(A[:, qcols], RG[:, dq(d)], TN).astype(BF)

        def body(t, carry):
            q, k = lax.rem(t, 2), lax.div(t, 2)
            d = lax.rem(k, 2)
            mine_c = lax.div(k, 2)
            cc = p.c * mine_c + (1 - p.c) * (1 - mine_c)
            one(q, 2 * d + cc)
            return carry

        return body

    body2 = weight_grads(A2, R2, R3, GU2, GD2)
    lax.fori_loop(0, 4, body2, 0)
    f0 = []
    for k, (theirs, mine_d) in enumerate(((p.gc, 0), (p.gd, 1))):
        f0 += go(
            cp.new(GU2.at[:, theirs], CRU.at[:, k], p.dev_c),
            cp.new(GD2.at[:, theirs], CRD.at[:, k], p.dev_c),
        )
    lax.fori_loop(4, 8, body2, 0)

    each(lambda j: r3(j).wait())
    middle_grad = OWN[2] + RB[1, 0].astype(F32) + RB[1, 1].astype(F32) + RB[1, 2].astype(F32)
    SUMS[1] = middle_grad
    R4[me, :] = (R3[me, :].astype(F32) + middle_grad).astype(BF)
    each(lambda j: g4(j).start())
    wait(*f0)
    f1 = []
    for k, d in enumerate((g, p.gx)):
        ZSU[k] = (GU2[1, d].astype(F32) + CRU[1, k].astype(F32)).astype(BF)
        ZSD[k] = (GD2[1, d].astype(F32) + CRD[1, k].astype(F32)).astype(BF)
        f1 += go(
            cp.new(ZSU.at[k], ZRU.at[k], p.dev_z(2)),
            cp.new(ZSD.at[k], ZRD.at[k], p.dev_z(2)),
        )

    each(lambda j: r2(j).wait())
    branch_two = OWN[1] + RB[2, 0].astype(F32) + RB[2, 1].astype(F32) + RB[2, 2].astype(F32)
    returned = (SUMS[0] + branch_two).astype(BF).astype(F32)
    upstream = GS[...].astype(F32)
    OUTS[...] = (AA[...] + gate * returned).astype(BF)
    score_grad = jnp.sum(upstream * returned, axis=1, keepdims=True) * gate * (1.0 - gate)
    CGR[...] = jnp.broadcast_to(jnp.sum(score_grad * AA[...], axis=0, keepdims=True), CGR.shape)
    OWN[1] = upstream + score_grad * centroid

    def first_backward(j):
        at = rows_of(j)
        total = None
        for q in (0, 1):
            grad = (GP1[at, cols_of(q)] * dot(R4[at, :], DN[0, q], NT)).astype(BF)
            DH[at, cols_of(q)] = grad
            term = dot(grad, UP[0, q], NT)
            total = term if total is None else total + term
        return total

    OWN[0] = first_backward(0)

    def step_three(j):
        g4(j).wait()
        PS[0, j - 1] = first_backward(j).astype(BF)
        r4(j).start()

    each(step_three)
    lax.fori_loop(0, 8, weight_grads(A1, R1, R4, GU1, GD1), 0)
    each(lambda j: r4(j).wait())
    arrived = (
        OWN[0] + RB[3, 0].astype(F32) + RB[3, 1].astype(F32) + RB[3, 2].astype(F32) + SUMS[1]
    ).astype(BF)
    RESS[...] = (OWN[1] + arrived.astype(F32)).astype(BF)

    wait(*f1)
    for k, d in enumerate((g, p.gx)):
        S2U[k] = GU2[0, d].astype(F32) + CRU[0, k].astype(F32) + ZRU[k].astype(F32)
        S2D[k] = GD2[0, d].astype(F32) + CRD[0, k].astype(F32) + ZRD[k].astype(F32)


def backward_kernel(
    XG, QKV, PR, MXH, WQ, WO, RT, OUTS, RESS, CGR, GU, GD, S2U, S2D,
    out, tgrad, pgrad, ograd, egrad, ugrad, dgrad,
    RP, OP, RL, XH, NRM, MG, DQ, NG, NGS, NGR,
    CRU, CRD, ZSU, ZSD, ZRU, ZRD, XSU, XSD, XRU, XRD,
    PW, PC, PXS, PXR, PYS, PYR, PK, PZR,
    OW, OC, OXS, OXR, OK, OZR,
    send, recv,
):
    p = Place()
    g, y, w, x = p.g, p.y, p.w, p.x
    cp = Copies(send, recv)
    greet([p.dev_x, p.dev_c, p.dev_y, p.dev_z(1), p.dev_z(2), p.dev_z(3)])

    def go(*items):
        for item in items:
            item.start()
        return items

    def wait(*items):
        for item in items:
            item.wait()

    own_slots = pl.ds(pl.multiple_of(y * CAP, 16), CAP)
    peer_slots = pl.ds(pl.multiple_of((1 - y) * CAP, 16), CAP)
    ry = go(cp.new(RESS, RP, p.dev_y))
    oy = go(cp.new(OUTS.at[peer_slots, :], OP, p.dev_y))

    f0 = []
    for k, theirs in enumerate((p.gc, p.gd)):
        f0 += go(
            cp.new(GU.at[:, theirs], CRU.at[:, k], p.dev_c),
            cp.new(GD.at[:, theirs], CRD.at[:, k], p.dev_c),
        )
    XSU[1] = S2U[1].astype(BF)
    XSD[1] = S2D[1].astype(BF)
    f2 = {1: go(cp.new(XSU.at[1], XRU.at[1], p.dev_x), cp.new(XSD.at[1], XRD.at[1], p.dev_x))}

    half = pl.ds(pl.multiple_of(x * 512, 512), 512)
    other = pl.ds(pl.multiple_of((1 - x) * 512, 512), 512)
    ugrad[1, :, half] = S2U[0]
    dgrad[1, half, :] = S2D[0]

    values = XG[...].astype(F32)
    centred = values - jnp.mean(values, axis=1, keepdims=True)
    inverse = lax.rsqrt(jnp.mean(centred * centred, axis=1, keepdims=True) + 1e-05)
    XH[...] = centred * inverse
    pick = (
        lax.broadcasted_iota(jnp.int32, (8, EXTRA), 0) == lax.broadcasted_iota(jnp.int32, (8, EXTRA), 1)
    ).astype(F32).astype(BF)
    gain = dot(pick, WQ[:, 1536:], NT)[0:1, :]
    NRM[...] = (XH[...] * gain).astype(BF)

    wait(*f0)
    f1 = []
    for k, d in enumerate((g, p.gx)):
        ZSU[k] = (GU[1, d].astype(F32) + CRU[1, k].astype(F32)).astype(BF)
        ZSD[k] = (GD[1, d].astype(F32) + CRD[1, k].astype(F32)).astype(BF)
        f1 += go(
            cp.new(ZSU.at[k], ZRU.at[k], p.dev_z(2)),
            cp.new(ZSD.at[k], ZRD.at[k], p.dev_z(2)),
        )

    wait(*ry)
    for b in (0, 1):
        slots = slice(b * CAP, (b + 1) * CAP)
        RL[b * 128 : (b + 1) * 128, :] = (
            dot(dispatch_block(RT[b], y), RESS[slots, :], TN)
            + dot(dispatch_block(RT[b], 1 - y), RP[slots, :], TN)
        ).astype(BF)
    MG[...] = dot(RL[...], WO[y], NT).astype(BF)

    def rows4(d):
        return pl.ds(pl.multiple_of(d * 128, 128), 128)

    def out_rows(d):
        OW[rows4(d), :] = dot(MXH[y, :, rows4(d)], RL[...], TN).astype(BF)

    for d in (p.gc, p.gd, g, p.gx):
        out_rows(d)
    oc = []
    for k, theirs in enumerate((p.gc, p.gd)):
        oc += go(cp.new(OW.at[rows4(theirs), :], OC.at[k], p.dev_c))

    low_half = lax.broadcasted_iota(jnp.int32, (256, 128), 1) < 64

    def heads(t, carry):
        c0 = pl.ds(pl.multiple_of(t * 128, 128), 128)
        c1 = pl.ds(pl.multiple_of(512 + t * 128, 128), 128)
        c2 = pl.ds(pl.multiple_of(1024 + t * 128, 128), 128)
        q2, k2, v2, m2 = QKV[:, c0], QKV[:, c1], QKV[:, c2], MG[:, c0]
        parts = []
        for i in (0, 1):
            keep = low_half if i == 0 else ~low_half
            probs = PR[2 * t + i]
            probs_grad = dot(jnp.where(keep, m2, jnp.zeros_like(m2)), v2, NT)
            delta = jnp.sum(probs_grad * probs, axis=1, keepdims=True)
            scores_grad = (probs * (probs_grad - delta)).astype(BF)
            parts.append(
                (
                    dot(scores_grad, k2) * 0.125,
                    dot(scores_grad, q2, TN) * 0.125,
                    dot(probs.astype(BF), m2, TN),
                )
            )
        DQ[:, c0] = jnp.where(low_half, parts[0][0], parts[1][0]).astype(BF)
        DQ[:, c1] = jnp.where(low_half, parts[0][1], parts[1][1]).astype(BF)
        DQ[:, c2] = jnp.where(low_half, parts[0][2], parts[1][2]).astype(BF)
        return carry

    lax.fori_loop(0, 4, heads, 0)

    NG[...] = dot(DQ[...], WQ[:, :1536], NT)
    NGS[...] = NG[pl.ds(pl.multiple_of((1 - y) * 128, 128), 128), :].astype(BF)
    ny = go(cp.new(NGS, NGR, p.dev_y))
    gain_row = jnp.sum(NG[...] * XH[...], axis=0, keepdims=True)

    line = lax.broadcasted_iota(jnp.int32, (8, 1024), 0)
    stack = jnp.where(line == 0, gain_row, jnp.where(line == 1 + y, CGR[0:1, :], 0.0)).astype(BF)

    def dq(d):
        return pl.ds(pl.multiple_of(d * 256, 256), 256)

    def weight_rows(d):
        PW[dq(d), :1536] = dot(NRM[:, dq(d)], DQ[...], TN).astype(BF)

    def weight_loop(t, carry):
        d, cc = lax.rem(t, 2), lax.div(t, 2)
        weight_rows(2 * d + (p.c * cc + (1 - p.c) * (1 - cc)))
        return carry

    PW[:, 1536:] = dot(stack, pick, TN).astype(BF)
    lax.fori_loop(0, 2, weight_loop, 0)
    pc = []
    for k, theirs in enumerate((p.gc, p.gd)):
        pc += go(cp.new(PW.at[dq(theirs), :], PC.at[k], p.dev_c))
    lax.fori_loop(2, 4, weight_loop, 0)

    wait(*oc)
    OXS[...] = (OW[rows4(p.gx), :].astype(F32) + OC[1].astype(F32)).astype(BF)
    ox = go(cp.new(OXS, OXR, p.dev_x))
    wait(*pc)
    PXS[...] = (PW[dq(p.gx), :].astype(F32) + PC[1].astype(F32)).astype(BF)
    px = go(cp.new(PXS, PXR, p.dev_x))

    wait(*ny)
    own_rows = pl.ds(pl.multiple_of(y * 128, 128), 128)
    normed = XH[own_rows, :]
    mine = XG[own_rows, :].astype(F32)
    mine = mine - jnp.mean(mine, axis=1, keepdims=True)
    inverse = lax.rsqrt(jnp.mean(mine * mine, axis=1, keepdims=True) + 1e-05)
    scaled = (NG[own_rows, :] + NGR[...].astype(F32)) * gain
    tgrad[...] = RL[own_rows, :].astype(F32) + inverse * (
        scaled
        - jnp.mean(scaled, axis=1, keepdims=True)
        - normed * jnp.mean(scaled * normed, axis=1, keepdims=True)
    )
    wait(*oy)
    route_own = RT[y]
    out[...] = (
        dot(dispatch_block(route_own, y), OUTS[own_slots, :], TN)
        + dot(dispatch_block(route_own, 1 - y), OP[...], TN)
    ).astype(BF)

    wait(*ox)
    OK[...] = (OW[rows4(g), :].astype(F32) + OC[0].astype(F32) + OXR[...].astype(F32)).astype(BF)

    def row32(v):
        return pl.ds(pl.multiple_of(v * 32, 32), 32)

    oz = []
    for k in (1, 3, 2):
        oz += go(cp.new(OK.at[row32(lax.rem(w + k, 4)), :], OZR.at[k - 1], p.dev_z(k)))
    wait(*px)

    def summed(part):
        rows = pl.ds(pl.multiple_of(part * 128, 128), 128)
        full = pl.ds(pl.multiple_of(g * 256 + part * 128, 128), 128)
        total = PW[full, :].astype(F32) + PC[0, rows, :].astype(F32) + PXR[rows, :].astype(F32)
        return total.astype(BF)

    PYS[...] = summed(1 - y)
    py = go(cp.new(PYS, PYR, p.dev_y))
    PK[...] = summed(y)
    pz = []
    for k in (1, 3, 2):
        pz += go(cp.new(PK.at[row32(lax.rem(w + k, 4)), :], PZR.at[k - 1, 0], p.dev_z(k)))
    wait(*py)
    for k in (1, 3, 2):
        pz += go(cp.new(PYR.at[row32(lax.rem(w + k, 4)), :], PZR.at[k - 1, 1], p.dev_z(k)))

    wait(*f1)
    ugrad[0, :, half] = GU[0, g].astype(F32) + CRU[0, 0].astype(F32) + ZRU[0].astype(F32)
    dgrad[0, half, :] = GD[0, g].astype(F32) + CRD[0, 0].astype(F32) + ZRD[0].astype(F32)
    XSU[0] = (GU[0, p.gx].astype(F32) + CRU[0, 1].astype(F32) + ZRU[1].astype(F32)).astype(BF)
    XSD[0] = (GD[0, p.gx].astype(F32) + CRD[0, 1].astype(F32) + ZRD[1].astype(F32)).astype(BF)
    f2[0] = go(cp.new(XSU.at[0], XRU.at[0], p.dev_x), cp.new(XSD.at[0], XRD.at[0], p.dev_x))
    for s in (1, 0):
        wait(*f2[s])
        ugrad[s, :, other] = XRU[s].astype(F32)
        dgrad[s, other, :] = XRD[s].astype(F32)

    wait(*oz)
    own32 = row32(w)
    ograd[...] = (
        OK[own32, :].astype(F32) + OZR[0].astype(F32) + OZR[1].astype(F32) + OZR[2].astype(F32)
    )
    wait(*pz)
    sums = []
    for i, kept in enumerate((PK, PYR)):
        sums.append(
            kept[own32, :].astype(F32)
            + PZR[0, i].astype(F32)
            + PZR[1, i].astype(F32)
            + PZR[2, i].astype(F32)
        )
    pgrad[y] = sums[0][:, :1536]
    pgrad[1 - y] = sums[1][:, :1536]
    egrad[...] = sums[0][:, 1536:] + sums[1][:, 1536:]


def vmem(shape, dtype=BF):
    return pltpu.VMEM(shape, dtype)


def fast_shards(
    tokens, cotangent, norm_gain, project_weight, output_weight, centroids,
    expert_up, expert_down, sequence_lengths, block_order, routes,
):
    in_vmem = pl.BlockSpec(memory_space=pltpu.VMEM)
    in_any = pl.BlockSpec(memory_space=pl.ANY)
    in_smem = pl.BlockSpec(memory_space=pltpu.SMEM)
    shape = jax.ShapeDtypeStruct
    extra = jnp.concatenate(
        [norm_gain[:, None], centroids.T, jnp.zeros((32, EXTRA - 3), BF)], axis=1
    )
    by_plane = project_weight.reshape(32, 3, 4, 2, 128).transpose(3, 0, 1, 2, 4).reshape(2, 32, 1536)
    wq = jnp.concatenate([by_plane, jnp.broadcast_to(extra[None], (2, 32, EXTRA))], axis=2)
    meta = jnp.concatenate([sequence_lengths[0], block_order[0]])
    rts = jnp.broadcast_to(routes[0, :, 0].astype(F32)[None, :], (8, 128))
    mid_shapes = [
        ((256, 1024), BF),
        ((256, 1536), BF),
        ((8, 256, 256), F32),
        ((2, 256, 512), BF),
        ((1024, 1536 + EXTRA), BF),
        ((2, 512, 1024), BF),
        ((2, 8, 128), F32),
        ((160, 1024), BF),
        ((160, 1024), BF),
        ((8, 1024), F32),
        ((2, 4, 256, 512), BF),
        ((2, 4, 512, 256), BF),
        ((2, 256, 512), F32),
        ((2, 512, 256), F32),
    ]
    mid = pl.pallas_call(
        forward_kernel,
        name="forward",
        out_shape=[shape(*s) for s in mid_shapes],
        in_specs=[in_smem] + [in_vmem] * 5 + [in_any] * 2,
        out_specs=[in_vmem] * len(mid_shapes),
        scratch_shapes=[
            vmem((128, 1536 + EXTRA)),
            vmem((256, 1024)),
            vmem((256, 1024), F32),
            vmem((256, 1024)),
            vmem((2, 2, 1024, 512)),
            vmem((2, 2, 512, 1024)),
            vmem((2, CAP, 128)),
            vmem((160, 1024), F32),
            vmem((160, 1024)),
            vmem((2, 160, 512)),
            vmem((160, 1024), F32),
        ]
        + [vmem((640, 1024))] * 4
        + [
            vmem((4, 3, 160, 1024)),
            vmem((3, 3, 160, 1024)),
            vmem((3, 160, 1024), F32),
            vmem((640, 1024), F32),
            vmem((640, 1024)),
            vmem((640, 1024)),
            vmem((640, 1024)),
            vmem((2, 160, 1024), F32),
            vmem((2, 4, 256, 512)),
            vmem((2, 4, 512, 256)),
            vmem((2, 2, 256, 512)),
            vmem((2, 2, 512, 256)),
            vmem((2, 256, 512)),
            vmem((2, 512, 256)),
            vmem((2, 256, 512)),
            vmem((2, 512, 256)),
            pltpu.SemaphoreType.DMA((96,)),
            pltpu.SemaphoreType.DMA((96,)),
            pltpu.SemaphoreType.DMA((12,)),
        ],
        compiler_params=pltpu.CompilerParams(
            collective_id=0, has_side_effects=True, vmem_limit_bytes=VMEM_LIMIT
        ),
    )(meta, tokens[0], cotangent[0], rts, wq, output_weight, expert_up[0], expert_down[0])
    out_shapes = [
        ((128, 1024), BF),
        ((128, 1024), F32),
        ((2, 32, 1536), F32),
        ((32, 1024), F32),
        ((32, EXTRA), F32),
        ((2, 256, 1024), F32),
        ((2, 1024, 256), F32),
    ]
    out, tgrad, pgrad, ograd, egrad, ugrad, dgrad = pl.pallas_call(
        backward_kernel,
        name="backward",
        out_shape=[shape(*s) for s in out_shapes],
        in_specs=[in_vmem] * len(mid_shapes),
        out_specs=[in_vmem] * len(out_shapes),
        scratch_shapes=[
            vmem((160, 1024)),
            vmem((CAP, 1024)),
            vmem((256, 1024)),
            vmem((256, 1024), F32),
            vmem((256, 1024)),
            vmem((256, 512)),
            vmem((256, 1536)),
            vmem((256, 1024), F32),
            vmem((128, 1024)),
            vmem((128, 1024)),
            vmem((2, 2, 256, 512)),
            vmem((2, 2, 512, 256)),
            vmem((2, 256, 512)),
            vmem((2, 512, 256)),
            vmem((2, 256, 512)),
            vmem((2, 512, 256)),
            vmem((2, 256, 512)),
            vmem((2, 512, 256)),
            vmem((2, 256, 512)),
            vmem((2, 512, 256)),
            vmem((1024, 1536 + EXTRA)),
            vmem((2, 256, 1536 + EXTRA)),
            vmem((256, 1536 + EXTRA)),
            vmem((256, 1536 + EXTRA)),
            vmem((128, 1536 + EXTRA)),
            vmem((128, 1536 + EXTRA)),
            vmem((128, 1536 + EXTRA)),
            vmem((3, 2, 32, 1536 + EXTRA)),
            vmem((512, 1024)),
            vmem((2, 128, 1024)),
            vmem((128, 1024)),
            vmem((128, 1024)),
            vmem((128, 1024)),
            vmem((3, 32, 1024)),
            pltpu.SemaphoreType.DMA((48,)),
            pltpu.SemaphoreType.DMA((48,)),
        ],
        compiler_params=pltpu.CompilerParams(
            collective_id=1, has_side_effects=True, vmem_limit_bytes=VMEM_LIMIT
        ),
    )(*mid)
    project_grad = pgrad.reshape(2, 32, 3, 4, 128).transpose(1, 2, 3, 0, 4).reshape(32, 3072)
    return (
        out[None],
        tgrad[None],
        egrad[:, 0],
        project_grad,
        ograd,
        egrad[:, 1:3].T,
        ugrad[None],
        dgrad[None],
    )


def solution(mesh):
    sizes = dict(mesh.shape)
    fast = sizes == {"grp": 4, "ctx": 2, "wsh": 4}
    return jax.shard_map(
        fast_shards if fast else shards,
        mesh=mesh,
        in_specs=IN_SPECS,
        out_specs=OUT_SPECS,
        check_vma=False,
    )
```

```python
import math

import jax
import jax.numpy as jnp
from jax import lax
from jax.experimental import pallas as pl
from jax.experimental.pallas import tpu as pltpu
from jax.sharding import PartitionSpec as P

HEADS = 16
HDIM = 64
BLK = 128


precise = lax.Precision.HIGHEST


def place_rows(order_row, lengths_row, total_rows):
    row_index = jnp.arange(total_rows, dtype=jnp.int32)
    picked = (row_index // BLK)[:, None] == jnp.arange(order_row.shape[0], dtype=jnp.int32)[None, :]
    blocks = jnp.sum(jnp.where(picked, order_row[None, :], 0), axis=1)
    token_place = blocks * BLK + row_index % BLK
    bounds = jnp.cumsum(lengths_row)
    sequence = jnp.sum((token_place[:, None] >= bounds[None, :]).astype(jnp.int32), axis=1)
    return (token_place, sequence)


def normalize(values):
    average = jnp.mean(values, axis=-1, keepdims=True)
    centred = values - average
    inverse = lax.rsqrt(jnp.mean(centred * centred, axis=-1, keepdims=True) + 1e-05)
    return (centred * inverse, inverse)


def head_slice(matrix, section, offset, heads_per):
    width_part = heads_per * HDIM
    first_col = offset + section * width_part
    return matrix[:, first_col : first_col + width_part].reshape(matrix.shape[0], heads_per, HDIM)


def spread_rows(local_rows):
    return lax.all_gather(local_rows, "wsh", axis=0, tiled=True)


def collect_rows(partial_term):
    return lax.psum_scatter(
        partial_term.astype(jnp.bfloat16), "wsh", scatter_dimension=0, tiled=True
    ).astype(jnp.float32)


def trade_rows(slots_rows, peer_count, capacity):
    shaped = slots_rows.reshape(peer_count, capacity, slots_rows.shape[-1])
    moved = lax.all_to_all(shaped, "ctx", split_axis=0, concat_axis=0, tiled=True)
    return moved.reshape(peer_count * capacity, slots_rows.shape[-1])


def gelu_pullback(hidden, incoming):
    value_out, pullback = jax.vjp(jax.nn.gelu, hidden)
    return pullback(incoming)[0]


def shards(
    tokens,
    cotangent,
    norm_gain,
    project_weight,
    output_weight,
    centroids,
    expert_up,
    expert_down,
    sequence_lengths,
    block_order,
    routes,
):
    local_rows = tokens.shape[1]
    model_width = tokens.shape[2]
    peer_count = lax.axis_size("ctx")
    position = lax.axis_index("ctx")
    total_rows = local_rows * peer_count
    capacity = max(2, (5 * local_rows + 4 * peer_count - 1) // (4 * peer_count))
    slot_count = peer_count * capacity
    score_scale = 1.0 / math.sqrt(HDIM)
    heads_per = 4
    sections = HEADS // heads_per
    inputs_f = tokens[0].astype(jnp.float32)
    upstream = cotangent[0].astype(jnp.float32)
    project_full, output_full, gain_full, centroid_full = (
        lax.all_gather(project_weight, ("grp", "ctx", "wsh"), axis=0, tiled=True),
        lax.all_gather(output_weight, ("grp", "ctx", "wsh"), axis=0, tiled=True),
        lax.all_gather(norm_gain, ("grp", "ctx", "wsh"), axis=0, tiled=True),
        lax.all_gather(centroids, ("grp", "ctx", "wsh"), axis=1, tiled=True),
    )
    up_full, down_full = (
        lax.all_gather(expert_up, "grp", axis=2, tiled=True),
        lax.all_gather(expert_down, "grp", axis=3, tiled=True),
    )
    place_all, sequence_all = place_rows(block_order[0], sequence_lengths[0], total_rows)
    place_own = lax.dynamic_slice_in_dim(place_all, position * local_rows, local_rows)
    sequence_own = lax.dynamic_slice_in_dim(sequence_all, position * local_rows, local_rows)
    allowed = (sequence_own[:, None] == sequence_all[None, :]) & (
        place_all[None, :] <= place_own[:, None]
    )
    normed, inverse = normalize(inputs_f)
    gain_values = gain_full.astype(jnp.float32)
    normed_low = (normed * gain_values).astype(jnp.bfloat16)
    projected = jnp.dot(normed_low, project_full, preferred_element_type=jnp.float32)
    queries = projected[:, :model_width].astype(jnp.bfloat16)
    keyvalue = projected[:, model_width:].astype(jnp.bfloat16)
    keyvalue_all = lax.all_gather(keyvalue, "ctx", axis=0, tiled=True)
    mixed_parts = []
    logsum_parts = []
    for section in range(sections):
        head_query = head_slice(queries, section, 0, heads_per)
        head_key = head_slice(keyvalue_all, section, 0, heads_per)
        head_value = head_slice(keyvalue_all, section, model_width, heads_per)
        scores = (
            jnp.einsum("tgd,sgd->gts", head_query, head_key, preferred_element_type=jnp.float32)
            * score_scale
        )
        scores = jnp.where(allowed[None], scores, -1000000000.0)
        largest = jnp.max(scores, axis=-1, keepdims=True)
        exponent = jnp.exp(scores - largest)
        totals = jnp.sum(exponent, axis=-1, keepdims=True)
        weights = (exponent / totals).astype(jnp.bfloat16)
        mixed_part = jnp.einsum(
            "gts,sgd->tgd", weights, head_value, preferred_element_type=jnp.float32
        )
        mixed_parts.append(mixed_part.reshape(local_rows, heads_per * HDIM))
        logsum_parts.append((largest + jnp.log(totals))[:, :, 0])
    mixed_all = jnp.concatenate(mixed_parts, axis=1).astype(jnp.bfloat16)
    logsum = jnp.concatenate(logsum_parts, axis=0)
    after_attention = inputs_f + jnp.dot(mixed_all, output_full, preferred_element_type=jnp.float32)
    route_ids = routes[0, :, 0]
    member = route_ids[:, None] == jnp.arange(peer_count, dtype=jnp.int32)[None, :]
    member_f = member.astype(jnp.float32)
    picked_centroid = jnp.dot(member_f, centroid_full.astype(jnp.float32), precision=precise)
    gate_value = jax.nn.sigmoid(jnp.sum(after_attention * picked_centroid, axis=-1))
    member_int = member.astype(jnp.int32)
    ranking = jnp.sum((jnp.cumsum(member_int, axis=0) - 1) * member_int, axis=1)
    slot_index = route_ids * capacity + ranking
    dispatch = (slot_index[None, :] == jnp.arange(slot_count, dtype=jnp.int32)[:, None]).astype(
        jnp.bfloat16
    )
    sent_rows = jnp.dot(
        dispatch, after_attention.astype(jnp.bfloat16), preferred_element_type=jnp.float32
    ).astype(jnp.bfloat16)
    arrived = trade_rows(sent_rows, peer_count, capacity)
    up_first = up_full[0, 0]
    up_second = up_full[0, 1]
    down_first = down_full[0, 0]
    down_second = down_full[0, 1]
    gathered_one = spread_rows(arrived)
    hidden_one = jnp.dot(gathered_one, up_first, preferred_element_type=jnp.float32)
    active_one = jax.nn.gelu(hidden_one).astype(jnp.bfloat16)
    branch_one = collect_rows(jnp.dot(active_one, down_first, preferred_element_type=jnp.float32))
    middle = (arrived.astype(jnp.float32) + branch_one).astype(jnp.bfloat16)
    gathered_two = spread_rows(middle)
    hidden_two = jnp.dot(gathered_two, up_second, preferred_element_type=jnp.float32)
    active_two = jax.nn.gelu(hidden_two).astype(jnp.bfloat16)
    branch_two = collect_rows(jnp.dot(active_two, down_second, preferred_element_type=jnp.float32))
    expert_out = (branch_one + branch_two).astype(jnp.bfloat16)
    returned = trade_rows(expert_out, peer_count, capacity)
    returned_tok = jnp.einsum("st,sd->td", dispatch, returned, preferred_element_type=jnp.float32)
    output = after_attention + gate_value[:, None] * returned_tok
    gate_grad = jnp.sum(upstream * returned_tok, axis=-1)
    score_grad = gate_grad * gate_value * (1.0 - gate_value)
    centroid_term = jnp.dot(member_f.T, score_grad[:, None] * after_attention, precision=precise)
    branch_grad = (gate_value[:, None] * upstream).astype(jnp.bfloat16)
    branch_sent = jnp.dot(dispatch, branch_grad, preferred_element_type=jnp.float32).astype(
        jnp.bfloat16
    )
    branch_arrived = trade_rows(branch_sent, peer_count, capacity)
    grad_two = spread_rows(branch_arrived)
    hidden_two_grad = gelu_pullback(
        hidden_two, jnp.dot(grad_two, down_second.T, preferred_element_type=jnp.float32)
    ).astype(jnp.bfloat16)
    down_second_grad = jnp.dot(active_two.T, grad_two, preferred_element_type=jnp.float32)
    up_second_grad = jnp.dot(gathered_two.T, hidden_two_grad, preferred_element_type=jnp.float32)
    middle_grad = collect_rows(
        jnp.dot(hidden_two_grad, up_second.T, preferred_element_type=jnp.float32)
    )
    first_branch_grad = (branch_arrived.astype(jnp.float32) + middle_grad).astype(jnp.bfloat16)
    grad_one = spread_rows(first_branch_grad)
    hidden_one_grad = gelu_pullback(
        hidden_one, jnp.dot(grad_one, down_first.T, preferred_element_type=jnp.float32)
    ).astype(jnp.bfloat16)
    down_first_grad = jnp.dot(active_one.T, grad_one, preferred_element_type=jnp.float32)
    up_first_grad = jnp.dot(gathered_one.T, hidden_one_grad, preferred_element_type=jnp.float32)
    arrived_grad = (
        collect_rows(jnp.dot(hidden_one_grad, up_first.T, preferred_element_type=jnp.float32))
        + middle_grad
    ).astype(jnp.bfloat16)
    home_grad = trade_rows(arrived_grad, peer_count, capacity)
    home_grad_tok = jnp.einsum("st,sd->td", dispatch, home_grad, preferred_element_type=jnp.float32)
    up_terms = jnp.stack([up_first_grad, up_second_grad])[None]
    down_terms = jnp.stack([down_first_grad, down_second_grad])[None]
    up_grad_out, down_grad_out = (
        lax.psum_scatter(
            up_terms.astype(jnp.bfloat16), "grp", scatter_dimension=2, tiled=True
        ).astype(jnp.float32),
        lax.psum_scatter(
            down_terms.astype(jnp.bfloat16), "grp", scatter_dimension=3, tiled=True
        ).astype(jnp.float32),
    )
    residual_grad = upstream + score_grad[:, None] * picked_centroid + home_grad_tok
    residual_low = residual_grad.astype(jnp.bfloat16)
    output_term = jnp.dot(mixed_all.T, residual_low, preferred_element_type=jnp.float32)
    mixed_grad = jnp.dot(residual_low, output_full.T, preferred_element_type=jnp.float32).astype(
        jnp.bfloat16
    )
    query_grads = []
    key_grads = []
    value_grads = []
    delta_parts = []
    for section in range(sections):
        head_query = head_slice(queries, section, 0, heads_per)
        head_key = head_slice(keyvalue_all, section, 0, heads_per)
        head_value = head_slice(keyvalue_all, section, model_width, heads_per)
        head_grad = head_slice(mixed_grad, section, 0, heads_per)
        scores = (
            jnp.einsum("tgd,sgd->gts", head_query, head_key, preferred_element_type=jnp.float32)
            * score_scale
        )
        scores = jnp.where(allowed[None], scores, -1000000000.0)
        probs = jnp.exp(
            scores - logsum[section * heads_per : (section + 1) * heads_per][:, :, None]
        )
        probs_grad = jnp.einsum(
            "tgd,sgd->gts", head_grad, head_value, preferred_element_type=jnp.float32
        )
        row_delta = jnp.sum(probs_grad * probs, axis=-1)
        scores_grad = (probs * (probs_grad - row_delta[:, :, None])).astype(jnp.bfloat16)
        query_part = (
            jnp.einsum("gts,sgd->tgd", scores_grad, head_key, preferred_element_type=jnp.float32)
            * score_scale
        )
        query_grads.append(query_part.reshape(local_rows, heads_per * HDIM))
        delta_parts.append(row_delta)
        key_part = (
            jnp.einsum("gts,tgd->sgd", scores_grad, head_query, preferred_element_type=jnp.float32)
            * score_scale
        )
        value_part = jnp.einsum(
            "gts,tgd->sgd",
            probs.astype(jnp.bfloat16),
            head_grad,
            preferred_element_type=jnp.float32,
        )
        key_grads.append(key_part.reshape(total_rows, heads_per * HDIM))
        value_grads.append(value_part.reshape(total_rows, heads_per * HDIM))
    query_grad = jnp.concatenate(query_grads, axis=1).astype(jnp.bfloat16)
    keyvalue_terms = jnp.concatenate(key_grads + value_grads, axis=1)
    keyvalue_grad = lax.psum_scatter(
        keyvalue_terms.astype(jnp.bfloat16), "ctx", scatter_dimension=0, tiled=True
    )
    projected_grad = jnp.concatenate([query_grad, keyvalue_grad], axis=1)
    project_term = jnp.dot(normed_low.T, projected_grad, preferred_element_type=jnp.float32)
    normed_grad = jnp.dot(projected_grad, project_full.T, preferred_element_type=jnp.float32)
    gain_term = jnp.sum(normed_grad * normed, axis=0)
    scaled_grad = normed_grad * gain_values
    input_grad = residual_grad + inverse * (
        scaled_grad
        - jnp.mean(scaled_grad, axis=-1, keepdims=True)
        - normed * jnp.mean(scaled_grad * normed, axis=-1, keepdims=True)
    )
    project_grad, output_grad, gain_grad, centroid_grad = (
        lax.psum_scatter(project_term, ("grp", "ctx", "wsh"), scatter_dimension=0, tiled=True),
        lax.psum_scatter(output_term, ("grp", "ctx", "wsh"), scatter_dimension=0, tiled=True),
        lax.psum_scatter(gain_term, ("grp", "ctx", "wsh"), scatter_dimension=0, tiled=True),
        lax.psum_scatter(centroid_term, ("grp", "ctx", "wsh"), scatter_dimension=1, tiled=True),
    )
    return (
        output.astype(jnp.bfloat16)[None],
        input_grad[None],
        gain_grad,
        project_grad,
        output_grad,
        centroid_grad,
        up_grad_out,
        down_grad_out,
    )


VMEM_LIMIT = 60 * 2**20

IN_SPECS = (
    P(("grp", "wsh"), "ctx", None),
    P(("grp", "wsh"), "ctx", None),
    P(("grp", "ctx", "wsh")),
    P(("grp", "ctx", "wsh"), None),
    P(("grp", "ctx", "wsh"), None),
    P(None, ("grp", "ctx", "wsh")),
    P("ctx", None, "grp", "wsh"),
    P("ctx", None, "wsh", "grp"),
    P(("grp", "wsh"), None),
    P(("grp", "wsh"), None),
    P(("grp", "wsh"), "ctx", None),
)
OUT_SPECS = (
    P(("grp", "wsh"), "ctx", None),
    P(("grp", "wsh"), "ctx", None),
    P(("grp", "ctx", "wsh")),
    P(("grp", "ctx", "wsh"), None),
    P(("grp", "ctx", "wsh"), None),
    P(None, ("grp", "ctx", "wsh")),
    P("ctx", None, "grp", "wsh"),
    P("ctx", None, "wsh", "grp"),
)

BF = jnp.bfloat16
F32 = jnp.float32
NN = ((1,), (0,))
NT = ((1,), (1,))
TN = ((0,), (0,))
MESH = pl.DeviceIdType.MESH
GELU_C = 0.7978845608028654
EXTRA = 128
CAP = 80


def dot(a, b, dims=NN):
    return lax.dot_general(a, b, (dims, ((), ())), preferred_element_type=F32)


def gelu_both(h):
    sq = h * h
    t = jnp.tanh(GELU_C * h * (1.0 + 0.044715 * sq))
    half = 0.5 * (1.0 + t)
    slope = half + 0.5 * h * (1.0 - t * t) * (GELU_C * (1.0 + 3.0 * 0.044715 * sq))
    return h * half, slope


def copy_in(src, dst, sem):
    return pltpu.make_async_copy(src, dst, sem)


class Copies:
    def __init__(self, send, recv):
        self.send, self.recv, self.used = send, recv, 0

    def block(self, count):
        first = self.used
        self.used += count
        return first

    def at(self, index, src, dst, device):
        return pltpu.make_async_remote_copy(
            src_ref=src,
            dst_ref=dst,
            send_sem=self.send.at[index],
            recv_sem=self.recv.at[index],
            device_id=device,
            device_id_type=MESH,
        )

    def new(self, src, dst, device):
        return self.at(self.block(1), src, dst, device)


class Place:
    def __init__(self):
        g, y, w = lax.axis_index("grp"), lax.axis_index("ctx"), lax.axis_index("wsh")
        self.g, self.y, self.w = g, y, w
        self.x = lax.div(g, 2)
        self.c = g - 2 * self.x
        self.gx = 2 * (1 - self.x) + self.c
        self.gc = 2 * self.x + 1 - self.c
        self.gd = 2 * (1 - self.x) + 1 - self.c
        self.wb = lax.rem(w, 2)
        self.w1 = w + 1 - 2 * self.wb
        self.w2 = lax.rem(w + 2, 4)
        self.dev_x = (self.gx, y, w)
        self.dev_c = (self.gc, y, w)
        self.dev_y = (g, 1 - y, w)
        self.dev_pair = (g, y, self.w1)
        self.dev_z = lambda k: (g, y, lax.rem(w + k, 4))

    def team_places(self):
        mine = 2 * self.x + lax.div(self.w, 2)
        x_side = 2 * (1 - self.x) + lax.div(self.w, 2)
        flip = 1 - 2 * lax.div(self.w, 2)
        return mine, x_side, mine + flip, x_side + flip


def greet(devices):
    barrier = pltpu.get_barrier_semaphore()
    for device in devices:
        pl.semaphore_signal(barrier, inc=1, device_id=device, device_id_type=MESH)
    return lambda: pl.semaphore_wait(barrier, len(devices))


def one_hot(rows, columns):
    same = lax.broadcasted_iota(jnp.int32, (rows, columns), 0) == lax.broadcasted_iota(
        jnp.int32, (rows, columns), 1
    )
    return same.astype(F32).astype(BF)


def dispatch_block(route_rows, expert):
    member = (route_rows == expert.astype(F32)).astype(F32)
    earlier = lax.broadcasted_iota(jnp.int32, (128, 128), 0) < lax.broadcasted_iota(jnp.int32, (128, 128), 1)
    rank = dot(member.astype(BF), earlier.astype(F32).astype(BF))
    slot = lax.broadcasted_iota(jnp.int32, (CAP, 128), 0).astype(F32)
    hit = (jnp.broadcast_to(rank[0:1, :], (CAP, 128)) == slot) & (
        jnp.broadcast_to(member[0:1, :], (CAP, 128)) > 0.5
    )
    return hit.astype(F32).astype(BF)


def place_of(lengths, order, index):
    place = jnp.where(index < 128, order[0], order[1]) * 128 + lax.rem(index, 128)
    bound = lengths[0]
    sequence = jnp.where(place >= bound, 1, 0)
    for part in (1, 2):
        bound = bound + lengths[part]
        sequence = sequence + jnp.where(place >= bound, 1, 0)
    return place, sequence


def forward_kernel(
    lengths, order, tok, cot, rts, pw, wo_in, ext, up_in, dn_in,
    XG, QKV, PR, MXH, W0, W1, W2, WO, RT, OUTS, RESS, CGR, P1U, P1D, Z1U, Z1D, S2U, S2D,
    WS0, WS1, WS2, CG, XH, NRM, UP, DN, DSP, XS, GS, MS, AA,
    R1, R2, R3, R4, RB, PS, OWN, RES, GP1, A1, A2, DH, SUMS,
    GU, GD, CRU, CRD, P2U, P2D, ZSU, ZSD, ZRU, ZRD,
    send, recv, local,
):
    p = Place()
    g, y, w, x = p.g, p.y, p.w, p.x
    cp = Copies(send, recv)
    all_in = greet([p.dev_x, p.dev_c, p.dev_y, p.dev_z(1), p.dev_z(2), p.dev_z(3)])
    nlocal = [0]

    def here(src, dst):
        nlocal[0] += 1
        return copy_in(src, dst, local.at[nlocal[0] - 1])

    def go(*items):
        for item in items:
            item.start()
        return items

    def wait(*items):
        for item in items:
            item.wait()

    W, WS = (W0, W1, W2), (WS0, WS1, WS2)
    for ch in range(3):
        for t in range(4):
            for plane in (0, 1):
                first = ch * 1024 + t * 256 + plane * 128
                WS[ch][plane, :, t * 128 : (t + 1) * 128] = pw[:, first : first + 128]
    extra_rows = jnp.concatenate([ext[...], jnp.zeros((EXTRA - 8, EXTRA), F32)], axis=0).astype(BF)
    extra_cols = dot(one_hot(32, EXTRA), extra_rows, NT).astype(BF)
    WS0[0, :, 512:] = extra_cols
    WS0[1, :, 512:] = extra_cols
    RT[y] = jnp.broadcast_to(rts[...].astype(F32), (8, 128))
    mine = pl.ds(pl.multiple_of(y * 128, 128), 128)
    XG[mine, :] = tok[...]
    CG[mine, :] = cot[...]

    def row(plane):
        return pl.ds(pl.multiple_of(g * 256 + plane * 128 + w * 32, 32), 32)

    for ch in range(3):
        W[ch][row(y), :] = WS[ch][y]
    row_o = pl.ds(pl.multiple_of(g * 128 + w * 32, 32), 32)
    WO[y, row_o, :] = wo_in[...]
    all_in()

    def z_rows(ch, plane):
        return sum(
            (go(cp.new(W[ch].at[row(plane), :], W[ch].at[row(plane), :], p.dev_z(k))) for k in (2, 1, 3)), ()
        )

    yw = [go(cp.new(WS[ch].at[1 - y], W[ch].at[row(y), :], p.dev_y)) for ch in range(3)]
    zo = sum((go(cp.new(wo_in, WO.at[y, row_o, :], p.dev_z(k))) for k in (2, 1, 3)), ())
    zw = [z_rows(0, y), (), ()]
    ty = go(cp.new(RT.at[y], RT.at[y], p.dev_y), cp.new(tok, XG.at[mine, :], p.dev_y))

    def dq(q):
        return pl.ds(pl.multiple_of(q * 256, 256), 256)

    half = pl.ds(pl.multiple_of(x * 512, 512), 512)
    other = pl.ds(pl.multiple_of((1 - x) * 512, 512), 512)

    def e_first(s):
        return go(
            cp.new(up_in.at[s, :, other], UP.at[s, 0, dq(g), :], p.dev_x),
            cp.new(dn_in.at[s, other, :], DN.at[s, 0, :, dq(g)], p.dev_x),
        )

    def e_core0(s):
        return go(
            cp.new(up_in.at[s, :, half], UP.at[s, 0, dq(g), :], p.dev_c),
            cp.new(dn_in.at[s, half, :], DN.at[s, 0, :, dq(g)], p.dev_c),
        )

    def e_local(s):
        return go(
            here(up_in.at[s, :, half], UP.at[s, 0, dq(g), :]),
            here(dn_in.at[s, half, :], DN.at[s, 0, :, dq(g)]),
        )

    def e_z(s):
        return go(
            cp.new(up_in.at[s, :, half], UP.at[s, 1, dq(g), :], p.dev_pair),
            cp.new(dn_in.at[s, half, :], DN.at[s, 1, :, dq(g)], p.dev_pair),
        )

    def e_relay(s):
        return go(
            cp.new(UP.at[s, 0, dq(p.gx), :], UP.at[s, 1, dq(p.gx), :], p.dev_pair),
            cp.new(DN.at[s, 0, :, dq(p.gx)], DN.at[s, 1, :, dq(p.gx)], p.dev_pair),
        )

    def e_core(s, q, which):
        return go(
            cp.new(UP.at[s, q, dq(which), :], UP.at[s, q, dq(which), :], p.dev_c),
            cp.new(DN.at[s, q, :, dq(which)], DN.at[s, q, :, dq(which)], p.dev_c),
        )

    wait(*yw[0])
    zw[0] += z_rows(0, 1 - y)
    for ch in (1, 2):
        wait(*yw[ch])
        zw[ch] = z_rows(ch, y) + z_rows(ch, 1 - y)
    el = e_local(0) + e_local(1)
    ec0 = [e_core0(0)]

    wait(*ty)
    values = XG[...].astype(F32)
    centred = values - jnp.mean(values, axis=1, keepdims=True)
    inverse = lax.rsqrt(jnp.mean(centred * centred, axis=1, keepdims=True) + 1e-05)
    XH[...] = centred * inverse
    for b in (0, 1):
        DSP[b] = dispatch_block(RT[b], y)
        XS[b * CAP : (b + 1) * CAP, :] = dot(DSP[b], XG[b * 128 : (b + 1) * 128, :])

    def quarter(d):
        return pl.ds(pl.multiple_of(d * 128, 128), 128)

    def wo_copy(plane, d, device):
        return cp.new(WO.at[plane, quarter(d), :], WO.at[plane, quarter(d), :], device)

    def w_copy(ch, d, device):
        return cp.new(W[ch].at[dq(d), :], W[ch].at[dq(d), :], device)

    xw, fw = [None] * 3, [None] * 3
    wait(*zo)
    xo = go(wo_copy(y, g, p.dev_x))
    wait(*zw[0])
    xw[0] = go(w_copy(0, g, p.dev_x), w_copy(0, g, p.dev_c))
    wait(*xo)
    yo = go(wo_copy(y, g, p.dev_y), wo_copy(y, p.gx, p.dev_y))
    co = go(wo_copy(y, g, p.dev_c), wo_copy(y, p.gx, p.dev_c))
    wait(*zw[1])
    xw[1] = go(w_copy(1, g, p.dev_x), w_copy(1, g, p.dev_c))
    wait(*zw[2])
    xw[2] = go(w_copy(2, g, p.dev_x), w_copy(2, g, p.dev_c))
    ez = [e_z(0), e_z(1)]
    e1 = [e_first(0), e_first(1)]
    ec0.append(e_core0(1))
    cy = go(cp.new(cot, CG.at[mine, :], p.dev_y))
    wait(*xw[0])
    fw[0] = go(w_copy(0, p.gx, p.dev_c))
    wait(*fw[0])
    extra = dot(one_hot(8, EXTRA), W0[:, 512:], NT)
    gain = extra[0:1, :]
    centroid = jnp.where(y == 0, extra[1:2, :], extra[2:3, :])
    NRM[...] = (XH[...] * gain).astype(BF)

    def project(ch):
        QKV[:, ch * 512 : (ch + 1) * 512] = dot(NRM[...], W[ch][:, :512]).astype(BF)

    project(0)
    wait(*xw[1])
    fw[1] = go(w_copy(1, p.gx, p.dev_c))
    wait(*fw[1])
    project(1)
    wait(*yo)
    co += go(wo_copy(1 - y, g, p.dev_c), wo_copy(1 - y, p.gx, p.dev_c))
    wait(*xw[2])
    fw[2] = go(w_copy(2, p.gx, p.dev_c))
    wait(*fw[2])
    project(2)

    place_q, seq_q = place_of(lengths, order, lax.broadcasted_iota(jnp.int32, (256, 256), 0))
    place_k, seq_k = place_of(lengths, order, lax.broadcasted_iota(jnp.int32, (256, 256), 1))
    allowed = (seq_q == seq_k) & (place_k <= place_q)
    low_half = lax.broadcasted_iota(jnp.int32, (256, 128), 1) < 64
    mixed_first = cp.block(4)

    def mixed_copy(t):
        cols = pl.ds(pl.multiple_of(t * 128, 128), 128)
        return cp.at(mixed_first + t, MXH.at[y, :, cols], MXH.at[y, :, cols], p.dev_y)

    def heads(t, carry):
        cols = pl.ds(pl.multiple_of(t * 128, 128), 128)
        q2 = QKV[:, cols]
        k2 = QKV[:, pl.ds(pl.multiple_of(512 + t * 128, 128), 128)]
        v2 = QKV[:, pl.ds(pl.multiple_of(1024 + t * 128, 128), 128)]
        parts = []
        for i in (0, 1):
            keep = low_half if i == 0 else ~low_half
            scores = dot(jnp.where(keep, q2, jnp.zeros_like(q2)), k2, NT) * 0.125
            scores = jnp.where(allowed, scores, -1000000000.0)
            exponent = jnp.exp(scores - jnp.max(scores, axis=1, keepdims=True))
            probs = exponent / jnp.sum(exponent, axis=1, keepdims=True)
            PR[2 * t + i] = probs
            parts.append(dot(probs.astype(BF), v2))
        MXH[y, :, cols] = jnp.where(low_half, parts[0], parts[1]).astype(BF)
        mixed_copy(t).start()
        return carry

    lax.fori_loop(0, 4, heads, 0)

    def mixed_pick(yy):
        for b in (0, 1):
            MS[yy, b * CAP : (b + 1) * CAP, :] = dot(DSP[b], MXH[yy, b * 128 : (b + 1) * 128, :]).astype(BF)

    wait(*e1[0])
    er = [e_relay(0)]
    ec = [e_core(0, 0, p.gx)]
    mixed_pick(y)
    wait(*cy)
    for b in (0, 1):
        GS[b * CAP : (b + 1) * CAP, :] = dot(DSP[b], CG[b * 128 : (b + 1) * 128, :]).astype(BF)
    wait(*co)
    AA[...] = XS[...] + dot(MS[y], WO[y])
    lax.fori_loop(0, 4, lambda t, carry: (mixed_copy(t).wait(), carry)[1], 0)
    mixed_pick(1 - y)
    AA[...] += dot(MS[1 - y], WO[1 - y])
    gate = jax.nn.sigmoid(jnp.sum(AA[...] * centroid, axis=1, keepdims=True))

    wait(*el)
    at_me, at_x, at_z, at_d = p.team_places()

    def rows_of(place):
        return pl.ds(pl.multiple_of(place * 160, 32), 160)

    def part(i, place=0):
        return pl.ds(pl.multiple_of(place * 160 + i * 32, 32), 32)

    def each(fn):
        def body(i, carry):
            fn(i)
            return carry

        lax.fori_loop(0, 5, body, 0)

    class Spread:
        def __init__(self, R):
            self.R = R
            self.zi, self.xi, self.fi = cp.block(5), cp.block(5), cp.block(5)

        def same(self, first, i, place, device):
            view = self.R.at[part(i, place), :]
            return cp.at(first + i, view, view, device)

        def z(self, i):
            return self.same(self.zi, i, at_me, p.dev_z(2))

        def x(self, i):
            return self.same(self.xi, i, at_me, p.dev_x)

        def forward(self, i):
            return self.same(self.fi, i, at_z, p.dev_x)

        def start_part(self, i):
            self.z(i).start()
            self.x(i).start()

        def relay_part(self, i):
            self.z(i).wait()
            self.forward(i).start()

    class Reduce:
        def __init__(self, staging, landing):
            self.put, self.got = PS.at[staging], RB.at[landing]
            self.xi, self.di, self.zi = cp.block(1), cp.block(5), cp.block(5)

        def x(self):
            return cp.at(self.xi, self.put.at[0], self.got.at[0], p.dev_x)

        def d(self, i):
            return cp.at(self.di + i, self.put.at[1, part(i), :], self.got.at[1, part(i), :], p.dev_x)

        def z(self, i):
            return cp.at(self.zi + i, self.put.at[2, part(i), :], self.got.at[2, part(i), :], p.dev_z(2))

        def start_x(self):
            each(lambda i: self.d(i).start())
            self.x().start()

        def relay_part(self, i, own_z):
            self.d(i).wait()
            self.put[2, part(i), :] = (own_z[part(i), :] + self.got[1, part(i), :].astype(F32)).astype(BF)
            self.z(i).start()

        def result_part(self, i, own):
            self.z(i).wait()
            return (
                own[part(i), :]
                + self.got[0, part(i), :].astype(F32)
                + self.got[2, part(i), :].astype(F32)
            )

    g1, g2, g3, g4 = Spread(R1), Spread(R2), Spread(R3), Spread(R4)
    r1, r2, r3, r4 = Reduce(0, 0), Reduce(1, 1), Reduce(0, 2), Reduce(0, 3)
    mine_r = rows_of(at_me)

    R1[mine_r, :] = AA[...].astype(BF)
    each(lambda i: g1.z(i).start())
    each(lambda i: g1.x(i).start())
    R3[mine_r, :] = (gate * GS[...].astype(F32)).astype(BF)
    each(lambda i: g3.z(i).start())

    wait(*ec0[0])
    wait(*ec[0])
    wait(*ez[0])
    ec1 = e_core(0, 1, g)
    wait(*er[0])
    ec2 = e_core(0, 1, p.gx)
    wait(*ec1)
    wait(*ec2)

    def cols_of(q):
        return slice(q * 512, (q + 1) * 512)

    def first_forward(place):
        at = rows_of(place)
        total = None
        for q in (0, 1):
            active, slope = gelu_both(dot(R1[at, :], UP[0, q]))
            GP1[at, cols_of(q)] = slope
            A1[at, cols_of(q)] = active.astype(BF)
            term = dot(active.astype(BF), DN[0, q])
            total = term if total is None else total + term
        return total

    OWN[0] = first_forward(at_me)
    each(g1.relay_part)
    each(lambda i: g1.x(i).wait())
    PS[0, 0] = first_forward(at_x).astype(BF)
    OWN[3] = first_forward(at_z)
    each(lambda i: g1.forward(i).wait())
    PS[0, 1] = first_forward(at_d).astype(BF)
    r1.start_x()
    wait(*e1[1])
    er.append(e_relay(1))
    ec.append(e_core(1, 0, p.gx))
    each(lambda i: r1.relay_part(i, OWN.at[3]))
    each(lambda i: g3.x(i).start())
    r1.x().wait()

    def middle_part(i):
        branch = r1.result_part(i, OWN.at[0])
        SUMS[0, part(i), :] = branch
        R2[part(i, at_me), :] = (AA[part(i), :].astype(BF).astype(F32) + branch).astype(BF)
        g2.start_part(i)

    each(middle_part)
    each(g3.relay_part)

    wait(*ec0[1])
    wait(*ec[1])
    wait(*ez[1])
    ec1 = e_core(1, 1, g)
    wait(*er[1])
    ec2 = e_core(1, 1, p.gx)
    wait(*ec1)
    wait(*ec2)

    def second_grad(place):
        at = rows_of(place)
        total_grad = None
        for q in (0, 1):
            active, slope = gelu_both(dot(R2[at, :], UP[1, q]))
            A2[at, cols_of(q)] = active.astype(BF)
            grad = (slope * dot(R3[at, :], DN[1, q], NT)).astype(BF)
            DH[at, cols_of(q)] = grad
            term = dot(grad, UP[1, q], NT)
            total_grad = term if total_grad is None else total_grad + term
        return total_grad

    def second_forward(place):
        at = rows_of(place)
        return dot(A2[at, :512], DN[1, 0]) + dot(A2[at, 512:], DN[1, 1])

    OWN[2] = second_grad(at_me)
    OWN[1] = second_forward(at_me)
    each(g2.relay_part)
    each(lambda i: g2.x(i).wait())
    each(lambda i: g3.x(i).wait())
    PS[0, 0] = second_grad(at_x).astype(BF)
    OWN[3] = second_grad(at_z)
    each(lambda i: g2.forward(i).wait())
    each(lambda i: g3.forward(i).wait())
    PS[0, 1] = second_grad(at_d).astype(BF)
    r3.start_x()
    PS[1, 1] = second_forward(at_d).astype(BF)
    PS[1, 0] = second_forward(at_x).astype(BF)
    OWN[4] = second_forward(at_z)
    each(lambda i: r3.relay_part(i, OWN.at[3]))
    r2.start_x()

    def weight_grads(A, R, RG, GU, GD):
        def one(q, d):
            qcols = pl.ds(pl.multiple_of(q * 512, 512), 512)
            GU[q, d] = dot(R[:, dq(d)], DH[:, qcols], TN).astype(BF)
            GD[q, d] = dot(A[:, qcols], RG[:, dq(d)], TN).astype(BF)

        def body(t, carry):
            q, k = lax.rem(t, 2), lax.div(t, 2)
            d = lax.rem(k, 2)
            mine_c = lax.div(k, 2)
            cc = p.c * mine_c + (1 - p.c) * (1 - mine_c)
            one(q, 2 * d + cc)
            return carry

        return body

    def to_core(n):
        out = ()
        for k, theirs in enumerate((p.gc, p.gd)):
            out += go(
                cp.new(GU.at[:, theirs], CRU.at[n, :, k], p.dev_c),
                cp.new(GD.at[:, theirs], CRD.at[n, :, k], p.dev_c),
            )
        return out

    def add_core(n, own_u, own_d, far_u, far_d):
        for k, d in enumerate((g, p.gx)):
            far_u[k] = (GU[1, d].astype(F32) + CRU[n, 1, k].astype(F32)).astype(BF)
            far_d[k] = (GD[1, d].astype(F32) + CRD[n, 1, k].astype(F32)).astype(BF)
            own_u[k] = (GU[0, d].astype(F32) + CRU[n, 0, k].astype(F32)).astype(BF)
            own_d[k] = (GD[0, d].astype(F32) + CRD[n, 0, k].astype(F32)).astype(BF)

    body2 = weight_grads(A2, R2, R3, GU, GD)
    lax.fori_loop(0, 4, body2, 0)
    f0 = to_core(0)
    lax.fori_loop(4, 8, body2, 0)

    r3.x().wait()

    def middle_grad_part(i):
        total = r3.result_part(i, OWN.at[2])
        SUMS[1, part(i), :] = total
        R4[part(i, at_me), :] = (R3[part(i, at_me), :].astype(F32) + total).astype(BF)
        g4.start_part(i)

    each(middle_grad_part)
    wait(*f0)
    add_core(0, P2U, P2D, ZSU, ZSD)
    f1 = []
    for k in (0, 1):
        f1 += go(
            cp.new(ZSU.at[k], ZRU.at[k], p.dev_pair),
            cp.new(ZSD.at[k], ZRD.at[k], p.dev_pair),
        )

    each(lambda i: r2.relay_part(i, OWN.at[4]))
    r2.x().wait()

    def first_backward(place):
        at = rows_of(place)
        total = None
        for q in (0, 1):
            grad = (GP1[at, cols_of(q)] * dot(R4[at, :], DN[0, q], NT)).astype(BF)
            DH[at, cols_of(q)] = grad
            term = dot(grad, UP[0, q], NT)
            total = term if total is None else total + term
        return total

    OWN[0] = first_backward(at_me)
    each(g4.relay_part)
    each(lambda i: g4.x(i).wait())
    PS[0, 0] = first_backward(at_x).astype(BF)
    OWN[3] = first_backward(at_z)
    each(lambda i: g4.forward(i).wait())
    PS[0, 1] = first_backward(at_d).astype(BF)
    r4.start_x()

    def output_part(i):
        branch_two = r2.result_part(i, OWN.at[1])
        returned = (SUMS[0, part(i), :] + branch_two).astype(BF).astype(F32)
        upstream = GS[part(i), :].astype(F32)
        after = AA[part(i), :]
        gate_part = jax.nn.sigmoid(jnp.sum(after * centroid, axis=1, keepdims=True))
        OUTS[part(i), :] = (after + gate_part * returned).astype(BF)
        score_grad = jnp.sum(upstream * returned, axis=1, keepdims=True) * gate_part * (1.0 - gate_part)
        RES[part(i), :] = upstream + score_grad * centroid
        CGR[...] += jnp.broadcast_to(jnp.sum(score_grad * after, axis=0, keepdims=True), CGR.shape)

    CGR[...] = jnp.zeros_like(CGR)

    each(lambda i: r4.relay_part(i, OWN.at[3]))
    each(output_part)
    body1 = weight_grads(A1, R1, R4, GU, GD)
    lax.fori_loop(0, 4, body1, 0)
    f0 = to_core(1)
    lax.fori_loop(4, 8, body1, 0)
    r4.x().wait()

    def residual_part(i):
        arrived = (r4.result_part(i, OWN.at[0]) + SUMS[1, part(i), :]).astype(BF)
        RESS[part(i), :] = (RES[part(i), :] + arrived.astype(F32)).astype(BF)

    each(residual_part)
    wait(*f0)
    add_core(1, P1U, P1D, Z1U, Z1D)
    wait(*f1)
    for k in (0, 1):
        S2U[k] = P2U[k].astype(F32) + ZRU[k].astype(F32)
        S2D[k] = P2D[k].astype(F32) + ZRD[k].astype(F32)


def backward_kernel(
    XG, QKV, PR, MXH, W0, W1, W2, WO, RT, OUTS, RESS, CGR, P1U, P1D, Z1U, Z1D, S2U, S2D,
    out, tgrad, pgrad, ograd, egrad, ugrad, dgrad,
    RP, OP, RL, XH, NRM, MG, DQ, NG, NGS, NGR,
    ZRU, ZRD, XSU, XSD, XRU, XRD,
    PW, PC, PXS, PXR, PYS, PYR, PK, PZR,
    OW, OC, OXS, OXR, OK, OZR, TE,
    send, recv,
):
    p = Place()
    g, y, w, x = p.g, p.y, p.w, p.x
    cp = Copies(send, recv)
    W = (W0, W1, W2)
    all_in = greet([p.dev_x, p.dev_c, p.dev_y, p.dev_z(1), p.dev_z(2), p.dev_z(3)])
    XSU[1] = S2U[1].astype(BF)
    XSD[1] = S2D[1].astype(BF)
    all_in()

    def go(*items):
        for item in items:
            item.start()
        return items

    def wait(*items):
        for item in items:
            item.wait()

    own_slots = pl.ds(pl.multiple_of(y * CAP, 16), CAP)
    peer_slots = pl.ds(pl.multiple_of((1 - y) * CAP, 16), CAP)
    ry = go(cp.new(RESS, RP, p.dev_y))
    oy = go(cp.new(OUTS.at[peer_slots, :], OP, p.dev_y))

    f1 = []
    for k in (1, 0):
        f1 += go(
            cp.new(Z1U.at[k], ZRU.at[k], p.dev_pair),
            cp.new(Z1D.at[k], ZRD.at[k], p.dev_pair),
        )
    f2 = {1: go(cp.new(XSU.at[1], XRU.at[1], p.dev_x), cp.new(XSD.at[1], XRD.at[1], p.dev_x))}

    half = pl.ds(pl.multiple_of(x * 512, 512), 512)
    other = pl.ds(pl.multiple_of((1 - x) * 512, 512), 512)
    ugrad[1, :, half] = S2U[0]
    dgrad[1, half, :] = S2D[0]

    values = XG[...].astype(F32)
    centred = values - jnp.mean(values, axis=1, keepdims=True)
    inverse = lax.rsqrt(jnp.mean(centred * centred, axis=1, keepdims=True) + 1e-05)
    XH[...] = centred * inverse
    pick = one_hot(8, EXTRA)
    gain = dot(pick, W0[:, 512:], NT)[0:1, :]
    NRM[...] = (XH[...] * gain).astype(BF)

    wait(*ry)
    for b in (0, 1):
        slots = slice(b * CAP, (b + 1) * CAP)
        RL[b * 128 : (b + 1) * 128, :] = (
            dot(dispatch_block(RT[b], y), RESS[slots, :], TN)
            + dot(dispatch_block(RT[b], 1 - y), RP[slots, :], TN)
        ).astype(BF)
    MG[...] = dot(RL[...], WO[y], NT).astype(BF)

    def rows4(d):
        return pl.ds(pl.multiple_of(d * 128, 128), 128)

    def out_rows(d):
        OW[rows4(d), :] = dot(MXH[y, :, rows4(d)], RL[...], TN).astype(BF)

    for d in (p.gc, p.gd, g, p.gx):
        out_rows(d)
    oc = []
    for k, theirs in enumerate((p.gc, p.gd)):
        oc += go(cp.new(OW.at[rows4(theirs), :], OC.at[k], p.dev_c))

    low_half = lax.broadcasted_iota(jnp.int32, (256, 128), 1) < 64

    def heads(t, carry):
        c0 = pl.ds(pl.multiple_of(t * 128, 128), 128)
        c1 = pl.ds(pl.multiple_of(512 + t * 128, 128), 128)
        c2 = pl.ds(pl.multiple_of(1024 + t * 128, 128), 128)
        q2, k2, v2, m2 = QKV[:, c0], QKV[:, c1], QKV[:, c2], MG[:, c0]
        parts = []
        for i in (0, 1):
            keep = low_half if i == 0 else ~low_half
            probs = PR[2 * t + i]
            probs_grad = dot(jnp.where(keep, m2, jnp.zeros_like(m2)), v2, NT)
            delta = jnp.sum(probs_grad * probs, axis=1, keepdims=True)
            scores_grad = (probs * (probs_grad - delta)).astype(BF)
            parts.append(
                (
                    dot(scores_grad, k2) * 0.125,
                    dot(scores_grad, q2, TN) * 0.125,
                    dot(probs.astype(BF), m2, TN),
                )
            )
        DQ[:, c0] = jnp.where(low_half, parts[0][0], parts[1][0]).astype(BF)
        DQ[:, c1] = jnp.where(low_half, parts[0][1], parts[1][1]).astype(BF)
        DQ[:, c2] = jnp.where(low_half, parts[0][2], parts[1][2]).astype(BF)
        return carry

    lax.fori_loop(0, 4, heads, 0)

    NG[...] = (
        dot(DQ[:, :512], W0[:, :512], NT) + dot(DQ[:, 512:1024], W1[...], NT) + dot(DQ[:, 1024:], W2[...], NT)
    )
    NGS[...] = NG[pl.ds(pl.multiple_of((1 - y) * 128, 128), 128), :].astype(BF)
    ny = go(cp.new(NGS, NGR, p.dev_y))
    gain_row = jnp.sum(NG[...] * XH[...], axis=0, keepdims=True)

    line = lax.broadcasted_iota(jnp.int32, (8, 1024), 0)
    stack = jnp.where(line == 0, gain_row, jnp.where(line == 1 + y, CGR[0:1, :], 0.0)).astype(BF)

    def dq(d):
        return pl.ds(pl.multiple_of(d * 256, 256), 256)

    def weight_rows(d):
        PW[dq(d), :1536] = dot(NRM[:, dq(d)], DQ[...], TN).astype(BF)

    def weight_loop(t, carry):
        d, cc = lax.rem(t, 2), lax.div(t, 2)
        weight_rows(2 * d + (p.c * cc + (1 - p.c) * (1 - cc)))
        return carry

    PW[:, 1536:] = dot(stack, pick, TN).astype(BF)
    lax.fori_loop(0, 2, weight_loop, 0)
    pc = []
    for k, theirs in enumerate((p.gc, p.gd)):
        pc += go(cp.new(PW.at[dq(theirs), :], PC.at[k], p.dev_c))
    lax.fori_loop(2, 4, weight_loop, 0)

    wait(*oc)
    OXS[...] = (OW[rows4(p.gx), :].astype(F32) + OC[1].astype(F32)).astype(BF)
    ox = go(cp.new(OXS, OXR, p.dev_x))
    wait(*pc)
    PXS[...] = (PW[dq(p.gx), :].astype(F32) + PC[1].astype(F32)).astype(BF)
    px = go(cp.new(PXS, PXR, p.dev_x))

    wait(*ny)
    own_rows = pl.ds(pl.multiple_of(y * 128, 128), 128)
    normed = XH[own_rows, :]
    mine = XG[own_rows, :].astype(F32)
    mine = mine - jnp.mean(mine, axis=1, keepdims=True)
    inverse = lax.rsqrt(jnp.mean(mine * mine, axis=1, keepdims=True) + 1e-05)
    scaled = (NG[own_rows, :] + NGR[...].astype(F32)) * gain
    tgrad[...] = RL[own_rows, :].astype(F32) + inverse * (
        scaled
        - jnp.mean(scaled, axis=1, keepdims=True)
        - normed * jnp.mean(scaled * normed, axis=1, keepdims=True)
    )
    wait(*oy)
    route_own = RT[y]
    out[...] = (
        dot(dispatch_block(route_own, y), OUTS[own_slots, :], TN)
        + dot(dispatch_block(route_own, 1 - y), OP[...], TN)
    ).astype(BF)

    wait(*ox)
    OK[...] = (OW[rows4(g), :].astype(F32) + OC[0].astype(F32) + OXR[...].astype(F32)).astype(BF)

    def row32(v):
        return pl.ds(pl.multiple_of(v * 32, 32), 32)

    oz = []
    for k in (1, 3, 2):
        oz += go(cp.new(OK.at[row32(lax.rem(w + k, 4)), :], OZR.at[k - 1], p.dev_z(k)))
    wait(*px)

    def summed(part):
        rows = pl.ds(pl.multiple_of(part * 128, 128), 128)
        full = pl.ds(pl.multiple_of(g * 256 + part * 128, 128), 128)
        total = PW[full, :].astype(F32) + PC[0, rows, :].astype(F32) + PXR[rows, :].astype(F32)
        return total.astype(BF)

    PYS[...] = summed(1 - y)
    py = go(cp.new(PYS, PYR, p.dev_y))
    PK[...] = summed(y)
    pz = []
    for k in (1, 3, 2):
        pz += go(cp.new(PK.at[row32(lax.rem(w + k, 4)), :], PZR.at[k - 1, 0], p.dev_z(k)))
    wait(*py)
    for k in (1, 3, 2):
        pz += go(cp.new(PYR.at[row32(lax.rem(w + k, 4)), :], PZR.at[k - 1, 1], p.dev_z(k)))

    wait(*f1)
    ugrad[0, :, half] = P1U[0].astype(F32) + ZRU[0].astype(F32)
    dgrad[0, half, :] = P1D[0].astype(F32) + ZRD[0].astype(F32)
    XSU[0] = (P1U[1].astype(F32) + ZRU[1].astype(F32)).astype(BF)
    XSD[0] = (P1D[1].astype(F32) + ZRD[1].astype(F32)).astype(BF)
    f2[0] = go(cp.new(XSU.at[0], XRU.at[0], p.dev_x), cp.new(XSD.at[0], XRD.at[0], p.dev_x))
    for s in (1, 0):
        wait(*f2[s])
        ugrad[s, :, other] = XRU[s].astype(F32)
        dgrad[s, other, :] = XRD[s].astype(F32)

    wait(*oz)
    own32 = row32(w)
    ograd[...] = (
        OK[own32, :].astype(F32) + OZR[0].astype(F32) + OZR[1].astype(F32) + OZR[2].astype(F32)
    )
    wait(*pz)
    sums = []
    for i, kept in enumerate((PK, PYR)):
        sums.append(
            kept[own32, :].astype(F32)
            + PZR[0, i].astype(F32)
            + PZR[1, i].astype(F32)
            + PZR[2, i].astype(F32)
        )
    for plane in (0, 1):
        kept = jnp.where(y == plane, sums[0], sums[1])
        for ch in range(3):
            for t in range(4):
                first = ch * 1024 + t * 256 + plane * 128
                pgrad[:, first : first + 128] = kept[:, ch * 512 + t * 128 : ch * 512 + (t + 1) * 128]
    TE[0:32, :] = sums[0][:, 1536:] + sums[1][:, 1536:]
    egrad[...] = TE[...].T[0:8, :]


def vmem(shape, dtype=BF):
    return pltpu.VMEM(shape, dtype)


def fast_shards(
    tokens, cotangent, norm_gain, project_weight, output_weight, centroids,
    expert_up, expert_down, sequence_lengths, block_order, routes,
):
    in_vmem = pl.BlockSpec(memory_space=pltpu.VMEM)
    in_any = pl.BlockSpec(memory_space=pl.ANY)
    in_smem = pl.BlockSpec(memory_space=pltpu.SMEM)
    shape = jax.ShapeDtypeStruct
    ext = jnp.pad(
        jnp.concatenate([norm_gain[None], centroids], axis=0).astype(F32), ((0, 5), (0, EXTRA - 32))
    )
    mid_shapes = [
        ((256, 1024), BF),
        ((256, 1536), BF),
        ((8, 256, 256), F32),
        ((2, 256, 512), BF),
        ((1024, 512 + EXTRA), BF),
        ((1024, 512), BF),
        ((1024, 512), BF),
        ((2, 512, 1024), BF),
        ((2, 8, 128), F32),
        ((160, 1024), BF),
        ((160, 1024), BF),
        ((8, 1024), F32),
        ((2, 256, 512), BF),
        ((2, 512, 256), BF),
        ((2, 256, 512), BF),
        ((2, 512, 256), BF),
        ((2, 256, 512), F32),
        ((2, 512, 256), F32),
    ]
    mid = pl.pallas_call(
        forward_kernel,
        name="forward",
        out_shape=[shape(*s) for s in mid_shapes],
        in_specs=[in_smem] * 2 + [in_vmem] * 6 + [in_any] * 2,
        out_specs=[in_vmem] * len(mid_shapes),
        scratch_shapes=[
            vmem((2, 32, 512 + EXTRA)),
            vmem((2, 32, 512)),
            vmem((2, 32, 512)),
            vmem((256, 1024)),
            vmem((256, 1024), F32),
            vmem((256, 1024)),
            vmem((2, 2, 1024, 512)),
            vmem((2, 2, 512, 1024)),
            vmem((2, CAP, 128)),
            vmem((160, 1024), F32),
            vmem((160, 1024)),
            vmem((2, 160, 512)),
            vmem((160, 1024), F32),
        ]
        + [vmem((640, 1024))] * 4
        + [
            vmem((4, 3, 160, 1024)),
            vmem((2, 3, 160, 1024)),
            vmem((5, 160, 1024), F32),
            vmem((160, 1024), F32),
            vmem((640, 1024), F32),
            vmem((640, 1024)),
            vmem((640, 1024)),
            vmem((640, 1024)),
            vmem((2, 160, 1024), F32),
            vmem((2, 4, 256, 512)),
            vmem((2, 4, 512, 256)),
            vmem((2, 2, 2, 256, 512)),
            vmem((2, 2, 2, 512, 256)),
            vmem((2, 256, 512)),
            vmem((2, 512, 256)),
            vmem((2, 256, 512)),
            vmem((2, 512, 256)),
            vmem((2, 256, 512)),
            vmem((2, 512, 256)),
            pltpu.SemaphoreType.DMA((208,)),
            pltpu.SemaphoreType.DMA((208,)),
            pltpu.SemaphoreType.DMA((12,)),
        ],
        compiler_params=pltpu.CompilerParams(
            collective_id=0, has_side_effects=True, vmem_limit_bytes=VMEM_LIMIT
        ),
    )(
        sequence_lengths[0], block_order[0], tokens[0], cotangent[0], routes.reshape(1, 128),
        project_weight, output_weight, ext, expert_up[0], expert_down[0],
    )
    out_shapes = [
        ((128, 1024), BF),
        ((128, 1024), F32),
        ((32, 3072), F32),
        ((32, 1024), F32),
        ((8, EXTRA), F32),
        ((2, 256, 1024), F32),
        ((2, 1024, 256), F32),
    ]
    out, tgrad, pgrad, ograd, egrad, ugrad, dgrad = pl.pallas_call(
        backward_kernel,
        name="backward",
        out_shape=[shape(*s) for s in out_shapes],
        in_specs=[in_vmem] * len(mid_shapes),
        out_specs=[in_vmem] * len(out_shapes),
        scratch_shapes=[
            vmem((160, 1024)),
            vmem((CAP, 1024)),
            vmem((256, 1024)),
            vmem((256, 1024), F32),
            vmem((256, 1024)),
            vmem((256, 512)),
            vmem((256, 1536)),
            vmem((256, 1024), F32),
            vmem((128, 1024)),
            vmem((128, 1024)),
            vmem((2, 256, 512)),
            vmem((2, 512, 256)),
            vmem((2, 256, 512)),
            vmem((2, 512, 256)),
            vmem((2, 256, 512)),
            vmem((2, 512, 256)),
            vmem((1024, 1536 + EXTRA)),
            vmem((2, 256, 1536 + EXTRA)),
            vmem((256, 1536 + EXTRA)),
            vmem((256, 1536 + EXTRA)),
            vmem((128, 1536 + EXTRA)),
            vmem((128, 1536 + EXTRA)),
            vmem((128, 1536 + EXTRA)),
            vmem((3, 2, 32, 1536 + EXTRA)),
            vmem((512, 1024)),
            vmem((2, 128, 1024)),
            vmem((128, 1024)),
            vmem((128, 1024)),
            vmem((128, 1024)),
            vmem((3, 32, 1024)),
            vmem((EXTRA, EXTRA), F32),
            pltpu.SemaphoreType.DMA((48,)),
            pltpu.SemaphoreType.DMA((48,)),
        ],
        compiler_params=pltpu.CompilerParams(
            collective_id=1, has_side_effects=True, vmem_limit_bytes=VMEM_LIMIT
        ),
    )(*mid)
    return (
        out[None],
        tgrad[None],
        egrad[0, :32],
        pgrad,
        ograd,
        egrad[1:3, :32],
        ugrad[None],
        dgrad[None],
    )


def solution(mesh):
    sizes = dict(mesh.shape)
    fast = sizes == {"grp": 4, "ctx": 2, "wsh": 4}
    return jax.shard_map(
        fast_shards if fast else shards,
        mesh=mesh,
        in_specs=IN_SPECS,
        out_specs=OUT_SPECS,
        check_vma=False,
    )
```

```python
import math

import jax
import jax.numpy as jnp
from jax import lax
from jax.experimental import pallas as pl
from jax.experimental.pallas import tpu as pltpu
from jax.sharding import PartitionSpec as P

HEADS = 16
HDIM = 64
BLK = 128


precise = lax.Precision.HIGHEST


def place_rows(order_row, lengths_row, total_rows):
    row_index = jnp.arange(total_rows, dtype=jnp.int32)
    picked = (row_index // BLK)[:, None] == jnp.arange(order_row.shape[0], dtype=jnp.int32)[None, :]
    blocks = jnp.sum(jnp.where(picked, order_row[None, :], 0), axis=1)
    token_place = blocks * BLK + row_index % BLK
    bounds = jnp.cumsum(lengths_row)
    sequence = jnp.sum((token_place[:, None] >= bounds[None, :]).astype(jnp.int32), axis=1)
    return (token_place, sequence)


def normalize(values):
    average = jnp.mean(values, axis=-1, keepdims=True)
    centred = values - average
    inverse = lax.rsqrt(jnp.mean(centred * centred, axis=-1, keepdims=True) + 1e-05)
    return (centred * inverse, inverse)


def head_slice(matrix, section, offset, heads_per):
    width_part = heads_per * HDIM
    first_col = offset + section * width_part
    return matrix[:, first_col : first_col + width_part].reshape(matrix.shape[0], heads_per, HDIM)


def spread_rows(local_rows):
    return lax.all_gather(local_rows, "wsh", axis=0, tiled=True)


def collect_rows(partial_term):
    return lax.psum_scatter(
        partial_term.astype(jnp.bfloat16), "wsh", scatter_dimension=0, tiled=True
    ).astype(jnp.float32)


def trade_rows(slots_rows, peer_count, capacity):
    shaped = slots_rows.reshape(peer_count, capacity, slots_rows.shape[-1])
    moved = lax.all_to_all(shaped, "ctx", split_axis=0, concat_axis=0, tiled=True)
    return moved.reshape(peer_count * capacity, slots_rows.shape[-1])


def gelu_pullback(hidden, incoming):
    value_out, pullback = jax.vjp(jax.nn.gelu, hidden)
    return pullback(incoming)[0]


def shards(
    tokens,
    cotangent,
    norm_gain,
    project_weight,
    output_weight,
    centroids,
    expert_up,
    expert_down,
    sequence_lengths,
    block_order,
    routes,
):
    local_rows = tokens.shape[1]
    model_width = tokens.shape[2]
    peer_count = lax.axis_size("ctx")
    position = lax.axis_index("ctx")
    total_rows = local_rows * peer_count
    capacity = max(2, (5 * local_rows + 4 * peer_count - 1) // (4 * peer_count))
    slot_count = peer_count * capacity
    score_scale = 1.0 / math.sqrt(HDIM)
    heads_per = 4
    sections = HEADS // heads_per
    inputs_f = tokens[0].astype(jnp.float32)
    upstream = cotangent[0].astype(jnp.float32)
    project_full, output_full, gain_full, centroid_full = (
        lax.all_gather(project_weight, ("grp", "ctx", "wsh"), axis=0, tiled=True),
        lax.all_gather(output_weight, ("grp", "ctx", "wsh"), axis=0, tiled=True),
        lax.all_gather(norm_gain, ("grp", "ctx", "wsh"), axis=0, tiled=True),
        lax.all_gather(centroids, ("grp", "ctx", "wsh"), axis=1, tiled=True),
    )
    up_full, down_full = (
        lax.all_gather(expert_up, "grp", axis=2, tiled=True),
        lax.all_gather(expert_down, "grp", axis=3, tiled=True),
    )
    place_all, sequence_all = place_rows(block_order[0], sequence_lengths[0], total_rows)
    place_own = lax.dynamic_slice_in_dim(place_all, position * local_rows, local_rows)
    sequence_own = lax.dynamic_slice_in_dim(sequence_all, position * local_rows, local_rows)
    allowed = (sequence_own[:, None] == sequence_all[None, :]) & (
        place_all[None, :] <= place_own[:, None]
    )
    normed, inverse = normalize(inputs_f)
    gain_values = gain_full.astype(jnp.float32)
    normed_low = (normed * gain_values).astype(jnp.bfloat16)
    projected = jnp.dot(normed_low, project_full, preferred_element_type=jnp.float32)
    queries = projected[:, :model_width].astype(jnp.bfloat16)
    keyvalue = projected[:, model_width:].astype(jnp.bfloat16)
    keyvalue_all = lax.all_gather(keyvalue, "ctx", axis=0, tiled=True)
    mixed_parts = []
    logsum_parts = []
    for section in range(sections):
        head_query = head_slice(queries, section, 0, heads_per)
        head_key = head_slice(keyvalue_all, section, 0, heads_per)
        head_value = head_slice(keyvalue_all, section, model_width, heads_per)
        scores = (
            jnp.einsum("tgd,sgd->gts", head_query, head_key, preferred_element_type=jnp.float32)
            * score_scale
        )
        scores = jnp.where(allowed[None], scores, -1000000000.0)
        largest = jnp.max(scores, axis=-1, keepdims=True)
        exponent = jnp.exp(scores - largest)
        totals = jnp.sum(exponent, axis=-1, keepdims=True)
        weights = (exponent / totals).astype(jnp.bfloat16)
        mixed_part = jnp.einsum(
            "gts,sgd->tgd", weights, head_value, preferred_element_type=jnp.float32
        )
        mixed_parts.append(mixed_part.reshape(local_rows, heads_per * HDIM))
        logsum_parts.append((largest + jnp.log(totals))[:, :, 0])
    mixed_all = jnp.concatenate(mixed_parts, axis=1).astype(jnp.bfloat16)
    logsum = jnp.concatenate(logsum_parts, axis=0)
    after_attention = inputs_f + jnp.dot(mixed_all, output_full, preferred_element_type=jnp.float32)
    route_ids = routes[0, :, 0]
    member = route_ids[:, None] == jnp.arange(peer_count, dtype=jnp.int32)[None, :]
    member_f = member.astype(jnp.float32)
    picked_centroid = jnp.dot(member_f, centroid_full.astype(jnp.float32), precision=precise)
    gate_value = jax.nn.sigmoid(jnp.sum(after_attention * picked_centroid, axis=-1))
    member_int = member.astype(jnp.int32)
    ranking = jnp.sum((jnp.cumsum(member_int, axis=0) - 1) * member_int, axis=1)
    slot_index = route_ids * capacity + ranking
    dispatch = (slot_index[None, :] == jnp.arange(slot_count, dtype=jnp.int32)[:, None]).astype(
        jnp.bfloat16
    )
    sent_rows = jnp.dot(
        dispatch, after_attention.astype(jnp.bfloat16), preferred_element_type=jnp.float32
    ).astype(jnp.bfloat16)
    arrived = trade_rows(sent_rows, peer_count, capacity)
    up_first = up_full[0, 0]
    up_second = up_full[0, 1]
    down_first = down_full[0, 0]
    down_second = down_full[0, 1]
    gathered_one = spread_rows(arrived)
    hidden_one = jnp.dot(gathered_one, up_first, preferred_element_type=jnp.float32)
    active_one = jax.nn.gelu(hidden_one).astype(jnp.bfloat16)
    branch_one = collect_rows(jnp.dot(active_one, down_first, preferred_element_type=jnp.float32))
    middle = (arrived.astype(jnp.float32) + branch_one).astype(jnp.bfloat16)
    gathered_two = spread_rows(middle)
    hidden_two = jnp.dot(gathered_two, up_second, preferred_element_type=jnp.float32)
    active_two = jax.nn.gelu(hidden_two).astype(jnp.bfloat16)
    branch_two = collect_rows(jnp.dot(active_two, down_second, preferred_element_type=jnp.float32))
    expert_out = (branch_one + branch_two).astype(jnp.bfloat16)
    returned = trade_rows(expert_out, peer_count, capacity)
    returned_tok = jnp.einsum("st,sd->td", dispatch, returned, preferred_element_type=jnp.float32)
    output = after_attention + gate_value[:, None] * returned_tok
    gate_grad = jnp.sum(upstream * returned_tok, axis=-1)
    score_grad = gate_grad * gate_value * (1.0 - gate_value)
    centroid_term = jnp.dot(member_f.T, score_grad[:, None] * after_attention, precision=precise)
    branch_grad = (gate_value[:, None] * upstream).astype(jnp.bfloat16)
    branch_sent = jnp.dot(dispatch, branch_grad, preferred_element_type=jnp.float32).astype(
        jnp.bfloat16
    )
    branch_arrived = trade_rows(branch_sent, peer_count, capacity)
    grad_two = spread_rows(branch_arrived)
    hidden_two_grad = gelu_pullback(
        hidden_two, jnp.dot(grad_two, down_second.T, preferred_element_type=jnp.float32)
    ).astype(jnp.bfloat16)
    down_second_grad = jnp.dot(active_two.T, grad_two, preferred_element_type=jnp.float32)
    up_second_grad = jnp.dot(gathered_two.T, hidden_two_grad, preferred_element_type=jnp.float32)
    middle_grad = collect_rows(
        jnp.dot(hidden_two_grad, up_second.T, preferred_element_type=jnp.float32)
    )
    first_branch_grad = (branch_arrived.astype(jnp.float32) + middle_grad).astype(jnp.bfloat16)
    grad_one = spread_rows(first_branch_grad)
    hidden_one_grad = gelu_pullback(
        hidden_one, jnp.dot(grad_one, down_first.T, preferred_element_type=jnp.float32)
    ).astype(jnp.bfloat16)
    down_first_grad = jnp.dot(active_one.T, grad_one, preferred_element_type=jnp.float32)
    up_first_grad = jnp.dot(gathered_one.T, hidden_one_grad, preferred_element_type=jnp.float32)
    arrived_grad = (
        collect_rows(jnp.dot(hidden_one_grad, up_first.T, preferred_element_type=jnp.float32))
        + middle_grad
    ).astype(jnp.bfloat16)
    home_grad = trade_rows(arrived_grad, peer_count, capacity)
    home_grad_tok = jnp.einsum("st,sd->td", dispatch, home_grad, preferred_element_type=jnp.float32)
    up_terms = jnp.stack([up_first_grad, up_second_grad])[None]
    down_terms = jnp.stack([down_first_grad, down_second_grad])[None]
    up_grad_out, down_grad_out = (
        lax.psum_scatter(
            up_terms.astype(jnp.bfloat16), "grp", scatter_dimension=2, tiled=True
        ).astype(jnp.float32),
        lax.psum_scatter(
            down_terms.astype(jnp.bfloat16), "grp", scatter_dimension=3, tiled=True
        ).astype(jnp.float32),
    )
    residual_grad = upstream + score_grad[:, None] * picked_centroid + home_grad_tok
    residual_low = residual_grad.astype(jnp.bfloat16)
    output_term = jnp.dot(mixed_all.T, residual_low, preferred_element_type=jnp.float32)
    mixed_grad = jnp.dot(residual_low, output_full.T, preferred_element_type=jnp.float32).astype(
        jnp.bfloat16
    )
    query_grads = []
    key_grads = []
    value_grads = []
    delta_parts = []
    for section in range(sections):
        head_query = head_slice(queries, section, 0, heads_per)
        head_key = head_slice(keyvalue_all, section, 0, heads_per)
        head_value = head_slice(keyvalue_all, section, model_width, heads_per)
        head_grad = head_slice(mixed_grad, section, 0, heads_per)
        scores = (
            jnp.einsum("tgd,sgd->gts", head_query, head_key, preferred_element_type=jnp.float32)
            * score_scale
        )
        scores = jnp.where(allowed[None], scores, -1000000000.0)
        probs = jnp.exp(
            scores - logsum[section * heads_per : (section + 1) * heads_per][:, :, None]
        )
        probs_grad = jnp.einsum(
            "tgd,sgd->gts", head_grad, head_value, preferred_element_type=jnp.float32
        )
        row_delta = jnp.sum(probs_grad * probs, axis=-1)
        scores_grad = (probs * (probs_grad - row_delta[:, :, None])).astype(jnp.bfloat16)
        query_part = (
            jnp.einsum("gts,sgd->tgd", scores_grad, head_key, preferred_element_type=jnp.float32)
            * score_scale
        )
        query_grads.append(query_part.reshape(local_rows, heads_per * HDIM))
        delta_parts.append(row_delta)
        key_part = (
            jnp.einsum("gts,tgd->sgd", scores_grad, head_query, preferred_element_type=jnp.float32)
            * score_scale
        )
        value_part = jnp.einsum(
            "gts,tgd->sgd",
            probs.astype(jnp.bfloat16),
            head_grad,
            preferred_element_type=jnp.float32,
        )
        key_grads.append(key_part.reshape(total_rows, heads_per * HDIM))
        value_grads.append(value_part.reshape(total_rows, heads_per * HDIM))
    query_grad = jnp.concatenate(query_grads, axis=1).astype(jnp.bfloat16)
    keyvalue_terms = jnp.concatenate(key_grads + value_grads, axis=1)
    keyvalue_grad = lax.psum_scatter(
        keyvalue_terms.astype(jnp.bfloat16), "ctx", scatter_dimension=0, tiled=True
    )
    projected_grad = jnp.concatenate([query_grad, keyvalue_grad], axis=1)
    project_term = jnp.dot(normed_low.T, projected_grad, preferred_element_type=jnp.float32)
    normed_grad = jnp.dot(projected_grad, project_full.T, preferred_element_type=jnp.float32)
    gain_term = jnp.sum(normed_grad * normed, axis=0)
    scaled_grad = normed_grad * gain_values
    input_grad = residual_grad + inverse * (
        scaled_grad
        - jnp.mean(scaled_grad, axis=-1, keepdims=True)
        - normed * jnp.mean(scaled_grad * normed, axis=-1, keepdims=True)
    )
    project_grad, output_grad, gain_grad, centroid_grad = (
        lax.psum_scatter(project_term, ("grp", "ctx", "wsh"), scatter_dimension=0, tiled=True),
        lax.psum_scatter(output_term, ("grp", "ctx", "wsh"), scatter_dimension=0, tiled=True),
        lax.psum_scatter(gain_term, ("grp", "ctx", "wsh"), scatter_dimension=0, tiled=True),
        lax.psum_scatter(centroid_term, ("grp", "ctx", "wsh"), scatter_dimension=1, tiled=True),
    )
    return (
        output.astype(jnp.bfloat16)[None],
        input_grad[None],
        gain_grad,
        project_grad,
        output_grad,
        centroid_grad,
        up_grad_out,
        down_grad_out,
    )


VMEM_LIMIT = 61 * 2**20
CHUNKS = (384, 384, 384, 512)

IN_SPECS = (
    P(("grp", "wsh"), "ctx", None),
    P(("grp", "wsh"), "ctx", None),
    P(("grp", "ctx", "wsh")),
    P(("grp", "ctx", "wsh"), None),
    P(("grp", "ctx", "wsh"), None),
    P(None, ("grp", "ctx", "wsh")),
    P("ctx", None, "grp", "wsh"),
    P("ctx", None, "wsh", "grp"),
    P(("grp", "wsh"), None),
    P(("grp", "wsh"), None),
    P(("grp", "wsh"), "ctx", None),
)
OUT_SPECS = (
    P(("grp", "wsh"), "ctx", None),
    P(("grp", "wsh"), "ctx", None),
    P(("grp", "ctx", "wsh")),
    P(("grp", "ctx", "wsh"), None),
    P(("grp", "ctx", "wsh"), None),
    P(None, ("grp", "ctx", "wsh")),
    P("ctx", None, "grp", "wsh"),
    P("ctx", None, "wsh", "grp"),
)

BF = jnp.bfloat16
F32 = jnp.float32
NN = ((1,), (0,))
NT = ((1,), (1,))
TN = ((0,), (0,))
MESH = pl.DeviceIdType.MESH
GELU_C = 0.7978845608028654
EXTRA = 128
CAP = 80


def dot(a, b, dims=NN):
    return lax.dot_general(a, b, (dims, ((), ())), preferred_element_type=F32)


def gelu_both(h):
    sq = h * h
    t = jnp.tanh(GELU_C * h * (1.0 + 0.044715 * sq))
    half = 0.5 * (1.0 + t)
    slope = half + 0.5 * h * (1.0 - t * t) * (GELU_C * (1.0 + 3.0 * 0.044715 * sq))
    return h * half, slope


def copy_in(src, dst, sem):
    return pltpu.make_async_copy(src, dst, sem)


class Copies:
    def __init__(self, send, recv):
        self.send, self.recv, self.used = send, recv, 0

    def block(self, count):
        first = self.used
        self.used += count
        return first

    def at(self, index, src, dst, device):
        return pltpu.make_async_remote_copy(
            src_ref=src,
            dst_ref=dst,
            send_sem=self.send.at[index],
            recv_sem=self.recv.at[index],
            device_id=device,
            device_id_type=MESH,
        )

    def new(self, src, dst, device):
        return self.at(self.block(1), src, dst, device)


class Place:
    def __init__(self):
        g, y, w = lax.axis_index("grp"), lax.axis_index("ctx"), lax.axis_index("wsh")
        self.g, self.y, self.w = g, y, w
        self.x = lax.div(g, 2)
        self.c = g - 2 * self.x
        self.gx = 2 * (1 - self.x) + self.c
        self.gc = 2 * self.x + 1 - self.c
        self.gd = 2 * (1 - self.x) + 1 - self.c
        self.wb = lax.rem(w, 2)
        self.w1 = w + 1 - 2 * self.wb
        self.w2 = lax.rem(w + 2, 4)
        self.dev_x = (self.gx, y, w)
        self.dev_c = (self.gc, y, w)
        self.dev_y = (g, 1 - y, w)
        self.dev_pair = (g, y, self.w1)
        self.dev_z = lambda k: (g, y, lax.rem(w + k, 4))

    def team_places(self):
        mine = 2 * self.x + lax.div(self.w, 2)
        x_side = 2 * (1 - self.x) + lax.div(self.w, 2)
        flip = 1 - 2 * lax.div(self.w, 2)
        return mine, x_side, mine + flip, x_side + flip


def greet(devices):
    barrier = pltpu.get_barrier_semaphore()
    for device in devices:
        pl.semaphore_signal(barrier, inc=1, device_id=device, device_id_type=MESH)
    return lambda: pl.semaphore_wait(barrier, len(devices))


def one_hot(rows, columns):
    same = lax.broadcasted_iota(jnp.int32, (rows, columns), 0) == lax.broadcasted_iota(
        jnp.int32, (rows, columns), 1
    )
    return same.astype(F32).astype(BF)


def dispatch_block(route_rows, expert):
    member = (route_rows == expert.astype(F32)).astype(F32)
    earlier = lax.broadcasted_iota(jnp.int32, (128, 128), 0) < lax.broadcasted_iota(jnp.int32, (128, 128), 1)
    rank = dot(member.astype(BF), earlier.astype(F32).astype(BF))
    slot = lax.broadcasted_iota(jnp.int32, (CAP, 128), 0).astype(F32)
    hit = (jnp.broadcast_to(rank[0:1, :], (CAP, 128)) == slot) & (
        jnp.broadcast_to(member[0:1, :], (CAP, 128)) > 0.5
    )
    return hit.astype(F32).astype(BF)


def place_of(lengths, order, index):
    place = jnp.where(index < 128, order[0], order[1]) * 128 + lax.rem(index, 128)
    bound = lengths[0]
    sequence = jnp.where(place >= bound, 1, 0)
    for part in (1, 2):
        bound = bound + lengths[part]
        sequence = sequence + jnp.where(place >= bound, 1, 0)
    return place, sequence


def forward_kernel(
    lengths, order, tok, cot, rts, pw, wo_in, ext, up_in, dn_in,
    xg_out, qkv_out, pr_out, mxh_out, w0_out, w1_out, w2_out, wo_out,
    RT, OUTS, RESS, CGR, P1U, P1D, Z1U, Z1D, S2U, S2D,
    XG, QKV, PR, MXH, W0, W1, W2, WO,
    WS0, WS1, WS2, CG, XH, NRM, UP, DN, DSP, XS, GS, MS, AA,
    R1, R2, R3, R4, RB, PS, OWN, RES, GP1, A1, A2, DH, SUMS,
    GU, GD, CRU, CRD, P2U, P2D, ZSU, ZSD, ZRU, ZRD,
    send, recv, local,
):
    p = Place()
    g, y, w, x = p.g, p.y, p.w, p.x
    cp = Copies(send, recv)
    all_in = greet([p.dev_x, p.dev_c, p.dev_y, p.dev_z(1), p.dev_z(2), p.dev_z(3)])
    nlocal = [0]

    def here(src, dst):
        nlocal[0] += 1
        return copy_in(src, dst, local.at[nlocal[0] - 1])

    def go(*items):
        for item in items:
            item.start()
        return items

    def wait(*items):
        for item in items:
            item.wait()

    W, WS = (W0, W1, W2), (WS0, WS1, WS2)
    for ch in range(3):
        for t in range(4):
            for plane in (0, 1):
                first = ch * 1024 + t * 256 + plane * 128
                WS[ch][plane, :, t * 128 : (t + 1) * 128] = pw[:, first : first + 128]
    extra_rows = jnp.concatenate([ext[...], jnp.zeros((EXTRA - 8, EXTRA), F32)], axis=0).astype(BF)
    extra_cols = dot(one_hot(32, EXTRA), extra_rows, NT).astype(BF)
    WS0[0, :, 512:] = extra_cols
    WS0[1, :, 512:] = extra_cols
    RT[y] = jnp.broadcast_to(rts[...].astype(F32), (8, 128))
    mine = pl.ds(pl.multiple_of(y * 128, 128), 128)
    XG[mine, :] = tok[...]
    CG[mine, :] = cot[...]

    def row(plane):
        return pl.ds(pl.multiple_of(g * 256 + plane * 128 + w * 32, 32), 32)

    for ch in range(3):
        W[ch][row(y), :] = WS[ch][y]
    row_o = pl.ds(pl.multiple_of(g * 128 + w * 32, 32), 32)
    WO[y, row_o, :] = wo_in[...]
    all_in()

    def z_rows(ch, plane):
        return sum(
            (go(cp.new(W[ch].at[row(plane), :], W[ch].at[row(plane), :], p.dev_z(k))) for k in (2, 1, 3)), ()
        )

    yw = [go(cp.new(WS[ch].at[1 - y], W[ch].at[row(y), :], p.dev_y)) for ch in range(3)]
    zw = [z_rows(0, y), (), ()]
    ty = go(cp.new(RT.at[y], RT.at[y], p.dev_y), cp.new(tok, XG.at[mine, :], p.dev_y))

    def dq(q):
        return pl.ds(pl.multiple_of(q * 256, 256), 256)

    half = pl.ds(pl.multiple_of(x * 512, 512), 512)
    other = pl.ds(pl.multiple_of((1 - x) * 512, 512), 512)

    def e_first(s):
        return (
            cp.new(up_in.at[s, :, other], UP.at[s, 0, dq(g), :], p.dev_x),
            cp.new(dn_in.at[s, other, :], DN.at[s, 0, :, dq(g)], p.dev_x),
        )

    def e_core0(s):
        return go(
            cp.new(up_in.at[s, :, half], UP.at[s, 0, dq(g), :], p.dev_c),
            cp.new(dn_in.at[s, half, :], DN.at[s, 0, :, dq(g)], p.dev_c),
        )

    def e_local(s):
        return go(
            here(up_in.at[s, :, half], UP.at[s, 0, dq(g), :]),
            here(dn_in.at[s, half, :], DN.at[s, 0, :, dq(g)]),
        )

    def e_z(s):
        return (
            cp.new(up_in.at[s, :, half], UP.at[s, 1, dq(g), :], p.dev_pair),
            cp.new(dn_in.at[s, half, :], DN.at[s, 1, :, dq(g)], p.dev_pair),
        )

    def e_relay(s):
        return go(
            cp.new(UP.at[s, 0, dq(p.gx), :], UP.at[s, 1, dq(p.gx), :], p.dev_pair),
            cp.new(DN.at[s, 0, :, dq(p.gx)], DN.at[s, 1, :, dq(p.gx)], p.dev_pair),
        )

    def e_core(s, q, which):
        return go(
            cp.new(UP.at[s, q, dq(which), :], UP.at[s, q, dq(which), :], p.dev_c),
            cp.new(DN.at[s, q, :, dq(which)], DN.at[s, q, :, dq(which)], p.dev_c),
        )

    e1 = [e_first(0), e_first(1)]
    go(*e1[0])
    wait(*yw[0])
    zw[0] += z_rows(0, 1 - y)
    for ch in (1, 2):
        wait(*yw[ch])
        zw[ch] = z_rows(ch, y) + z_rows(ch, 1 - y)
    zo = sum((go(cp.new(wo_in, WO.at[y, row_o, :], p.dev_z(k))) for k in (2, 1, 3)), ())
    el = e_local(0) + e_local(1)
    ec0 = [e_core0(0), e_core0(1)]

    wait(*ty)
    values = XG[...].astype(F32)
    centred = values - jnp.mean(values, axis=1, keepdims=True)
    inverse = lax.rsqrt(jnp.mean(centred * centred, axis=1, keepdims=True) + 1e-05)
    XH[...] = centred * inverse
    for b in (0, 1):
        DSP[b] = dispatch_block(RT[b], y)
        XS[b * CAP : (b + 1) * CAP, :] = dot(DSP[b], XG[b * 128 : (b + 1) * 128, :])

    def quarter(d):
        return pl.ds(pl.multiple_of(d * 128, 128), 128)

    def wo_copy(plane, d, device):
        return cp.new(WO.at[plane, quarter(d), :], WO.at[plane, quarter(d), :], device)

    def w_copy(ch, d, device):
        return cp.new(W[ch].at[dq(d), :], W[ch].at[dq(d), :], device)

    xw, fw = [None] * 3, [None] * 3
    for ch in range(3):
        wait(*zw[ch])
        xw[ch] = go(w_copy(ch, g, p.dev_x), w_copy(ch, g, p.dev_c))
    wait(*zo)
    yo = go(wo_copy(y, g, p.dev_y))
    ez = [go(*e_z(0)), e_z(1)]
    cy = go(cp.new(cot, CG.at[mine, :], p.dev_y))
    wait(*xw[0])
    fw[0] = go(w_copy(0, p.gx, p.dev_c))
    wait(*fw[0])
    extra = dot(one_hot(8, EXTRA), W0[:, 512:], NT)
    gain = extra[0:1, :]
    centroid = jnp.where(y == 0, extra[1:2, :], extra[2:3, :])
    NRM[...] = (XH[...] * gain).astype(BF)

    def project(ch):
        QKV[:, ch * 512 : (ch + 1) * 512] = dot(NRM[...], W[ch][:, :512]).astype(BF)

    project(0)
    wait(*xw[1])
    fw[1] = go(w_copy(1, p.gx, p.dev_c))
    wait(*fw[1])
    project(1)
    wait(*yo)
    xo = go(
        cp.new(WO.at[:, quarter(g), :], WO.at[:, quarter(g), :], p.dev_x),
        cp.new(WO.at[:, quarter(g), :], WO.at[:, quarter(g), :], p.dev_c),
    )
    go(*e1[1])
    wait(*e1[0])
    er = [e_relay(0)]
    ec = [e_core(0, 0, p.gx)]
    go(*ez[1])
    wait(*xw[2])
    fw[2] = go(w_copy(2, p.gx, p.dev_c))
    wait(*fw[2])
    project(2)

    place_q, seq_q = place_of(lengths, order, lax.broadcasted_iota(jnp.int32, (256, 256), 0))
    place_k, seq_k = place_of(lengths, order, lax.broadcasted_iota(jnp.int32, (256, 256), 1))
    allowed = (seq_q == seq_k) & (place_k <= place_q)
    low_half = lax.broadcasted_iota(jnp.int32, (256, 128), 1) < 64
    mixed_first = cp.block(4)

    def mixed_copy(t):
        cols = pl.ds(pl.multiple_of(t * 128, 128), 128)
        return cp.at(mixed_first + t, MXH.at[y, :, cols], MXH.at[y, :, cols], p.dev_y)

    def heads(t, carry):
        cols = pl.ds(pl.multiple_of(t * 128, 128), 128)
        q2 = QKV[:, cols]
        k2 = QKV[:, pl.ds(pl.multiple_of(512 + t * 128, 128), 128)]
        v2 = QKV[:, pl.ds(pl.multiple_of(1024 + t * 128, 128), 128)]
        parts = []
        for i in (0, 1):
            keep = low_half if i == 0 else ~low_half
            scores = dot(jnp.where(keep, q2, jnp.zeros_like(q2)), k2, NT) * 0.125
            scores = jnp.where(allowed, scores, -1000000000.0)
            exponent = jnp.exp(scores - jnp.max(scores, axis=1, keepdims=True))
            probs = exponent / jnp.sum(exponent, axis=1, keepdims=True)
            PR[2 * t + i] = probs
            parts.append(dot(probs.astype(BF), v2))
        MXH[y, :, cols] = jnp.where(low_half, parts[0], parts[1]).astype(BF)
        mixed_copy(t).start()
        return carry

    lax.fori_loop(0, 4, heads, 0)

    def mixed_pick(yy):
        for b in (0, 1):
            MS[yy, b * CAP : (b + 1) * CAP, :] = dot(DSP[b], MXH[yy, b * 128 : (b + 1) * 128, :]).astype(BF)

    mixed_pick(y)
    wait(*cy)
    for b in (0, 1):
        GS[b * CAP : (b + 1) * CAP, :] = dot(DSP[b], CG[b * 128 : (b + 1) * 128, :]).astype(BF)
    wait(*xo)
    co = go(cp.new(WO.at[:, quarter(p.gx), :], WO.at[:, quarter(p.gx), :], p.dev_c))
    wait(*co)
    AA[...] = XS[...] + dot(MS[y], WO[y])
    lax.fori_loop(0, 4, lambda t, carry: (mixed_copy(t).wait(), carry)[1], 0)
    mixed_pick(1 - y)
    AA[...] += dot(MS[1 - y], WO[1 - y])
    gate = jax.nn.sigmoid(jnp.sum(AA[...] * centroid, axis=1, keepdims=True))

    early = [
        here(src, dst)
        for src, dst in (
            (XG, xg_out), (QKV, qkv_out), (PR, pr_out), (MXH, mxh_out),
            (W0, w0_out), (W1, w1_out), (W2, w2_out), (WO, wo_out),
        )
    ]
    go(*early)

    wait(*el)
    at_me, at_x, at_z, at_d = p.team_places()

    def rows_of(place):
        return pl.ds(pl.multiple_of(place * 160, 32), 160)

    def part(i, place=0):
        return pl.ds(pl.multiple_of(place * 160 + i * 32, 32), 32)

    def each(fn):
        def body(i, carry):
            fn(i)
            return carry

        lax.fori_loop(0, 5, body, 0)

    class Spread:
        def __init__(self, R):
            self.R = R
            self.zi, self.xi, self.fi = cp.block(5), cp.block(5), cp.block(5)

        def same(self, first, i, place, device):
            view = self.R.at[part(i, place), :]
            return cp.at(first + i, view, view, device)

        def z(self, i):
            return self.same(self.zi, i, at_me, p.dev_z(2))

        def x(self, i):
            return self.same(self.xi, i, at_me, p.dev_x)

        def forward(self, i):
            return self.same(self.fi, i, at_z, p.dev_x)

        def start_part(self, i):
            self.z(i).start()
            self.x(i).start()

        def relay_part(self, i):
            self.z(i).wait()
            self.forward(i).start()

    class Reduce:
        def __init__(self, staging, landing):
            self.put, self.got = PS.at[staging], RB.at[landing]
            self.xi, self.di, self.zi = cp.block(1), cp.block(5), cp.block(5)

        def x(self):
            return cp.at(self.xi, self.put.at[0], self.got.at[0], p.dev_x)

        def d(self, i):
            return cp.at(self.di + i, self.put.at[1, part(i), :], self.got.at[1, part(i), :], p.dev_x)

        def z(self, i):
            return cp.at(self.zi + i, self.put.at[2, part(i), :], self.got.at[2, part(i), :], p.dev_z(2))

        def start_x(self):
            each(lambda i: self.d(i).start())
            self.x().start()

        def relay_part(self, i, own_z):
            self.d(i).wait()
            self.put[2, part(i), :] = (own_z[part(i), :] + self.got[1, part(i), :].astype(F32)).astype(BF)
            self.z(i).start()

        def result_part(self, i, own):
            self.z(i).wait()
            return (
                own[part(i), :]
                + self.got[0, part(i), :].astype(F32)
                + self.got[2, part(i), :].astype(F32)
            )

    g1, g2, g3, g4 = Spread(R1), Spread(R2), Spread(R3), Spread(R4)
    r1, r2, r3, r4 = Reduce(0, 0), Reduce(1, 1), Reduce(0, 2), Reduce(0, 3)
    mine_r = rows_of(at_me)

    R1[mine_r, :] = AA[...].astype(BF)
    each(lambda i: g1.z(i).start())
    each(lambda i: g1.x(i).start())
    R3[mine_r, :] = (gate * GS[...].astype(F32)).astype(BF)
    each(lambda i: g3.z(i).start())

    wait(*ec0[0])
    wait(*ec[0])
    wait(*ez[0])
    ec1 = e_core(0, 1, g)
    wait(*er[0])
    ec2 = e_core(0, 1, p.gx)
    wait(*ec1)
    wait(*ec2)

    def cols_of(q):
        return slice(q * 512, (q + 1) * 512)

    def first_forward(place):
        at = rows_of(place)
        total = None
        for q in (0, 1):
            active, slope = gelu_both(dot(R1[at, :], UP[0, q]))
            GP1[at, cols_of(q)] = slope
            A1[at, cols_of(q)] = active.astype(BF)
            term = dot(active.astype(BF), DN[0, q])
            total = term if total is None else total + term
        return total

    OWN[0] = first_forward(at_me)
    each(g1.relay_part)
    wait(*e1[1])
    er.append(e_relay(1))
    ec.append(e_core(1, 0, p.gx))
    each(lambda i: g1.x(i).wait())
    PS[0, 0] = first_forward(at_x).astype(BF)
    OWN[3] = first_forward(at_z)
    each(lambda i: g1.forward(i).wait())
    PS[0, 1] = first_forward(at_d).astype(BF)
    r1.start_x()
    each(lambda i: r1.relay_part(i, OWN.at[3]))
    each(lambda i: g3.x(i).start())
    r1.x().wait()

    def middle_part(i):
        branch = r1.result_part(i, OWN.at[0])
        SUMS[0, part(i), :] = branch
        R2[part(i, at_me), :] = (AA[part(i), :].astype(BF).astype(F32) + branch).astype(BF)
        g2.start_part(i)

    each(middle_part)
    each(g3.relay_part)

    wait(*ec0[1])
    wait(*ec[1])
    wait(*ez[1])
    ec1 = e_core(1, 1, g)
    wait(*er[1])
    ec2 = e_core(1, 1, p.gx)
    wait(*ec1)
    wait(*ec2)

    def second_grad(place):
        at = rows_of(place)
        total_grad = None
        for q in (0, 1):
            active, slope = gelu_both(dot(R2[at, :], UP[1, q]))
            A2[at, cols_of(q)] = active.astype(BF)
            grad = (slope * dot(R3[at, :], DN[1, q], NT)).astype(BF)
            DH[at, cols_of(q)] = grad
            term = dot(grad, UP[1, q], NT)
            total_grad = term if total_grad is None else total_grad + term
        return total_grad

    def second_forward(place):
        at = rows_of(place)
        return dot(A2[at, :512], DN[1, 0]) + dot(A2[at, 512:], DN[1, 1])

    OWN[2] = second_grad(at_me)
    OWN[1] = second_forward(at_me)
    each(g2.relay_part)
    each(lambda i: g2.x(i).wait())
    each(lambda i: g3.x(i).wait())
    PS[0, 0] = second_grad(at_x).astype(BF)
    OWN[3] = second_grad(at_z)
    each(lambda i: g2.forward(i).wait())
    each(lambda i: g3.forward(i).wait())
    PS[0, 1] = second_grad(at_d).astype(BF)
    r3.start_x()
    PS[1, 1] = second_forward(at_d).astype(BF)
    PS[1, 0] = second_forward(at_x).astype(BF)
    OWN[4] = second_forward(at_z)
    each(lambda i: r3.relay_part(i, OWN.at[3]))
    r2.start_x()

    def weight_grads(A, R, RG, GU, GD):
        def one(q, d):
            qcols = pl.ds(pl.multiple_of(q * 512, 512), 512)
            GU[q, d] = dot(R[:, dq(d)], DH[:, qcols], TN).astype(BF)
            GD[q, d] = dot(A[:, qcols], RG[:, dq(d)], TN).astype(BF)

        def body(t, carry):
            q, k = lax.rem(t, 2), lax.div(t, 2)
            d = lax.rem(k, 2)
            mine_c = lax.div(k, 2)
            cc = p.c * mine_c + (1 - p.c) * (1 - mine_c)
            one(q, 2 * d + cc)
            return carry

        return body

    def to_core(n):
        out = ()
        for k, theirs in enumerate((p.gc, p.gd)):
            out += go(
                cp.new(GU.at[:, theirs], CRU.at[n, :, k], p.dev_c),
                cp.new(GD.at[:, theirs], CRD.at[n, :, k], p.dev_c),
            )
        return out

    def add_core(n, own_u, own_d, far_u, far_d):
        for k, d in enumerate((g, p.gx)):
            far_u[k] = (GU[1, d].astype(F32) + CRU[n, 1, k].astype(F32)).astype(BF)
            far_d[k] = (GD[1, d].astype(F32) + CRD[n, 1, k].astype(F32)).astype(BF)
            own_u[k] = (GU[0, d].astype(F32) + CRU[n, 0, k].astype(F32)).astype(BF)
            own_d[k] = (GD[0, d].astype(F32) + CRD[n, 0, k].astype(F32)).astype(BF)

    body2 = weight_grads(A2, R2, R3, GU, GD)
    lax.fori_loop(0, 4, body2, 0)
    f0 = to_core(0)
    lax.fori_loop(4, 8, body2, 0)

    r3.x().wait()

    def middle_grad_part(i):
        total = r3.result_part(i, OWN.at[2])
        SUMS[1, part(i), :] = total
        R4[part(i, at_me), :] = (R3[part(i, at_me), :].astype(F32) + total).astype(BF)
        g4.start_part(i)

    each(middle_grad_part)
    wait(*f0)
    add_core(0, P2U, P2D, ZSU, ZSD)
    f1 = []
    for k in (0, 1):
        f1 += go(
            cp.new(ZSU.at[k], ZRU.at[k], p.dev_pair),
            cp.new(ZSD.at[k], ZRD.at[k], p.dev_pair),
        )

    each(lambda i: r2.relay_part(i, OWN.at[4]))
    r2.x().wait()

    def first_backward(place):
        at = rows_of(place)
        total = None
        for q in (0, 1):
            grad = (GP1[at, cols_of(q)] * dot(R4[at, :], DN[0, q], NT)).astype(BF)
            DH[at, cols_of(q)] = grad
            term = dot(grad, UP[0, q], NT)
            total = term if total is None else total + term
        return total

    OWN[0] = first_backward(at_me)
    each(g4.relay_part)
    each(lambda i: g4.x(i).wait())
    PS[0, 0] = first_backward(at_x).astype(BF)
    OWN[3] = first_backward(at_z)
    each(lambda i: g4.forward(i).wait())
    PS[0, 1] = first_backward(at_d).astype(BF)
    r4.start_x()

    def output_part(i):
        branch_two = r2.result_part(i, OWN.at[1])
        returned = (SUMS[0, part(i), :] + branch_two).astype(BF).astype(F32)
        upstream = GS[part(i), :].astype(F32)
        after = AA[part(i), :]
        gate_part = jax.nn.sigmoid(jnp.sum(after * centroid, axis=1, keepdims=True))
        OUTS[part(i), :] = (after + gate_part * returned).astype(BF)
        score_grad = jnp.sum(upstream * returned, axis=1, keepdims=True) * gate_part * (1.0 - gate_part)
        RES[part(i), :] = upstream + score_grad * centroid
        CGR[...] += jnp.broadcast_to(jnp.sum(score_grad * after, axis=0, keepdims=True), CGR.shape)

    CGR[...] = jnp.zeros_like(CGR)

    each(lambda i: r4.relay_part(i, OWN.at[3]))
    each(output_part)
    body1 = weight_grads(A1, R1, R4, GU, GD)
    lax.fori_loop(0, 4, body1, 0)
    f0 = to_core(1)
    lax.fori_loop(4, 8, body1, 0)
    r4.x().wait()

    def residual_part(i):
        arrived = (r4.result_part(i, OWN.at[0]) + SUMS[1, part(i), :]).astype(BF)
        RESS[part(i), :] = (RES[part(i), :] + arrived.astype(F32)).astype(BF)

    each(residual_part)
    wait(*f0)
    add_core(1, P1U, P1D, Z1U, Z1D)
    wait(*f1)
    for k in (0, 1):
        S2U[k] = P2U[k].astype(F32) + ZRU[k].astype(F32)
        S2D[k] = P2D[k].astype(F32) + ZRD[k].astype(F32)
    wait(*early)


def backward_kernel(
    xg_in, qkv_in, pr_in, mxh_in, w0_in, w1_in, w2_in, wo_in,
    RT, OUTS, RESS, CGR, P1U, P1D, Z1U, Z1D, S2U, S2D,
    out, tgrad, pgrad, ograd, egrad, ugrad, dgrad,
    XG, QKV, PR, MXH, W0, W1, W2, WO,
    RP, OP, RL, XH, NRM, NRMT, MG, DQ, DT, NG, NGS, NGR,
    ZRU, ZRD, XSU, XSD, XRU, XRD,
    PW0, PW1, PW2, PW3, PC0, PC1, PC2, PC3, PXS0, PXS1, PXS2, PXS3, PXR0, PXR1, PXR2, PXR3,
    PYS0, PYS1, PYS2, PYS3, PK0, PK1, PK2, PK3, PZ0, PZ1, PZ2, PZ3,
    OW, OC, OXS, OXR, OK, OZR, TE,
    send, recv, local,
):
    PW, PC, PXS, PXR = (PW0, PW1, PW2, PW3), (PC0, PC1, PC2, PC3), (PXS0, PXS1, PXS2, PXS3), (PXR0, PXR1, PXR2, PXR3)
    PYS, PK, PZ = (PYS0, PYS1, PYS2, PYS3), (PK0, PK1, PK2, PK3), (PZ0, PZ1, PZ2, PZ3)
    p = Place()
    g, y, w, x = p.g, p.y, p.w, p.x
    cp = Copies(send, recv)
    all_in = greet([p.dev_x, p.dev_c, p.dev_y, p.dev_z(1), p.dev_z(2), p.dev_z(3)])

    def go(*items):
        for item in items:
            item.start()
        return items

    def wait(*items):
        for item in items:
            item.wait()

    loads = [
        copy_in(src, dst, local.at[i])
        for i, (src, dst) in enumerate(
            (
                (xg_in, XG), (w0_in, W0), (wo_in, WO), (mxh_in, MXH),
                (qkv_in, QKV), (pr_in, PR), (w1_in, W1), (w2_in, W2),
            )
        )
    ]
    go(*loads)
    XSU[1] = S2U[1].astype(BF)
    XSD[1] = S2D[1].astype(BF)
    all_in()

    own_slots = pl.ds(pl.multiple_of(y * CAP, 16), CAP)
    peer_slots = pl.ds(pl.multiple_of((1 - y) * CAP, 16), CAP)
    ry = go(cp.new(RESS, RP, p.dev_y))
    oy = go(cp.new(OUTS.at[peer_slots, :], OP, p.dev_y))

    f1 = []
    for k in (1, 0):
        f1 += go(
            cp.new(Z1U.at[k], ZRU.at[k], p.dev_pair),
            cp.new(Z1D.at[k], ZRD.at[k], p.dev_pair),
        )
    f2 = {1: go(cp.new(XSU.at[1], XRU.at[1], p.dev_x), cp.new(XSD.at[1], XRD.at[1], p.dev_x))}

    half = pl.ds(pl.multiple_of(x * 512, 512), 512)
    other = pl.ds(pl.multiple_of((1 - x) * 512, 512), 512)

    wait(loads[0], loads[1])
    values = XG[...].astype(F32)
    centred = values - jnp.mean(values, axis=1, keepdims=True)
    inverse = lax.rsqrt(jnp.mean(centred * centred, axis=1, keepdims=True) + 1e-05)
    XH[...] = centred * inverse
    pick = one_hot(8, EXTRA)
    gain = dot(pick, W0[:, 512:], NT)[0:1, :]
    NRM[...] = (XH[...] * gain).astype(BF)
    NRMT[...] = NRM[...].T
    ugrad[1, :, half] = S2U[0]
    dgrad[1, half, :] = S2D[0]

    wait(*ry)
    for b in (0, 1):
        slots = slice(b * CAP, (b + 1) * CAP)
        RL[b * 128 : (b + 1) * 128, :] = (
            dot(dispatch_block(RT[b], y), RESS[slots, :], TN)
            + dot(dispatch_block(RT[b], 1 - y), RP[slots, :], TN)
        ).astype(BF)
    wait(loads[2])
    MG[...] = dot(RL[...], WO[y], NT).astype(BF)

    def rows4(d):
        return pl.ds(pl.multiple_of(d * 128, 128), 128)

    def dq(d):
        return pl.ds(pl.multiple_of(d * 256, 256), 256)

    def row32(v):
        return pl.ds(pl.multiple_of(v * 32, 32), 32)

    def out_rows(d):
        OW[rows4(d), :] = dot(MXH[y, :, rows4(d)], RL[...], TN).astype(BF)

    low_half = lax.broadcasted_iota(jnp.int32, (256, 128), 1) < 64

    def heads(t):
        c0 = slice(t * 128, (t + 1) * 128)
        c1 = slice(512 + t * 128, 512 + (t + 1) * 128)
        c2 = slice(1024 + t * 128, 1024 + (t + 1) * 128)
        q2, k2, v2, m2 = QKV[:, c0], QKV[:, c1], QKV[:, c2], MG[:, c0]
        parts = []
        for i in (0, 1):
            keep = low_half if i == 0 else ~low_half
            probs = PR[2 * t + i]
            probs_grad = dot(jnp.where(keep, m2, jnp.zeros_like(m2)), v2, NT)
            delta = jnp.sum(probs_grad * probs, axis=1, keepdims=True)
            scores_grad = (probs * (probs_grad - delta)).astype(BF)
            parts.append(
                (
                    dot(scores_grad, k2) * 0.125,
                    dot(scores_grad, q2, TN) * 0.125,
                    dot(probs.astype(BF), m2, TN),
                )
            )
        for s, c in enumerate((c0, c1, c2)):
            grad = jnp.where(low_half, parts[0][s], parts[1][s]).astype(BF)
            DQ[:, c] = grad
            DT[t, :, s * 128 : (s + 1) * 128] = grad

    pc, px, py, pz = [None] * 4, [None] * 4, [None] * 4, [None] * 4

    def to_core(t):
        PW[t][:, :384] = dot(NRMT[...], DT[t]).astype(BF)
        pc[t] = sum(
            (go(cp.new(PW[t].at[dq(d), :], PC[t].at[k], p.dev_c)) for k, d in enumerate((p.gc, p.gd))), ()
        )

    def to_x(t):
        wait(*pc[t])
        PXS[t][...] = (PW[t][dq(p.gx), :].astype(F32) + PC[t][1].astype(F32)).astype(BF)
        px[t] = go(cp.new(PXS[t], PXR[t], p.dev_x))

    def summed(t, plane):
        rows = rows4(plane)
        full = pl.ds(pl.multiple_of(g * 256 + plane * 128, 128), 128)
        total = PW[t][full, :].astype(F32) + PC[t][0, rows, :].astype(F32) + PXR[t][rows, :].astype(F32)
        return total.astype(BF)

    def to_y(t):
        wait(*px[t])
        PYS[t][...] = summed(t, 1 - y)
        py[t] = go(cp.new(PYS[t], PK[t].at[1], p.dev_y))
        PK[t][0] = summed(t, y)

    def to_z(t):
        wait(*py[t])
        pz[t] = sum(
            (
                go(cp.new(PK[t].at[:, row32(lax.rem(w + k, 4)), :], PZ[t].at[k - 1], p.dev_z(k)))
                for k in (2, 1, 3)
            ),
            (),
        )

    wait(loads[4], loads[5])
    heads(0)
    to_core(0)
    wait(loads[3])
    out_rows(p.gc)
    out_rows(p.gd)
    oc = sum((go(cp.new(OW.at[rows4(d), :], OC.at[k], p.dev_c)) for k, d in enumerate((p.gc, p.gd))), ())
    heads(1)
    to_core(1)
    to_x(0)
    out_rows(g)
    out_rows(p.gx)
    heads(2)
    to_core(2)
    to_x(1)
    wait(*oc)
    OXS[...] = (OW[rows4(p.gx), :].astype(F32) + OC[1].astype(F32)).astype(BF)
    heads(3)

    wait(loads[6], loads[7])
    NG[...] = (
        dot(DQ[:, :512], W0[:, :512], NT) + dot(DQ[:, 512:1024], W1[...], NT) + dot(DQ[:, 1024:], W2[...], NT)
    )
    NGS[...] = NG[rows4(1 - y), :].astype(BF)
    ny = go(cp.new(NGS, NGR, p.dev_y))
    gain_row = jnp.sum(NG[...] * XH[...], axis=0, keepdims=True)
    line = lax.broadcasted_iota(jnp.int32, (8, 1024), 0)
    stack = jnp.where(line == 0, gain_row, jnp.where(line == 1 + y, CGR[0:1, :], 0.0)).astype(BF)
    PW3[:, 384:] = dot(stack, pick, TN).astype(BF)
    to_core(3)
    to_x(2)
    to_y(0)
    to_x(3)
    ox = go(cp.new(OXS, OXR, p.dev_x))
    to_y(1)
    to_z(0)

    wait(*ny)
    own_rows = rows4(y)
    normed = XH[own_rows, :]
    mine = XG[own_rows, :].astype(F32)
    mine = mine - jnp.mean(mine, axis=1, keepdims=True)
    inverse = lax.rsqrt(jnp.mean(mine * mine, axis=1, keepdims=True) + 1e-05)
    scaled = (NG[own_rows, :] + NGR[...].astype(F32)) * gain
    tgrad[...] = RL[own_rows, :].astype(F32) + inverse * (
        scaled
        - jnp.mean(scaled, axis=1, keepdims=True)
        - normed * jnp.mean(scaled * normed, axis=1, keepdims=True)
    )
    to_y(2)
    to_z(1)

    wait(*f1)
    XSU[0] = (P1U[1].astype(F32) + ZRU[1].astype(F32)).astype(BF)
    XSD[0] = (P1D[1].astype(F32) + ZRD[1].astype(F32)).astype(BF)
    f2[0] = go(cp.new(XSU.at[0], XRU.at[0], p.dev_x), cp.new(XSD.at[0], XRD.at[0], p.dev_x))
    wait(*oy)
    route_own = RT[y]
    out[...] = (
        dot(dispatch_block(route_own, y), OUTS[own_slots, :], TN)
        + dot(dispatch_block(route_own, 1 - y), OP[...], TN)
    ).astype(BF)
    to_y(3)
    to_z(2)
    ugrad[0, :, half] = P1U[0].astype(F32) + ZRU[0].astype(F32)
    dgrad[0, half, :] = P1D[0].astype(F32) + ZRD[0].astype(F32)
    wait(*f2[1])
    ugrad[1, :, other] = XRU[1].astype(F32)
    dgrad[1, other, :] = XRD[1].astype(F32)
    to_z(3)

    wait(*ox)
    OK[...] = (OW[rows4(g), :].astype(F32) + OC[0].astype(F32) + OXR[...].astype(F32)).astype(BF)
    oz = sum(
        (go(cp.new(OK.at[row32(lax.rem(w + k, 4)), :], OZR.at[k - 1], p.dev_z(k))) for k in (2, 1, 3)), ()
    )
    own32 = row32(w)
    for t in range(4):
        wait(*pz[t])
        sums = [
            PK[t][i, own32, :].astype(F32)
            + PZ[t][0, i].astype(F32)
            + PZ[t][1, i].astype(F32)
            + PZ[t][2, i].astype(F32)
            for i in (0, 1)
        ]
        for plane in (0, 1):
            kept = jnp.where(y == plane, sums[0], sums[1])
            for s in range(3):
                first = s * 1024 + t * 256 + plane * 128
                pgrad[:, first : first + 128] = kept[:, s * 128 : (s + 1) * 128]
        if t == 3:
            TE[0:32, :] = sums[0][:, 384:] + sums[1][:, 384:]
    egrad[...] = TE[...].T[0:8, :]
    wait(*f2[0])
    ugrad[0, :, other] = XRU[0].astype(F32)
    dgrad[0, other, :] = XRD[0].astype(F32)
    wait(*oz)
    ograd[...] = OK[own32, :].astype(F32) + OZR[0].astype(F32) + OZR[1].astype(F32) + OZR[2].astype(F32)


def finish_kernel(
    out, tgrad, pgrad, ograd, egrad, ugrad, dgrad, out2, tgrad2, gain, pgrad2, ograd2, cent, ugrad2, dgrad2
):
    out2[0] = out[...]
    tgrad2[0] = tgrad[...]
    pgrad2[...] = pgrad[...]
    ograd2[...] = ograd[...]
    gain[...] = egrad[0:1, :32]
    cent[...] = egrad[1:3, :32]
    ugrad2[0] = ugrad[...]
    dgrad2[0] = dgrad[...]


def vmem(shape, dtype=BF):
    return pltpu.VMEM(shape, dtype)


def fast_shards(
    tokens, cotangent, norm_gain, project_weight, output_weight, centroids,
    expert_up, expert_down, sequence_lengths, block_order, routes,
):
    in_vmem = pl.BlockSpec(memory_space=pltpu.VMEM)
    in_any = pl.BlockSpec(memory_space=pl.ANY)
    in_smem = pl.BlockSpec(memory_space=pltpu.SMEM)
    shape = jax.ShapeDtypeStruct
    ext = jnp.pad(
        jnp.concatenate([norm_gain[None], centroids], axis=0).astype(F32), ((0, 5), (0, EXTRA - 32))
    )
    mid_shapes = [
        ((256, 1024), BF),
        ((256, 1536), BF),
        ((8, 256, 256), F32),
        ((2, 256, 512), BF),
        ((1024, 512 + EXTRA), BF),
        ((1024, 512), BF),
        ((1024, 512), BF),
        ((2, 512, 1024), BF),
        ((2, 8, 128), F32),
        ((160, 1024), BF),
        ((160, 1024), BF),
        ((8, 1024), F32),
        ((2, 256, 512), BF),
        ((2, 512, 256), BF),
        ((2, 256, 512), BF),
        ((2, 512, 256), BF),
        ((2, 256, 512), F32),
        ((2, 512, 256), F32),
    ]
    mid = pl.pallas_call(
        forward_kernel,
        name="forward",
        out_shape=[shape(*s) for s in mid_shapes],
        in_specs=[in_smem] * 2 + [in_vmem] * 6 + [in_any] * 2,
        out_specs=[in_any] * 8 + [in_vmem] * (len(mid_shapes) - 8),
        scratch_shapes=[vmem(*s) for s in mid_shapes[:8]]
        + [
            vmem((2, 32, 512 + EXTRA)),
            vmem((2, 32, 512)),
            vmem((2, 32, 512)),
            vmem((256, 1024)),
            vmem((256, 1024), F32),
            vmem((256, 1024)),
            vmem((2, 2, 1024, 512)),
            vmem((2, 2, 512, 1024)),
            vmem((2, CAP, 128)),
            vmem((160, 1024), F32),
            vmem((160, 1024)),
            vmem((2, 160, 512)),
            vmem((160, 1024), F32),
        ]
        + [vmem((640, 1024))] * 4
        + [
            vmem((4, 3, 160, 1024)),
            vmem((2, 3, 160, 1024)),
            vmem((5, 160, 1024), F32),
            vmem((160, 1024), F32),
            vmem((640, 1024), F32),
            vmem((640, 1024)),
            vmem((640, 1024)),
            vmem((640, 1024)),
            vmem((2, 160, 1024), F32),
            vmem((2, 4, 256, 512)),
            vmem((2, 4, 512, 256)),
            vmem((2, 2, 2, 256, 512)),
            vmem((2, 2, 2, 512, 256)),
            vmem((2, 256, 512)),
            vmem((2, 512, 256)),
            vmem((2, 256, 512)),
            vmem((2, 512, 256)),
            vmem((2, 256, 512)),
            vmem((2, 512, 256)),
            pltpu.SemaphoreType.DMA((208,)),
            pltpu.SemaphoreType.DMA((208,)),
            pltpu.SemaphoreType.DMA((24,)),
        ],
        compiler_params=pltpu.CompilerParams(
            collective_id=0, has_side_effects=True, vmem_limit_bytes=VMEM_LIMIT
        ),
    )(
        sequence_lengths[0], block_order[0], tokens[0], cotangent[0], routes.reshape(1, 128),
        project_weight, output_weight, ext, expert_up[0], expert_down[0],
    )
    out_shapes = [
        ((128, 1024), BF),
        ((128, 1024), F32),
        ((32, 3072), F32),
        ((32, 1024), F32),
        ((8, EXTRA), F32),
        ((2, 256, 1024), F32),
        ((2, 1024, 256), F32),
    ]
    out, tgrad, pgrad, ograd, egrad, ugrad, dgrad = pl.pallas_call(
        backward_kernel,
        name="backward",
        out_shape=[shape(*s) for s in out_shapes],
        in_specs=[in_any] * 8 + [in_vmem] * (len(mid_shapes) - 8),
        out_specs=[in_vmem] * len(out_shapes),
        scratch_shapes=[vmem(*s) for s in mid_shapes[:8]]
        + [
            vmem((160, 1024)),
            vmem((CAP, 1024)),
            vmem((256, 1024)),
            vmem((256, 1024), F32),
            vmem((256, 1024)),
            vmem((1024, 256)),
            vmem((256, 512)),
            vmem((256, 1536)),
            vmem((4, 256, 384)),
            vmem((256, 1024), F32),
            vmem((128, 1024)),
            vmem((128, 1024)),
            vmem((2, 256, 512)),
            vmem((2, 512, 256)),
            vmem((2, 256, 512)),
            vmem((2, 512, 256)),
            vmem((2, 256, 512)),
            vmem((2, 512, 256)),
        ]
        + [vmem((1024, c)) for c in CHUNKS]
        + [vmem((2, 256, c)) for c in CHUNKS]
        + [vmem((256, c)) for c in CHUNKS]
        + [vmem((256, c)) for c in CHUNKS]
        + [vmem((128, c)) for c in CHUNKS]
        + [vmem((2, 128, c)) for c in CHUNKS]
        + [vmem((3, 2, 32, c)) for c in CHUNKS]
        + [
            vmem((512, 1024)),
            vmem((2, 128, 1024)),
            vmem((128, 1024)),
            vmem((128, 1024)),
            vmem((128, 1024)),
            vmem((3, 32, 1024)),
            vmem((EXTRA, EXTRA), F32),
            pltpu.SemaphoreType.DMA((64,)),
            pltpu.SemaphoreType.DMA((64,)),
            pltpu.SemaphoreType.DMA((8,)),
        ],
        compiler_params=pltpu.CompilerParams(
            collective_id=1, has_side_effects=True, vmem_limit_bytes=VMEM_LIMIT
        ),
    )(*mid)
    out, tgrad, gain, pgrad, ograd, cent, ugrad, dgrad = pl.pallas_call(
        finish_kernel,
        name="finish",
        out_shape=[
            shape((1, 128, 1024), BF),
            shape((1, 128, 1024), F32),
            shape((1, 32), F32),
            shape((32, 3072), F32),
            shape((32, 1024), F32),
            shape((2, 32), F32),
            shape((1, 2, 256, 1024), F32),
            shape((1, 2, 1024, 256), F32),
        ],
        in_specs=[in_vmem] * 7,
        out_specs=[in_vmem] * 8,
        compiler_params=pltpu.CompilerParams(vmem_limit_bytes=VMEM_LIMIT),
    )(out, tgrad, pgrad, ograd, egrad, ugrad, dgrad)
    return out, tgrad, gain[0], pgrad, ograd, cent, ugrad, dgrad


def solution(mesh):
    sizes = dict(mesh.shape)
    fast = sizes == {"grp": 4, "ctx": 2, "wsh": 4}
    return jax.shard_map(
        fast_shards if fast else shards,
        mesh=mesh,
        in_specs=IN_SPECS,
        out_specs=OUT_SPECS,
        check_vma=False,
    )
```

```python
import math

import jax
import jax.numpy as jnp
from jax import lax
from jax.experimental import pallas as pl
from jax.experimental.pallas import tpu as pltpu
from jax.sharding import PartitionSpec as P

HEADS = 16
HDIM = 64
BLK = 128


precise = lax.Precision.HIGHEST


def place_rows(order_row, lengths_row, total_rows):
    row_index = jnp.arange(total_rows, dtype=jnp.int32)
    picked = (row_index // BLK)[:, None] == jnp.arange(order_row.shape[0], dtype=jnp.int32)[None, :]
    blocks = jnp.sum(jnp.where(picked, order_row[None, :], 0), axis=1)
    token_place = blocks * BLK + row_index % BLK
    bounds = jnp.cumsum(lengths_row)
    sequence = jnp.sum((token_place[:, None] >= bounds[None, :]).astype(jnp.int32), axis=1)
    return (token_place, sequence)


def normalize(values):
    average = jnp.mean(values, axis=-1, keepdims=True)
    centred = values - average
    inverse = lax.rsqrt(jnp.mean(centred * centred, axis=-1, keepdims=True) + 1e-05)
    return (centred * inverse, inverse)


def head_slice(matrix, section, offset, heads_per):
    width_part = heads_per * HDIM
    first_col = offset + section * width_part
    return matrix[:, first_col : first_col + width_part].reshape(matrix.shape[0], heads_per, HDIM)


def spread_rows(local_rows):
    return lax.all_gather(local_rows, "wsh", axis=0, tiled=True)


def collect_rows(partial_term):
    return lax.psum_scatter(
        partial_term.astype(jnp.bfloat16), "wsh", scatter_dimension=0, tiled=True
    ).astype(jnp.float32)


def trade_rows(slots_rows, peer_count, capacity):
    shaped = slots_rows.reshape(peer_count, capacity, slots_rows.shape[-1])
    moved = lax.all_to_all(shaped, "ctx", split_axis=0, concat_axis=0, tiled=True)
    return moved.reshape(peer_count * capacity, slots_rows.shape[-1])


def gelu_pullback(hidden, incoming):
    value_out, pullback = jax.vjp(jax.nn.gelu, hidden)
    return pullback(incoming)[0]


def shards(
    tokens,
    cotangent,
    norm_gain,
    project_weight,
    output_weight,
    centroids,
    expert_up,
    expert_down,
    sequence_lengths,
    block_order,
    routes,
):
    local_rows = tokens.shape[1]
    model_width = tokens.shape[2]
    peer_count = lax.axis_size("ctx")
    position = lax.axis_index("ctx")
    total_rows = local_rows * peer_count
    capacity = max(2, (5 * local_rows + 4 * peer_count - 1) // (4 * peer_count))
    slot_count = peer_count * capacity
    score_scale = 1.0 / math.sqrt(HDIM)
    heads_per = 4
    sections = HEADS // heads_per
    inputs_f = tokens[0].astype(jnp.float32)
    upstream = cotangent[0].astype(jnp.float32)
    project_full, output_full, gain_full, centroid_full = (
        lax.all_gather(project_weight, ("grp", "ctx", "wsh"), axis=0, tiled=True),
        lax.all_gather(output_weight, ("grp", "ctx", "wsh"), axis=0, tiled=True),
        lax.all_gather(norm_gain, ("grp", "ctx", "wsh"), axis=0, tiled=True),
        lax.all_gather(centroids, ("grp", "ctx", "wsh"), axis=1, tiled=True),
    )
    up_full, down_full = (
        lax.all_gather(expert_up, "grp", axis=2, tiled=True),
        lax.all_gather(expert_down, "grp", axis=3, tiled=True),
    )
    place_all, sequence_all = place_rows(block_order[0], sequence_lengths[0], total_rows)
    place_own = lax.dynamic_slice_in_dim(place_all, position * local_rows, local_rows)
    sequence_own = lax.dynamic_slice_in_dim(sequence_all, position * local_rows, local_rows)
    allowed = (sequence_own[:, None] == sequence_all[None, :]) & (
        place_all[None, :] <= place_own[:, None]
    )
    normed, inverse = normalize(inputs_f)
    gain_values = gain_full.astype(jnp.float32)
    normed_low = (normed * gain_values).astype(jnp.bfloat16)
    projected = jnp.dot(normed_low, project_full, preferred_element_type=jnp.float32)
    queries = projected[:, :model_width].astype(jnp.bfloat16)
    keyvalue = projected[:, model_width:].astype(jnp.bfloat16)
    keyvalue_all = lax.all_gather(keyvalue, "ctx", axis=0, tiled=True)
    mixed_parts = []
    logsum_parts = []
    for section in range(sections):
        head_query = head_slice(queries, section, 0, heads_per)
        head_key = head_slice(keyvalue_all, section, 0, heads_per)
        head_value = head_slice(keyvalue_all, section, model_width, heads_per)
        scores = (
            jnp.einsum("tgd,sgd->gts", head_query, head_key, preferred_element_type=jnp.float32)
            * score_scale
        )
        scores = jnp.where(allowed[None], scores, -1000000000.0)
        largest = jnp.max(scores, axis=-1, keepdims=True)
        exponent = jnp.exp(scores - largest)
        totals = jnp.sum(exponent, axis=-1, keepdims=True)
        weights = (exponent / totals).astype(jnp.bfloat16)
        mixed_part = jnp.einsum(
            "gts,sgd->tgd", weights, head_value, preferred_element_type=jnp.float32
        )
        mixed_parts.append(mixed_part.reshape(local_rows, heads_per * HDIM))
        logsum_parts.append((largest + jnp.log(totals))[:, :, 0])
    mixed_all = jnp.concatenate(mixed_parts, axis=1).astype(jnp.bfloat16)
    logsum = jnp.concatenate(logsum_parts, axis=0)
    after_attention = inputs_f + jnp.dot(mixed_all, output_full, preferred_element_type=jnp.float32)
    route_ids = routes[0, :, 0]
    member = route_ids[:, None] == jnp.arange(peer_count, dtype=jnp.int32)[None, :]
    member_f = member.astype(jnp.float32)
    picked_centroid = jnp.dot(member_f, centroid_full.astype(jnp.float32), precision=precise)
    gate_value = jax.nn.sigmoid(jnp.sum(after_attention * picked_centroid, axis=-1))
    member_int = member.astype(jnp.int32)
    ranking = jnp.sum((jnp.cumsum(member_int, axis=0) - 1) * member_int, axis=1)
    slot_index = route_ids * capacity + ranking
    dispatch = (slot_index[None, :] == jnp.arange(slot_count, dtype=jnp.int32)[:, None]).astype(
        jnp.bfloat16
    )
    sent_rows = jnp.dot(
        dispatch, after_attention.astype(jnp.bfloat16), preferred_element_type=jnp.float32
    ).astype(jnp.bfloat16)
    arrived = trade_rows(sent_rows, peer_count, capacity)
    up_first = up_full[0, 0]
    up_second = up_full[0, 1]
    down_first = down_full[0, 0]
    down_second = down_full[0, 1]
    gathered_one = spread_rows(arrived)
    hidden_one = jnp.dot(gathered_one, up_first, preferred_element_type=jnp.float32)
    active_one = jax.nn.gelu(hidden_one).astype(jnp.bfloat16)
    branch_one = collect_rows(jnp.dot(active_one, down_first, preferred_element_type=jnp.float32))
    middle = (arrived.astype(jnp.float32) + branch_one).astype(jnp.bfloat16)
    gathered_two = spread_rows(middle)
    hidden_two = jnp.dot(gathered_two, up_second, preferred_element_type=jnp.float32)
    active_two = jax.nn.gelu(hidden_two).astype(jnp.bfloat16)
    branch_two = collect_rows(jnp.dot(active_two, down_second, preferred_element_type=jnp.float32))
    expert_out = (branch_one + branch_two).astype(jnp.bfloat16)
    returned = trade_rows(expert_out, peer_count, capacity)
    returned_tok = jnp.einsum("st,sd->td", dispatch, returned, preferred_element_type=jnp.float32)
    output = after_attention + gate_value[:, None] * returned_tok
    gate_grad = jnp.sum(upstream * returned_tok, axis=-1)
    score_grad = gate_grad * gate_value * (1.0 - gate_value)
    centroid_term = jnp.dot(member_f.T, score_grad[:, None] * after_attention, precision=precise)
    branch_grad = (gate_value[:, None] * upstream).astype(jnp.bfloat16)
    branch_sent = jnp.dot(dispatch, branch_grad, preferred_element_type=jnp.float32).astype(
        jnp.bfloat16
    )
    branch_arrived = trade_rows(branch_sent, peer_count, capacity)
    grad_two = spread_rows(branch_arrived)
    hidden_two_grad = gelu_pullback(
        hidden_two, jnp.dot(grad_two, down_second.T, preferred_element_type=jnp.float32)
    ).astype(jnp.bfloat16)
    down_second_grad = jnp.dot(active_two.T, grad_two, preferred_element_type=jnp.float32)
    up_second_grad = jnp.dot(gathered_two.T, hidden_two_grad, preferred_element_type=jnp.float32)
    middle_grad = collect_rows(
        jnp.dot(hidden_two_grad, up_second.T, preferred_element_type=jnp.float32)
    )
    first_branch_grad = (branch_arrived.astype(jnp.float32) + middle_grad).astype(jnp.bfloat16)
    grad_one = spread_rows(first_branch_grad)
    hidden_one_grad = gelu_pullback(
        hidden_one, jnp.dot(grad_one, down_first.T, preferred_element_type=jnp.float32)
    ).astype(jnp.bfloat16)
    down_first_grad = jnp.dot(active_one.T, grad_one, preferred_element_type=jnp.float32)
    up_first_grad = jnp.dot(gathered_one.T, hidden_one_grad, preferred_element_type=jnp.float32)
    arrived_grad = (
        collect_rows(jnp.dot(hidden_one_grad, up_first.T, preferred_element_type=jnp.float32))
        + middle_grad
    ).astype(jnp.bfloat16)
    home_grad = trade_rows(arrived_grad, peer_count, capacity)
    home_grad_tok = jnp.einsum("st,sd->td", dispatch, home_grad, preferred_element_type=jnp.float32)
    up_terms = jnp.stack([up_first_grad, up_second_grad])[None]
    down_terms = jnp.stack([down_first_grad, down_second_grad])[None]
    up_grad_out, down_grad_out = (
        lax.psum_scatter(
            up_terms.astype(jnp.bfloat16), "grp", scatter_dimension=2, tiled=True
        ).astype(jnp.float32),
        lax.psum_scatter(
            down_terms.astype(jnp.bfloat16), "grp", scatter_dimension=3, tiled=True
        ).astype(jnp.float32),
    )
    residual_grad = upstream + score_grad[:, None] * picked_centroid + home_grad_tok
    residual_low = residual_grad.astype(jnp.bfloat16)
    output_term = jnp.dot(mixed_all.T, residual_low, preferred_element_type=jnp.float32)
    mixed_grad = jnp.dot(residual_low, output_full.T, preferred_element_type=jnp.float32).astype(
        jnp.bfloat16
    )
    query_grads = []
    key_grads = []
    value_grads = []
    delta_parts = []
    for section in range(sections):
        head_query = head_slice(queries, section, 0, heads_per)
        head_key = head_slice(keyvalue_all, section, 0, heads_per)
        head_value = head_slice(keyvalue_all, section, model_width, heads_per)
        head_grad = head_slice(mixed_grad, section, 0, heads_per)
        scores = (
            jnp.einsum("tgd,sgd->gts", head_query, head_key, preferred_element_type=jnp.float32)
            * score_scale
        )
        scores = jnp.where(allowed[None], scores, -1000000000.0)
        probs = jnp.exp(
            scores - logsum[section * heads_per : (section + 1) * heads_per][:, :, None]
        )
        probs_grad = jnp.einsum(
            "tgd,sgd->gts", head_grad, head_value, preferred_element_type=jnp.float32
        )
        row_delta = jnp.sum(probs_grad * probs, axis=-1)
        scores_grad = (probs * (probs_grad - row_delta[:, :, None])).astype(jnp.bfloat16)
        query_part = (
            jnp.einsum("gts,sgd->tgd", scores_grad, head_key, preferred_element_type=jnp.float32)
            * score_scale
        )
        query_grads.append(query_part.reshape(local_rows, heads_per * HDIM))
        delta_parts.append(row_delta)
        key_part = (
            jnp.einsum("gts,tgd->sgd", scores_grad, head_query, preferred_element_type=jnp.float32)
            * score_scale
        )
        value_part = jnp.einsum(
            "gts,tgd->sgd",
            probs.astype(jnp.bfloat16),
            head_grad,
            preferred_element_type=jnp.float32,
        )
        key_grads.append(key_part.reshape(total_rows, heads_per * HDIM))
        value_grads.append(value_part.reshape(total_rows, heads_per * HDIM))
    query_grad = jnp.concatenate(query_grads, axis=1).astype(jnp.bfloat16)
    keyvalue_terms = jnp.concatenate(key_grads + value_grads, axis=1)
    keyvalue_grad = lax.psum_scatter(
        keyvalue_terms.astype(jnp.bfloat16), "ctx", scatter_dimension=0, tiled=True
    )
    projected_grad = jnp.concatenate([query_grad, keyvalue_grad], axis=1)
    project_term = jnp.dot(normed_low.T, projected_grad, preferred_element_type=jnp.float32)
    normed_grad = jnp.dot(projected_grad, project_full.T, preferred_element_type=jnp.float32)
    gain_term = jnp.sum(normed_grad * normed, axis=0)
    scaled_grad = normed_grad * gain_values
    input_grad = residual_grad + inverse * (
        scaled_grad
        - jnp.mean(scaled_grad, axis=-1, keepdims=True)
        - normed * jnp.mean(scaled_grad * normed, axis=-1, keepdims=True)
    )
    project_grad, output_grad, gain_grad, centroid_grad = (
        lax.psum_scatter(project_term, ("grp", "ctx", "wsh"), scatter_dimension=0, tiled=True),
        lax.psum_scatter(output_term, ("grp", "ctx", "wsh"), scatter_dimension=0, tiled=True),
        lax.psum_scatter(gain_term, ("grp", "ctx", "wsh"), scatter_dimension=0, tiled=True),
        lax.psum_scatter(centroid_term, ("grp", "ctx", "wsh"), scatter_dimension=1, tiled=True),
    )
    return (
        output.astype(jnp.bfloat16)[None],
        input_grad[None],
        gain_grad,
        project_grad,
        output_grad,
        centroid_grad,
        up_grad_out,
        down_grad_out,
    )


VMEM_LIMIT = 61 * 2**20
CHUNKS = (384, 384, 384, 512)

IN_SPECS = (
    P(("grp", "wsh"), "ctx", None),
    P(("grp", "wsh"), "ctx", None),
    P(("grp", "ctx", "wsh")),
    P(("grp", "ctx", "wsh"), None),
    P(("grp", "ctx", "wsh"), None),
    P(None, ("grp", "ctx", "wsh")),
    P("ctx", None, "grp", "wsh"),
    P("ctx", None, "wsh", "grp"),
    P(("grp", "wsh"), None),
    P(("grp", "wsh"), None),
    P(("grp", "wsh"), "ctx", None),
)
OUT_SPECS = (
    P(("grp", "wsh"), "ctx", None),
    P(("grp", "wsh"), "ctx", None),
    P(("grp", "ctx", "wsh")),
    P(("grp", "ctx", "wsh"), None),
    P(("grp", "ctx", "wsh"), None),
    P(None, ("grp", "ctx", "wsh")),
    P("ctx", None, "grp", "wsh"),
    P("ctx", None, "wsh", "grp"),
)

BF = jnp.bfloat16
F32 = jnp.float32
NN = ((1,), (0,))
NT = ((1,), (1,))
TN = ((0,), (0,))
MESH = pl.DeviceIdType.MESH
GELU_C = 0.7978845608028654
EXTRA = 128
CAP = 80


def dot(a, b, dims=NN):
    return lax.dot_general(a, b, (dims, ((), ())), preferred_element_type=F32)


def gelu_both(h):
    sq = h * h
    t = jnp.tanh(GELU_C * h * (1.0 + 0.044715 * sq))
    half = 0.5 * (1.0 + t)
    slope = half + 0.5 * h * (1.0 - t * t) * (GELU_C * (1.0 + 3.0 * 0.044715 * sq))
    return h * half, slope


def copy_in(src, dst, sem):
    return pltpu.make_async_copy(src, dst, sem)


class Copies:
    def __init__(self, send, recv):
        self.send, self.recv, self.used = send, recv, 0

    def block(self, count):
        first = self.used
        self.used += count
        return first

    def at(self, index, src, dst, device):
        return pltpu.make_async_remote_copy(
            src_ref=src,
            dst_ref=dst,
            send_sem=self.send.at[index],
            recv_sem=self.recv.at[index],
            device_id=device,
            device_id_type=MESH,
        )

    def new(self, src, dst, device):
        return self.at(self.block(1), src, dst, device)


class Place:
    def __init__(self):
        g, y, w = lax.axis_index("grp"), lax.axis_index("ctx"), lax.axis_index("wsh")
        self.g, self.y, self.w = g, y, w
        self.x = lax.div(g, 2)
        self.c = g - 2 * self.x
        self.gx = 2 * (1 - self.x) + self.c
        self.gc = 2 * self.x + 1 - self.c
        self.gd = 2 * (1 - self.x) + 1 - self.c
        self.wb = lax.rem(w, 2)
        self.w1 = w + 1 - 2 * self.wb
        self.w2 = lax.rem(w + 2, 4)
        self.dev_x = (self.gx, y, w)
        self.dev_c = (self.gc, y, w)
        self.dev_y = (g, 1 - y, w)
        self.dev_pair = (g, y, self.w1)
        self.dev_z = lambda k: (g, y, lax.rem(w + k, 4))

    def team_places(self):
        mine = 2 * self.x + lax.div(self.w, 2)
        x_side = 2 * (1 - self.x) + lax.div(self.w, 2)
        flip = 1 - 2 * lax.div(self.w, 2)
        return mine, x_side, mine + flip, x_side + flip


def greet(devices):
    barrier = pltpu.get_barrier_semaphore()
    for device in devices:
        pl.semaphore_signal(barrier, inc=1, device_id=device, device_id_type=MESH)
    return lambda: pl.semaphore_wait(barrier, len(devices))


def one_hot(rows, columns):
    same = lax.broadcasted_iota(jnp.int32, (rows, columns), 0) == lax.broadcasted_iota(
        jnp.int32, (rows, columns), 1
    )
    return same.astype(F32).astype(BF)


def dispatch_block(route_rows, expert):
    member = (route_rows == expert.astype(F32)).astype(F32)
    earlier = lax.broadcasted_iota(jnp.int32, (128, 128), 0) < lax.broadcasted_iota(jnp.int32, (128, 128), 1)
    rank = dot(member.astype(BF), earlier.astype(F32).astype(BF))
    slot = lax.broadcasted_iota(jnp.int32, (CAP, 128), 0).astype(F32)
    hit = (jnp.broadcast_to(rank[0:1, :], (CAP, 128)) == slot) & (
        jnp.broadcast_to(member[0:1, :], (CAP, 128)) > 0.5
    )
    return hit.astype(F32).astype(BF)


def place_of(lengths, order, index):
    place = jnp.where(index < 128, order[0], order[1]) * 128 + lax.rem(index, 128)
    bound = lengths[0]
    sequence = jnp.where(place >= bound, 1, 0)
    for part in (1, 2):
        bound = bound + lengths[part]
        sequence = sequence + jnp.where(place >= bound, 1, 0)
    return place, sequence


def forward_kernel(
    lengths, order, tok, cot, rts, pw, wo_in, ext, up_in, dn_in,
    xg_out, qkv_out, pr_out, mxh_out, w0_out, w1_out, w2_out, wo_out,
    RT, OUTS, RESS, CGR, P1U, P1D, Z1U, Z1D, S2U, S2D,
    XG, QKV, PR, MXH, W0, W1, W2, WO,
    WS0, WS1, WS2, CG, XH, NRM, UP, DN, DSP, XS, GS, MS, AA,
    R1, R2, R3, R4, RB, PS, OWN, RES, GP1, A1, A2, DH, SUMS,
    GU, GD, CRU, CRD, P2U, P2D, ZSU, ZSD, ZRU, ZRD,
    send, recv, local,
):
    p = Place()
    g, y, w, x = p.g, p.y, p.w, p.x
    cp = Copies(send, recv)
    all_in = greet([p.dev_x, p.dev_c, p.dev_y, p.dev_z(1), p.dev_z(2), p.dev_z(3)])
    nlocal = [0]

    def here(src, dst):
        nlocal[0] += 1
        return copy_in(src, dst, local.at[nlocal[0] - 1])

    def go(*items):
        for item in items:
            item.start()
        return items

    def wait(*items):
        for item in items:
            item.wait()

    W, WS = (W0, W1, W2), (WS0, WS1, WS2)
    for ch in range(3):
        for t in range(4):
            for plane in (0, 1):
                first = ch * 1024 + t * 256 + plane * 128
                WS[ch][plane, :, t * 128 : (t + 1) * 128] = pw[:, first : first + 128]
    extra_rows = jnp.concatenate([ext[...], jnp.zeros((EXTRA - 8, EXTRA), F32)], axis=0).astype(BF)
    extra_cols = dot(one_hot(32, EXTRA), extra_rows, NT).astype(BF)
    WS0[0, :, 512:] = extra_cols
    WS0[1, :, 512:] = extra_cols
    RT[y] = jnp.broadcast_to(rts[...].astype(F32), (8, 128))
    mine = pl.ds(pl.multiple_of(y * 128, 128), 128)
    XG[mine, :] = tok[...]
    CG[mine, :] = cot[...]

    def row(plane):
        return pl.ds(pl.multiple_of(g * 256 + plane * 128 + w * 32, 32), 32)

    for ch in range(3):
        W[ch][row(y), :] = WS[ch][y]
    row_o = pl.ds(pl.multiple_of(g * 128 + w * 32, 32), 32)
    WO[y, row_o, :] = wo_in[...]
    all_in()

    def z_rows(ch, plane):
        return sum(
            (go(cp.new(W[ch].at[row(plane), :], W[ch].at[row(plane), :], p.dev_z(k))) for k in (2, 1, 3)), ()
        )

    yw = [go(cp.new(WS[ch].at[1 - y], W[ch].at[row(y), :], p.dev_y)) for ch in range(3)]
    zw = [z_rows(0, y), (), ()]
    ty = go(cp.new(RT.at[y], RT.at[y], p.dev_y), cp.new(tok, XG.at[mine, :], p.dev_y))

    def dq(q):
        return pl.ds(pl.multiple_of(q * 256, 256), 256)

    half = pl.ds(pl.multiple_of(x * 512, 512), 512)
    other = pl.ds(pl.multiple_of((1 - x) * 512, 512), 512)

    def e_first(s):
        return (
            cp.new(up_in.at[s, :, other], UP.at[s, 0, dq(g), :], p.dev_x),
            cp.new(dn_in.at[s, other, :], DN.at[s, 0, :, dq(g)], p.dev_x),
        )

    def e_core0(s):
        return go(
            cp.new(up_in.at[s, :, half], UP.at[s, 0, dq(g), :], p.dev_c),
            cp.new(dn_in.at[s, half, :], DN.at[s, 0, :, dq(g)], p.dev_c),
        )

    def e_local(s):
        return go(
            here(up_in.at[s, :, half], UP.at[s, 0, dq(g), :]),
            here(dn_in.at[s, half, :], DN.at[s, 0, :, dq(g)]),
        )

    def e_z(s):
        return (
            cp.new(up_in.at[s, :, half], UP.at[s, 1, dq(g), :], p.dev_pair),
            cp.new(dn_in.at[s, half, :], DN.at[s, 1, :, dq(g)], p.dev_pair),
        )

    def e_relay(s):
        return go(
            cp.new(UP.at[s, 0, dq(p.gx), :], UP.at[s, 1, dq(p.gx), :], p.dev_pair),
            cp.new(DN.at[s, 0, :, dq(p.gx)], DN.at[s, 1, :, dq(p.gx)], p.dev_pair),
        )

    def e_core(s, q, which):
        return go(
            cp.new(UP.at[s, q, dq(which), :], UP.at[s, q, dq(which), :], p.dev_c),
            cp.new(DN.at[s, q, :, dq(which)], DN.at[s, q, :, dq(which)], p.dev_c),
        )

    e1 = [e_first(0), e_first(1)]
    go(*e1[0])
    wait(*yw[0])
    zw[0] += z_rows(0, 1 - y)
    for ch in (1, 2):
        wait(*yw[ch])
        zw[ch] = z_rows(ch, y) + z_rows(ch, 1 - y)
    zo = sum((go(cp.new(wo_in, WO.at[y, row_o, :], p.dev_z(k))) for k in (2, 1, 3)), ())
    el = e_local(0) + e_local(1)
    ec0 = [e_core0(0), e_core0(1)]

    wait(*ty)
    values = XG[...].astype(F32)
    centred = values - jnp.mean(values, axis=1, keepdims=True)
    inverse = lax.rsqrt(jnp.mean(centred * centred, axis=1, keepdims=True) + 1e-05)
    XH[...] = centred * inverse
    for b in (0, 1):
        DSP[b] = dispatch_block(RT[b], y)
        XS[b * CAP : (b + 1) * CAP, :] = dot(DSP[b], XG[b * 128 : (b + 1) * 128, :])

    def quarter(d):
        return pl.ds(pl.multiple_of(d * 128, 128), 128)

    def wo_copy(plane, d, device):
        return cp.new(WO.at[plane, quarter(d), :], WO.at[plane, quarter(d), :], device)

    def w_copy(ch, d, device):
        return cp.new(W[ch].at[dq(d), :], W[ch].at[dq(d), :], device)

    xw, fw = [None] * 3, [None] * 3
    for ch in range(3):
        wait(*zw[ch])
        xw[ch] = go(w_copy(ch, g, p.dev_x), w_copy(ch, g, p.dev_c))
    wait(*zo)
    yo = go(wo_copy(y, g, p.dev_y))
    ez = [go(*e_z(0)), e_z(1)]
    cy = go(cp.new(cot, CG.at[mine, :], p.dev_y))
    wait(*xw[0])
    fw[0] = go(w_copy(0, p.gx, p.dev_c))
    wait(*fw[0])
    extra = dot(one_hot(8, EXTRA), W0[:, 512:], NT)
    gain = extra[0:1, :]
    centroid = jnp.where(y == 0, extra[1:2, :], extra[2:3, :])
    NRM[...] = (XH[...] * gain).astype(BF)

    def project(ch):
        QKV[:, ch * 512 : (ch + 1) * 512] = dot(NRM[...], W[ch][:, :512]).astype(BF)

    project(0)
    wait(*xw[1])
    fw[1] = go(w_copy(1, p.gx, p.dev_c))
    wait(*fw[1])
    project(1)
    wait(*yo)
    xo = go(
        cp.new(WO.at[:, quarter(g), :], WO.at[:, quarter(g), :], p.dev_x),
        cp.new(WO.at[:, quarter(g), :], WO.at[:, quarter(g), :], p.dev_c),
    )
    go(*e1[1])
    wait(*e1[0])
    er = [e_relay(0)]
    ec = [e_core(0, 0, p.gx)]
    go(*ez[1])
    wait(*xw[2])
    fw[2] = go(w_copy(2, p.gx, p.dev_c))
    wait(*fw[2])
    project(2)

    place_q, seq_q = place_of(lengths, order, lax.broadcasted_iota(jnp.int32, (256, 256), 0))
    place_k, seq_k = place_of(lengths, order, lax.broadcasted_iota(jnp.int32, (256, 256), 1))
    allowed = (seq_q == seq_k) & (place_k <= place_q)
    low_half = lax.broadcasted_iota(jnp.int32, (256, 128), 1) < 64
    mixed_first = cp.block(4)

    def mixed_copy(t):
        cols = pl.ds(pl.multiple_of(t * 128, 128), 128)
        return cp.at(mixed_first + t, MXH.at[y, :, cols], MXH.at[y, :, cols], p.dev_y)

    def heads(t, carry):
        cols = pl.ds(pl.multiple_of(t * 128, 128), 128)
        q2 = QKV[:, cols]
        k2 = QKV[:, pl.ds(pl.multiple_of(512 + t * 128, 128), 128)]
        v2 = QKV[:, pl.ds(pl.multiple_of(1024 + t * 128, 128), 128)]
        parts = []
        for i in (0, 1):
            keep = low_half if i == 0 else ~low_half
            scores = dot(jnp.where(keep, q2, jnp.zeros_like(q2)), k2, NT) * 0.125
            scores = jnp.where(allowed, scores, -1000000000.0)
            exponent = jnp.exp(scores - jnp.max(scores, axis=1, keepdims=True))
            probs = exponent / jnp.sum(exponent, axis=1, keepdims=True)
            PR[2 * t + i] = probs
            parts.append(dot(probs.astype(BF), v2))
        MXH[y, :, cols] = jnp.where(low_half, parts[0], parts[1]).astype(BF)
        mixed_copy(t).start()
        return carry

    lax.fori_loop(0, 4, heads, 0)

    def mixed_pick(yy):
        for b in (0, 1):
            MS[yy, b * CAP : (b + 1) * CAP, :] = dot(DSP[b], MXH[yy, b * 128 : (b + 1) * 128, :]).astype(BF)

    mixed_pick(y)
    wait(*cy)
    for b in (0, 1):
        GS[b * CAP : (b + 1) * CAP, :] = dot(DSP[b], CG[b * 128 : (b + 1) * 128, :]).astype(BF)
    wait(*xo)
    co = go(cp.new(WO.at[:, quarter(p.gx), :], WO.at[:, quarter(p.gx), :], p.dev_c))
    wait(*co)
    AA[...] = XS[...] + dot(MS[y], WO[y])
    lax.fori_loop(0, 4, lambda t, carry: (mixed_copy(t).wait(), carry)[1], 0)
    mixed_pick(1 - y)
    AA[...] += dot(MS[1 - y], WO[1 - y])
    gate = jax.nn.sigmoid(jnp.sum(AA[...] * centroid, axis=1, keepdims=True))

    early = [
        here(src, dst)
        for src, dst in (
            (XG, xg_out), (QKV, qkv_out), (PR, pr_out), (MXH, mxh_out),
            (W0, w0_out), (W1, w1_out), (W2, w2_out), (WO, wo_out),
        )
    ]
    go(*early)

    wait(*el)
    at_me, at_x, at_z, at_d = p.team_places()

    def rows_of(place):
        return pl.ds(pl.multiple_of(place * 160, 32), 160)

    def part(i, place=0):
        return pl.ds(pl.multiple_of(place * 160 + i * 32, 32), 32)

    def each(fn):
        def body(i, carry):
            fn(i)
            return carry

        lax.fori_loop(0, 5, body, 0)

    class Spread:
        def __init__(self, R):
            self.R = R
            self.zi, self.xi, self.fi = cp.block(5), cp.block(5), cp.block(5)

        def same(self, first, i, place, device):
            view = self.R.at[part(i, place), :]
            return cp.at(first + i, view, view, device)

        def z(self, i):
            return self.same(self.zi, i, at_me, p.dev_z(2))

        def x(self, i):
            return self.same(self.xi, i, at_me, p.dev_x)

        def forward(self, i):
            return self.same(self.fi, i, at_z, p.dev_x)

        def start_part(self, i):
            self.z(i).start()
            self.x(i).start()

        def relay_part(self, i):
            self.z(i).wait()
            self.forward(i).start()

    class Reduce:
        def __init__(self, staging, landing):
            self.put, self.got = PS.at[staging], RB.at[landing]
            self.xi, self.di, self.zi = cp.block(1), cp.block(5), cp.block(5)

        def x(self):
            return cp.at(self.xi, self.put.at[0], self.got.at[0], p.dev_x)

        def d(self, i):
            return cp.at(self.di + i, self.put.at[1, part(i), :], self.got.at[1, part(i), :], p.dev_x)

        def z(self, i):
            return cp.at(self.zi + i, self.put.at[2, part(i), :], self.got.at[2, part(i), :], p.dev_z(2))

        def start_x(self):
            each(lambda i: self.d(i).start())
            self.x().start()

        def relay_part(self, i, own_z):
            self.d(i).wait()
            self.put[2, part(i), :] = (own_z[part(i), :] + self.got[1, part(i), :].astype(F32)).astype(BF)
            self.z(i).start()

        def result_part(self, i, own):
            self.z(i).wait()
            return (
                own[part(i), :]
                + self.got[0, part(i), :].astype(F32)
                + self.got[2, part(i), :].astype(F32)
            )

    g1, g2, g3, g4 = Spread(R1), Spread(R2), Spread(R3), Spread(R4)
    r1, r2, r3, r4 = Reduce(0, 0), Reduce(1, 1), Reduce(0, 2), Reduce(0, 3)
    mine_r = rows_of(at_me)

    R1[mine_r, :] = AA[...].astype(BF)
    each(lambda i: g1.z(i).start())
    each(lambda i: g1.x(i).start())
    R3[mine_r, :] = (gate * GS[...].astype(F32)).astype(BF)
    each(lambda i: g3.z(i).start())
    each(lambda i: g3.x(i).start())

    wait(*ec0[0])
    wait(*ec[0])
    wait(*ez[0])
    ec1 = e_core(0, 1, g)
    wait(*er[0])
    ec2 = e_core(0, 1, p.gx)
    wait(*ec1)
    wait(*ec2)

    def cols_of(q):
        return slice(q * 512, (q + 1) * 512)

    def first_forward(place):
        at = rows_of(place)
        total = None
        for q in (0, 1):
            active, slope = gelu_both(dot(R1[at, :], UP[0, q]))
            GP1[at, cols_of(q)] = slope
            A1[at, cols_of(q)] = active.astype(BF)
            term = dot(active.astype(BF), DN[0, q])
            total = term if total is None else total + term
        return total

    OWN[0] = first_forward(at_me)
    each(g1.relay_part)
    wait(*e1[1])
    er.append(e_relay(1))
    ec.append(e_core(1, 0, p.gx))
    each(lambda i: g1.x(i).wait())
    PS[0, 0] = first_forward(at_x).astype(BF)
    OWN[3] = first_forward(at_z)
    each(lambda i: g1.forward(i).wait())
    PS[0, 1] = first_forward(at_d).astype(BF)
    r1.start_x()
    each(lambda i: r1.relay_part(i, OWN.at[3]))
    r1.x().wait()

    def middle_part(i):
        branch = r1.result_part(i, OWN.at[0])
        SUMS[0, part(i), :] = branch
        R2[part(i, at_me), :] = (AA[part(i), :].astype(BF).astype(F32) + branch).astype(BF)
        g2.start_part(i)

    each(middle_part)
    each(g3.relay_part)

    wait(*ec0[1])
    wait(*ec[1])
    wait(*ez[1])
    ec1 = e_core(1, 1, g)
    wait(*er[1])
    ec2 = e_core(1, 1, p.gx)
    wait(*ec1)
    wait(*ec2)

    def second_grad(place):
        at = rows_of(place)
        total_grad = None
        for q in (0, 1):
            active, slope = gelu_both(dot(R2[at, :], UP[1, q]))
            A2[at, cols_of(q)] = active.astype(BF)
            grad = (slope * dot(R3[at, :], DN[1, q], NT)).astype(BF)
            DH[at, cols_of(q)] = grad
            term = dot(grad, UP[1, q], NT)
            total_grad = term if total_grad is None else total_grad + term
        return total_grad

    def second_forward(place):
        at = rows_of(place)
        return dot(A2[at, :512], DN[1, 0]) + dot(A2[at, 512:], DN[1, 1])

    OWN[2] = second_grad(at_me)
    OWN[1] = second_forward(at_me)
    each(g2.relay_part)
    each(lambda i: g2.x(i).wait())
    each(lambda i: g3.x(i).wait())
    PS[0, 0] = second_grad(at_x).astype(BF)
    OWN[3] = second_grad(at_z)
    each(lambda i: g2.forward(i).wait())
    each(lambda i: g3.forward(i).wait())
    PS[0, 1] = second_grad(at_d).astype(BF)
    r3.start_x()
    PS[1, 1] = second_forward(at_d).astype(BF)
    PS[1, 0] = second_forward(at_x).astype(BF)
    OWN[4] = second_forward(at_z)
    each(lambda i: r3.relay_part(i, OWN.at[3]))
    r2.start_x()

    def weight_grads(A, R, RG, GU, GD):
        def one(q, d):
            qcols = pl.ds(pl.multiple_of(q * 512, 512), 512)
            GU[q, d] = dot(R[:, dq(d)], DH[:, qcols], TN).astype(BF)
            GD[q, d] = dot(A[:, qcols], RG[:, dq(d)], TN).astype(BF)

        def body(t, carry):
            q, k = lax.rem(t, 2), lax.div(t, 2)
            d = lax.rem(k, 2)
            mine_c = lax.div(k, 2)
            cc = p.c * mine_c + (1 - p.c) * (1 - mine_c)
            one(q, 2 * d + cc)
            return carry

        return body

    def to_core(n):
        out = ()
        for k, theirs in enumerate((p.gc, p.gd)):
            out += go(
                cp.new(GU.at[:, theirs], CRU.at[n, :, k], p.dev_c),
                cp.new(GD.at[:, theirs], CRD.at[n, :, k], p.dev_c),
            )
        return out

    def add_core(n, own_u, own_d, far_u, far_d):
        for k, d in enumerate((g, p.gx)):
            far_u[k] = (GU[1, d].astype(F32) + CRU[n, 1, k].astype(F32)).astype(BF)
            far_d[k] = (GD[1, d].astype(F32) + CRD[n, 1, k].astype(F32)).astype(BF)
            own_u[k] = (GU[0, d].astype(F32) + CRU[n, 0, k].astype(F32)).astype(BF)
            own_d[k] = (GD[0, d].astype(F32) + CRD[n, 0, k].astype(F32)).astype(BF)

    body2 = weight_grads(A2, R2, R3, GU, GD)
    lax.fori_loop(0, 4, body2, 0)
    f0 = to_core(0)
    lax.fori_loop(4, 8, body2, 0)

    r3.x().wait()

    def middle_grad_part(i):
        total = r3.result_part(i, OWN.at[2])
        SUMS[1, part(i), :] = total
        R4[part(i, at_me), :] = (R3[part(i, at_me), :].astype(F32) + total).astype(BF)
        g4.start_part(i)

    each(middle_grad_part)
    wait(*f0)
    add_core(0, P2U, P2D, ZSU, ZSD)
    f1 = []
    for k in (0, 1):
        f1 += go(
            cp.new(ZSU.at[k], ZRU.at[k], p.dev_pair),
            cp.new(ZSD.at[k], ZRD.at[k], p.dev_pair),
        )

    each(lambda i: r2.relay_part(i, OWN.at[4]))
    r2.x().wait()

    def first_backward(place):
        at = rows_of(place)
        total = None
        for q in (0, 1):
            grad = (GP1[at, cols_of(q)] * dot(R4[at, :], DN[0, q], NT)).astype(BF)
            DH[at, cols_of(q)] = grad
            term = dot(grad, UP[0, q], NT)
            total = term if total is None else total + term
        return total

    OWN[0] = first_backward(at_me)
    each(g4.relay_part)
    each(lambda i: g4.x(i).wait())
    PS[0, 0] = first_backward(at_x).astype(BF)
    OWN[3] = first_backward(at_z)
    each(lambda i: g4.forward(i).wait())
    PS[0, 1] = first_backward(at_d).astype(BF)
    r4.start_x()

    def output_part(i):
        branch_two = r2.result_part(i, OWN.at[1])
        returned = (SUMS[0, part(i), :] + branch_two).astype(BF).astype(F32)
        upstream = GS[part(i), :].astype(F32)
        after = AA[part(i), :]
        gate_part = jax.nn.sigmoid(jnp.sum(after * centroid, axis=1, keepdims=True))
        OUTS[part(i), :] = (after + gate_part * returned).astype(BF)
        score_grad = jnp.sum(upstream * returned, axis=1, keepdims=True) * gate_part * (1.0 - gate_part)
        RES[part(i), :] = upstream + score_grad * centroid
        CGR[...] += jnp.broadcast_to(jnp.sum(score_grad * after, axis=0, keepdims=True), CGR.shape)

    CGR[...] = jnp.zeros_like(CGR)

    each(lambda i: r4.relay_part(i, OWN.at[3]))
    each(output_part)
    body1 = weight_grads(A1, R1, R4, GU, GD)
    lax.fori_loop(0, 4, body1, 0)
    f0 = to_core(1)
    lax.fori_loop(4, 8, body1, 0)
    r4.x().wait()

    def residual_part(i):
        arrived = (r4.result_part(i, OWN.at[0]) + SUMS[1, part(i), :]).astype(BF)
        RESS[part(i), :] = (RES[part(i), :] + arrived.astype(F32)).astype(BF)

    each(residual_part)
    wait(*f0)
    add_core(1, P1U, P1D, Z1U, Z1D)
    wait(*f1)
    for k in (0, 1):
        S2U[k] = P2U[k].astype(F32) + ZRU[k].astype(F32)
        S2D[k] = P2D[k].astype(F32) + ZRD[k].astype(F32)
    wait(*early)


def backward_kernel(
    xg_in, qkv_in, pr_in, mxh_in, w0_in, w1_in, w2_in, wo_in,
    RT, OUTS, RESS, CGR, P1U, P1D, Z1U, Z1D, S2U, S2D,
    out, tgrad, pgrad, ograd, egrad, ugrad, dgrad,
    XG, QKV, PR, MXH, W0, W1, W2, WO,
    RP, OP, RL, XH, NRM, NRMT, MG, DQ, DT, NG, NGS, NGR,
    ZRU, ZRD, XSU, XSD, XRU, XRD,
    PW0, PW1, PW2, PW3, PC0, PC1, PC2, PC3, PXS0, PXS1, PXS2, PXS3, PXR0, PXR1, PXR2, PXR3,
    PYS0, PYS1, PYS2, PYS3, PK0, PK1, PK2, PK3, PZ0, PZ1, PZ2, PZ3,
    OW, OC, OXS, OXR, OK, OZR, TE,
    send, recv, local,
):
    PW, PC, PXS, PXR = (PW0, PW1, PW2, PW3), (PC0, PC1, PC2, PC3), (PXS0, PXS1, PXS2, PXS3), (PXR0, PXR1, PXR2, PXR3)
    PYS, PK, PZ = (PYS0, PYS1, PYS2, PYS3), (PK0, PK1, PK2, PK3), (PZ0, PZ1, PZ2, PZ3)
    p = Place()
    g, y, w, x = p.g, p.y, p.w, p.x
    cp = Copies(send, recv)
    all_in = greet([p.dev_x, p.dev_c, p.dev_y, p.dev_z(1), p.dev_z(2), p.dev_z(3)])

    def go(*items):
        for item in items:
            item.start()
        return items

    def wait(*items):
        for item in items:
            item.wait()

    loads = [
        copy_in(src, dst, local.at[i])
        for i, (src, dst) in enumerate(
            (
                (xg_in, XG), (w0_in, W0), (wo_in, WO), (mxh_in, MXH),
                (qkv_in, QKV), (pr_in, PR), (w1_in, W1), (w2_in, W2),
            )
        )
    ]
    go(*loads)
    XSU[1] = S2U[1].astype(BF)
    XSD[1] = S2D[1].astype(BF)
    all_in()

    own_slots = pl.ds(pl.multiple_of(y * CAP, 16), CAP)
    peer_slots = pl.ds(pl.multiple_of((1 - y) * CAP, 16), CAP)
    ry = go(cp.new(RESS, RP, p.dev_y))
    oy = go(cp.new(OUTS.at[peer_slots, :], OP, p.dev_y))

    f1 = []
    for k in (1, 0):
        f1 += go(
            cp.new(Z1U.at[k], ZRU.at[k], p.dev_pair),
            cp.new(Z1D.at[k], ZRD.at[k], p.dev_pair),
        )
    f2 = {1: go(cp.new(XSU.at[1], XRU.at[1], p.dev_x), cp.new(XSD.at[1], XRD.at[1], p.dev_x))}

    half = pl.ds(pl.multiple_of(x * 512, 512), 512)
    other = pl.ds(pl.multiple_of((1 - x) * 512, 512), 512)

    wait(loads[0], loads[1])
    values = XG[...].astype(F32)
    centred = values - jnp.mean(values, axis=1, keepdims=True)
    inverse = lax.rsqrt(jnp.mean(centred * centred, axis=1, keepdims=True) + 1e-05)
    XH[...] = centred * inverse
    pick = one_hot(8, EXTRA)
    gain = dot(pick, W0[:, 512:], NT)[0:1, :]
    NRM[...] = (XH[...] * gain).astype(BF)
    NRMT[...] = NRM[...].T
    ugrad[1, :, half] = S2U[0]
    dgrad[1, half, :] = S2D[0]

    wait(*ry)
    for b in (0, 1):
        slots = slice(b * CAP, (b + 1) * CAP)
        RL[b * 128 : (b + 1) * 128, :] = (
            dot(dispatch_block(RT[b], y), RESS[slots, :], TN)
            + dot(dispatch_block(RT[b], 1 - y), RP[slots, :], TN)
        ).astype(BF)
    wait(loads[2])
    MG[...] = dot(RL[...], WO[y], NT).astype(BF)

    def rows4(d):
        return pl.ds(pl.multiple_of(d * 128, 128), 128)

    def dq(d):
        return pl.ds(pl.multiple_of(d * 256, 256), 256)

    def row32(v):
        return pl.ds(pl.multiple_of(v * 32, 32), 32)

    def out_rows(d):
        OW[rows4(d), :] = dot(MXH[y, :, rows4(d)], RL[...], TN).astype(BF)

    low_half = lax.broadcasted_iota(jnp.int32, (256, 128), 1) < 64

    def heads(t):
        c0 = slice(t * 128, (t + 1) * 128)
        c1 = slice(512 + t * 128, 512 + (t + 1) * 128)
        c2 = slice(1024 + t * 128, 1024 + (t + 1) * 128)
        q2, k2, v2, m2 = QKV[:, c0], QKV[:, c1], QKV[:, c2], MG[:, c0]
        parts = []
        for i in (0, 1):
            keep = low_half if i == 0 else ~low_half
            probs = PR[2 * t + i]
            probs_grad = dot(jnp.where(keep, m2, jnp.zeros_like(m2)), v2, NT)
            delta = jnp.sum(probs_grad * probs, axis=1, keepdims=True)
            scores_grad = (probs * (probs_grad - delta)).astype(BF)
            parts.append(
                (
                    dot(scores_grad, k2) * 0.125,
                    dot(scores_grad, q2, TN) * 0.125,
                    dot(probs.astype(BF), m2, TN),
                )
            )
        for s, c in enumerate((c0, c1, c2)):
            grad = jnp.where(low_half, parts[0][s], parts[1][s]).astype(BF)
            DQ[:, c] = grad
            DT[t, :, s * 128 : (s + 1) * 128] = grad

    pc, px, py, pz = [None] * 4, [None] * 4, [None] * 4, [None] * 4

    def to_core(t):
        PW[t][:, :384] = dot(NRMT[...], DT[t]).astype(BF)
        pc[t] = sum(
            (go(cp.new(PW[t].at[dq(d), :], PC[t].at[k], p.dev_c)) for k, d in enumerate((p.gc, p.gd))), ()
        )

    def to_x(t):
        wait(*pc[t])
        PXS[t][...] = (PW[t][dq(p.gx), :].astype(F32) + PC[t][1].astype(F32)).astype(BF)
        px[t] = go(cp.new(PXS[t], PXR[t], p.dev_x))

    def summed(t, plane):
        rows = rows4(plane)
        full = pl.ds(pl.multiple_of(g * 256 + plane * 128, 128), 128)
        total = PW[t][full, :].astype(F32) + PC[t][0, rows, :].astype(F32) + PXR[t][rows, :].astype(F32)
        return total.astype(BF)

    def to_y(t):
        wait(*px[t])
        PYS[t][...] = summed(t, 1 - y)
        py[t] = go(cp.new(PYS[t], PK[t].at[1], p.dev_y))
        PK[t][0] = summed(t, y)

    def to_z(t):
        wait(*py[t])
        pz[t] = sum(
            (
                go(cp.new(PK[t].at[:, row32(lax.rem(w + k, 4)), :], PZ[t].at[k - 1], p.dev_z(k)))
                for k in (2, 1, 3)
            ),
            (),
        )

    wait(loads[4], loads[5])
    heads(0)
    to_core(0)
    wait(loads[3])
    out_rows(p.gc)
    out_rows(p.gd)
    oc = sum((go(cp.new(OW.at[rows4(d), :], OC.at[k], p.dev_c)) for k, d in enumerate((p.gc, p.gd))), ())
    heads(1)
    to_core(1)
    to_x(0)
    out_rows(g)
    out_rows(p.gx)
    heads(2)
    to_core(2)
    to_x(1)
    wait(*oc)
    for k, d in enumerate((g, p.gx)):
        OK[k] = (OW[rows4(d), :].astype(F32) + OC[k].astype(F32)).astype(BF)
    oz = sum(
        (go(cp.new(OK.at[:, row32(lax.rem(w + k, 4)), :], OZR.at[k - 1], p.dev_z(k))) for k in (2, 1, 3)), ()
    )
    own32 = row32(w)
    heads(3)

    wait(loads[6], loads[7])
    NG[...] = (
        dot(DQ[:, :512], W0[:, :512], NT) + dot(DQ[:, 512:1024], W1[...], NT) + dot(DQ[:, 1024:], W2[...], NT)
    )
    NGS[...] = NG[rows4(1 - y), :].astype(BF)
    ny = go(cp.new(NGS, NGR, p.dev_y))
    gain_row = jnp.sum(NG[...] * XH[...], axis=0, keepdims=True)
    line = lax.broadcasted_iota(jnp.int32, (8, 1024), 0)
    stack = jnp.where(line == 0, gain_row, jnp.where(line == 1 + y, CGR[0:1, :], 0.0)).astype(BF)
    PW3[:, 384:] = dot(stack, pick, TN).astype(BF)
    to_core(3)
    to_x(2)
    to_y(0)
    to_x(3)
    to_y(1)
    to_z(0)

    wait(*oz)

    def out_sum(k):
        return (
            OK[k, own32, :].astype(F32)
            + OZR[0, k].astype(F32)
            + OZR[1, k].astype(F32)
            + OZR[2, k].astype(F32)
        )

    OXS[...] = out_sum(1).astype(BF)
    ox = go(cp.new(OXS, OXR, p.dev_x))

    wait(*ny)
    own_rows = rows4(y)
    normed = XH[own_rows, :]
    mine = XG[own_rows, :].astype(F32)
    mine = mine - jnp.mean(mine, axis=1, keepdims=True)
    inverse = lax.rsqrt(jnp.mean(mine * mine, axis=1, keepdims=True) + 1e-05)
    scaled = (NG[own_rows, :] + NGR[...].astype(F32)) * gain
    tgrad[...] = RL[own_rows, :].astype(F32) + inverse * (
        scaled
        - jnp.mean(scaled, axis=1, keepdims=True)
        - normed * jnp.mean(scaled * normed, axis=1, keepdims=True)
    )
    to_y(2)
    to_z(1)

    wait(*f1)
    XSU[0] = (P1U[1].astype(F32) + ZRU[1].astype(F32)).astype(BF)
    XSD[0] = (P1D[1].astype(F32) + ZRD[1].astype(F32)).astype(BF)
    f2[0] = go(cp.new(XSU.at[0], XRU.at[0], p.dev_x), cp.new(XSD.at[0], XRD.at[0], p.dev_x))
    wait(*oy)
    route_own = RT[y]
    out[...] = (
        dot(dispatch_block(route_own, y), OUTS[own_slots, :], TN)
        + dot(dispatch_block(route_own, 1 - y), OP[...], TN)
    ).astype(BF)
    to_y(3)
    to_z(2)
    ugrad[0, :, half] = P1U[0].astype(F32) + ZRU[0].astype(F32)
    dgrad[0, half, :] = P1D[0].astype(F32) + ZRD[0].astype(F32)
    wait(*f2[1])
    ugrad[1, :, other] = XRU[1].astype(F32)
    dgrad[1, other, :] = XRD[1].astype(F32)
    to_z(3)

    for t in range(4):
        wait(*pz[t])
        sums = [
            PK[t][i, own32, :].astype(F32)
            + PZ[t][0, i].astype(F32)
            + PZ[t][1, i].astype(F32)
            + PZ[t][2, i].astype(F32)
            for i in (0, 1)
        ]
        for plane in (0, 1):
            kept = jnp.where(y == plane, sums[0], sums[1])
            for s in range(3):
                first = s * 1024 + t * 256 + plane * 128
                pgrad[:, first : first + 128] = kept[:, s * 128 : (s + 1) * 128]
        if t == 3:
            TE[0:32, :] = sums[0][:, 384:] + sums[1][:, 384:]
    egrad[...] = TE[...].T[0:8, :]
    wait(*f2[0])
    ugrad[0, :, other] = XRU[0].astype(F32)
    dgrad[0, other, :] = XRD[0].astype(F32)
    wait(*ox)
    ograd[...] = out_sum(0) + OXR[...].astype(F32)


def finish_kernel(
    out, tgrad, pgrad, ograd, egrad, ugrad, dgrad, out2, tgrad2, gain, pgrad2, ograd2, cent, ugrad2, dgrad2
):
    out2[0] = out[...]
    tgrad2[0] = tgrad[...]
    pgrad2[...] = pgrad[...]
    ograd2[...] = ograd[...]
    gain[...] = egrad[0:1, :32]
    cent[...] = egrad[1:3, :32]
    ugrad2[0] = ugrad[...]
    dgrad2[0] = dgrad[...]


def vmem(shape, dtype=BF):
    return pltpu.VMEM(shape, dtype)


def fast_shards(
    tokens, cotangent, norm_gain, project_weight, output_weight, centroids,
    expert_up, expert_down, sequence_lengths, block_order, routes,
):
    in_vmem = pl.BlockSpec(memory_space=pltpu.VMEM)
    in_any = pl.BlockSpec(memory_space=pl.ANY)
    in_smem = pl.BlockSpec(memory_space=pltpu.SMEM)
    shape = jax.ShapeDtypeStruct
    ext = jnp.pad(
        jnp.concatenate([norm_gain[None], centroids], axis=0).astype(F32), ((0, 5), (0, EXTRA - 32))
    )
    mid_shapes = [
        ((256, 1024), BF),
        ((256, 1536), BF),
        ((8, 256, 256), F32),
        ((2, 256, 512), BF),
        ((1024, 512 + EXTRA), BF),
        ((1024, 512), BF),
        ((1024, 512), BF),
        ((2, 512, 1024), BF),
        ((2, 8, 128), F32),
        ((160, 1024), BF),
        ((160, 1024), BF),
        ((8, 1024), F32),
        ((2, 256, 512), BF),
        ((2, 512, 256), BF),
        ((2, 256, 512), BF),
        ((2, 512, 256), BF),
        ((2, 256, 512), F32),
        ((2, 512, 256), F32),
    ]
    mid = pl.pallas_call(
        forward_kernel,
        name="forward",
        out_shape=[shape(*s) for s in mid_shapes],
        in_specs=[in_smem] * 2 + [in_vmem] * 6 + [in_any] * 2,
        out_specs=[in_any] * 8 + [in_vmem] * (len(mid_shapes) - 8),
        scratch_shapes=[vmem(*s) for s in mid_shapes[:8]]
        + [
            vmem((2, 32, 512 + EXTRA)),
            vmem((2, 32, 512)),
            vmem((2, 32, 512)),
            vmem((256, 1024)),
            vmem((256, 1024), F32),
            vmem((256, 1024)),
            vmem((2, 2, 1024, 512)),
            vmem((2, 2, 512, 1024)),
            vmem((2, CAP, 128)),
            vmem((160, 1024), F32),
            vmem((160, 1024)),
            vmem((2, 160, 512)),
            vmem((160, 1024), F32),
        ]
        + [vmem((640, 1024))] * 4
        + [
            vmem((4, 3, 160, 1024)),
            vmem((2, 3, 160, 1024)),
            vmem((5, 160, 1024), F32),
            vmem((160, 1024), F32),
            vmem((640, 1024), F32),
            vmem((640, 1024)),
            vmem((640, 1024)),
            vmem((640, 1024)),
            vmem((2, 160, 1024), F32),
            vmem((2, 4, 256, 512)),
            vmem((2, 4, 512, 256)),
            vmem((2, 2, 2, 256, 512)),
            vmem((2, 2, 2, 512, 256)),
            vmem((2, 256, 512)),
            vmem((2, 512, 256)),
            vmem((2, 256, 512)),
            vmem((2, 512, 256)),
            vmem((2, 256, 512)),
            vmem((2, 512, 256)),
            pltpu.SemaphoreType.DMA((208,)),
            pltpu.SemaphoreType.DMA((208,)),
            pltpu.SemaphoreType.DMA((24,)),
        ],
        compiler_params=pltpu.CompilerParams(
            collective_id=0, has_side_effects=True, vmem_limit_bytes=VMEM_LIMIT
        ),
    )(
        sequence_lengths[0], block_order[0], tokens[0], cotangent[0], routes.reshape(1, 128),
        project_weight, output_weight, ext, expert_up[0], expert_down[0],
    )
    out_shapes = [
        ((128, 1024), BF),
        ((128, 1024), F32),
        ((32, 3072), F32),
        ((32, 1024), F32),
        ((8, EXTRA), F32),
        ((2, 256, 1024), F32),
        ((2, 1024, 256), F32),
    ]
    out, tgrad, pgrad, ograd, egrad, ugrad, dgrad = pl.pallas_call(
        backward_kernel,
        name="backward",
        out_shape=[shape(*s) for s in out_shapes],
        in_specs=[in_any] * 8 + [in_vmem] * (len(mid_shapes) - 8),
        out_specs=[in_vmem] * len(out_shapes),
        scratch_shapes=[vmem(*s) for s in mid_shapes[:8]]
        + [
            vmem((160, 1024)),
            vmem((CAP, 1024)),
            vmem((256, 1024)),
            vmem((256, 1024), F32),
            vmem((256, 1024)),
            vmem((1024, 256)),
            vmem((256, 512)),
            vmem((256, 1536)),
            vmem((4, 256, 384)),
            vmem((256, 1024), F32),
            vmem((128, 1024)),
            vmem((128, 1024)),
            vmem((2, 256, 512)),
            vmem((2, 512, 256)),
            vmem((2, 256, 512)),
            vmem((2, 512, 256)),
            vmem((2, 256, 512)),
            vmem((2, 512, 256)),
        ]
        + [vmem((1024, c)) for c in CHUNKS]
        + [vmem((2, 256, c)) for c in CHUNKS]
        + [vmem((256, c)) for c in CHUNKS]
        + [vmem((256, c)) for c in CHUNKS]
        + [vmem((128, c)) for c in CHUNKS]
        + [vmem((2, 128, c)) for c in CHUNKS]
        + [vmem((3, 2, 32, c)) for c in CHUNKS]
        + [
            vmem((512, 1024)),
            vmem((2, 128, 1024)),
            vmem((32, 1024)),
            vmem((32, 1024)),
            vmem((2, 128, 1024)),
            vmem((3, 2, 32, 1024)),
            vmem((EXTRA, EXTRA), F32),
            pltpu.SemaphoreType.DMA((64,)),
            pltpu.SemaphoreType.DMA((64,)),
            pltpu.SemaphoreType.DMA((8,)),
        ],
        compiler_params=pltpu.CompilerParams(
            collective_id=1, has_side_effects=True, vmem_limit_bytes=VMEM_LIMIT
        ),
    )(*mid)
    out, tgrad, gain, pgrad, ograd, cent, ugrad, dgrad = pl.pallas_call(
        finish_kernel,
        name="finish",
        out_shape=[
            shape((1, 128, 1024), BF),
            shape((1, 128, 1024), F32),
            shape((1, 32), F32),
            shape((32, 3072), F32),
            shape((32, 1024), F32),
            shape((2, 32), F32),
            shape((1, 2, 256, 1024), F32),
            shape((1, 2, 1024, 256), F32),
        ],
        in_specs=[in_vmem] * 7,
        out_specs=[in_vmem] * 8,
        compiler_params=pltpu.CompilerParams(vmem_limit_bytes=VMEM_LIMIT),
    )(out, tgrad, pgrad, ograd, egrad, ugrad, dgrad)
    return out, tgrad, gain[0], pgrad, ograd, cent, ugrad, dgrad


def solution(mesh):
    sizes = dict(mesh.shape)
    fast = sizes == {"grp": 4, "ctx": 2, "wsh": 4}
    return jax.shard_map(
        fast_shards if fast else shards,
        mesh=mesh,
        in_specs=IN_SPECS,
        out_specs=OUT_SPECS,
        check_vma=False,
    )
```

```python
import math

import jax
import jax.numpy as jnp
from jax import lax
from jax.experimental import pallas as pl
from jax.experimental.pallas import tpu as pltpu
from jax.sharding import PartitionSpec as P

HEADS = 16
HDIM = 64
BLK = 128


precise = lax.Precision.HIGHEST


def place_rows(order_row, lengths_row, total_rows):
    row_index = jnp.arange(total_rows, dtype=jnp.int32)
    picked = (row_index // BLK)[:, None] == jnp.arange(order_row.shape[0], dtype=jnp.int32)[None, :]
    blocks = jnp.sum(jnp.where(picked, order_row[None, :], 0), axis=1)
    token_place = blocks * BLK + row_index % BLK
    bounds = jnp.cumsum(lengths_row)
    sequence = jnp.sum((token_place[:, None] >= bounds[None, :]).astype(jnp.int32), axis=1)
    return (token_place, sequence)


def normalize(values):
    average = jnp.mean(values, axis=-1, keepdims=True)
    centred = values - average
    inverse = lax.rsqrt(jnp.mean(centred * centred, axis=-1, keepdims=True) + 1e-05)
    return (centred * inverse, inverse)


def head_slice(matrix, section, offset, heads_per):
    width_part = heads_per * HDIM
    first_col = offset + section * width_part
    return matrix[:, first_col : first_col + width_part].reshape(matrix.shape[0], heads_per, HDIM)


def spread_rows(local_rows):
    return lax.all_gather(local_rows, "wsh", axis=0, tiled=True)


def collect_rows(partial_term):
    return lax.psum_scatter(
        partial_term.astype(jnp.bfloat16), "wsh", scatter_dimension=0, tiled=True
    ).astype(jnp.float32)


def trade_rows(slots_rows, peer_count, capacity):
    shaped = slots_rows.reshape(peer_count, capacity, slots_rows.shape[-1])
    moved = lax.all_to_all(shaped, "ctx", split_axis=0, concat_axis=0, tiled=True)
    return moved.reshape(peer_count * capacity, slots_rows.shape[-1])


def gelu_pullback(hidden, incoming):
    value_out, pullback = jax.vjp(jax.nn.gelu, hidden)
    return pullback(incoming)[0]


def shards(
    tokens,
    cotangent,
    norm_gain,
    project_weight,
    output_weight,
    centroids,
    expert_up,
    expert_down,
    sequence_lengths,
    block_order,
    routes,
):
    local_rows = tokens.shape[1]
    model_width = tokens.shape[2]
    peer_count = lax.axis_size("ctx")
    position = lax.axis_index("ctx")
    total_rows = local_rows * peer_count
    capacity = max(2, (5 * local_rows + 4 * peer_count - 1) // (4 * peer_count))
    slot_count = peer_count * capacity
    score_scale = 1.0 / math.sqrt(HDIM)
    heads_per = 4
    sections = HEADS // heads_per
    inputs_f = tokens[0].astype(jnp.float32)
    upstream = cotangent[0].astype(jnp.float32)
    project_full, output_full, gain_full, centroid_full = (
        lax.all_gather(project_weight, ("grp", "ctx", "wsh"), axis=0, tiled=True),
        lax.all_gather(output_weight, ("grp", "ctx", "wsh"), axis=0, tiled=True),
        lax.all_gather(norm_gain, ("grp", "ctx", "wsh"), axis=0, tiled=True),
        lax.all_gather(centroids, ("grp", "ctx", "wsh"), axis=1, tiled=True),
    )
    up_full, down_full = (
        lax.all_gather(expert_up, "grp", axis=2, tiled=True),
        lax.all_gather(expert_down, "grp", axis=3, tiled=True),
    )
    place_all, sequence_all = place_rows(block_order[0], sequence_lengths[0], total_rows)
    place_own = lax.dynamic_slice_in_dim(place_all, position * local_rows, local_rows)
    sequence_own = lax.dynamic_slice_in_dim(sequence_all, position * local_rows, local_rows)
    allowed = (sequence_own[:, None] == sequence_all[None, :]) & (
        place_all[None, :] <= place_own[:, None]
    )
    normed, inverse = normalize(inputs_f)
    gain_values = gain_full.astype(jnp.float32)
    normed_low = (normed * gain_values).astype(jnp.bfloat16)
    projected = jnp.dot(normed_low, project_full, preferred_element_type=jnp.float32)
    queries = projected[:, :model_width].astype(jnp.bfloat16)
    keyvalue = projected[:, model_width:].astype(jnp.bfloat16)
    keyvalue_all = lax.all_gather(keyvalue, "ctx", axis=0, tiled=True)
    mixed_parts = []
    logsum_parts = []
    for section in range(sections):
        head_query = head_slice(queries, section, 0, heads_per)
        head_key = head_slice(keyvalue_all, section, 0, heads_per)
        head_value = head_slice(keyvalue_all, section, model_width, heads_per)
        scores = (
            jnp.einsum("tgd,sgd->gts", head_query, head_key, preferred_element_type=jnp.float32)
            * score_scale
        )
        scores = jnp.where(allowed[None], scores, -1000000000.0)
        largest = jnp.max(scores, axis=-1, keepdims=True)
        exponent = jnp.exp(scores - largest)
        totals = jnp.sum(exponent, axis=-1, keepdims=True)
        weights = (exponent / totals).astype(jnp.bfloat16)
        mixed_part = jnp.einsum(
            "gts,sgd->tgd", weights, head_value, preferred_element_type=jnp.float32
        )
        mixed_parts.append(mixed_part.reshape(local_rows, heads_per * HDIM))
        logsum_parts.append((largest + jnp.log(totals))[:, :, 0])
    mixed_all = jnp.concatenate(mixed_parts, axis=1).astype(jnp.bfloat16)
    logsum = jnp.concatenate(logsum_parts, axis=0)
    after_attention = inputs_f + jnp.dot(mixed_all, output_full, preferred_element_type=jnp.float32)
    route_ids = routes[0, :, 0]
    member = route_ids[:, None] == jnp.arange(peer_count, dtype=jnp.int32)[None, :]
    member_f = member.astype(jnp.float32)
    picked_centroid = jnp.dot(member_f, centroid_full.astype(jnp.float32), precision=precise)
    gate_value = jax.nn.sigmoid(jnp.sum(after_attention * picked_centroid, axis=-1))
    member_int = member.astype(jnp.int32)
    ranking = jnp.sum((jnp.cumsum(member_int, axis=0) - 1) * member_int, axis=1)
    slot_index = route_ids * capacity + ranking
    dispatch = (slot_index[None, :] == jnp.arange(slot_count, dtype=jnp.int32)[:, None]).astype(
        jnp.bfloat16
    )
    sent_rows = jnp.dot(
        dispatch, after_attention.astype(jnp.bfloat16), preferred_element_type=jnp.float32
    ).astype(jnp.bfloat16)
    arrived = trade_rows(sent_rows, peer_count, capacity)
    up_first = up_full[0, 0]
    up_second = up_full[0, 1]
    down_first = down_full[0, 0]
    down_second = down_full[0, 1]
    gathered_one = spread_rows(arrived)
    hidden_one = jnp.dot(gathered_one, up_first, preferred_element_type=jnp.float32)
    active_one = jax.nn.gelu(hidden_one).astype(jnp.bfloat16)
    branch_one = collect_rows(jnp.dot(active_one, down_first, preferred_element_type=jnp.float32))
    middle = (arrived.astype(jnp.float32) + branch_one).astype(jnp.bfloat16)
    gathered_two = spread_rows(middle)
    hidden_two = jnp.dot(gathered_two, up_second, preferred_element_type=jnp.float32)
    active_two = jax.nn.gelu(hidden_two).astype(jnp.bfloat16)
    branch_two = collect_rows(jnp.dot(active_two, down_second, preferred_element_type=jnp.float32))
    expert_out = (branch_one + branch_two).astype(jnp.bfloat16)
    returned = trade_rows(expert_out, peer_count, capacity)
    returned_tok = jnp.einsum("st,sd->td", dispatch, returned, preferred_element_type=jnp.float32)
    output = after_attention + gate_value[:, None] * returned_tok
    gate_grad = jnp.sum(upstream * returned_tok, axis=-1)
    score_grad = gate_grad * gate_value * (1.0 - gate_value)
    centroid_term = jnp.dot(member_f.T, score_grad[:, None] * after_attention, precision=precise)
    branch_grad = (gate_value[:, None] * upstream).astype(jnp.bfloat16)
    branch_sent = jnp.dot(dispatch, branch_grad, preferred_element_type=jnp.float32).astype(
        jnp.bfloat16
    )
    branch_arrived = trade_rows(branch_sent, peer_count, capacity)
    grad_two = spread_rows(branch_arrived)
    hidden_two_grad = gelu_pullback(
        hidden_two, jnp.dot(grad_two, down_second.T, preferred_element_type=jnp.float32)
    ).astype(jnp.bfloat16)
    down_second_grad = jnp.dot(active_two.T, grad_two, preferred_element_type=jnp.float32)
    up_second_grad = jnp.dot(gathered_two.T, hidden_two_grad, preferred_element_type=jnp.float32)
    middle_grad = collect_rows(
        jnp.dot(hidden_two_grad, up_second.T, preferred_element_type=jnp.float32)
    )
    first_branch_grad = (branch_arrived.astype(jnp.float32) + middle_grad).astype(jnp.bfloat16)
    grad_one = spread_rows(first_branch_grad)
    hidden_one_grad = gelu_pullback(
        hidden_one, jnp.dot(grad_one, down_first.T, preferred_element_type=jnp.float32)
    ).astype(jnp.bfloat16)
    down_first_grad = jnp.dot(active_one.T, grad_one, preferred_element_type=jnp.float32)
    up_first_grad = jnp.dot(gathered_one.T, hidden_one_grad, preferred_element_type=jnp.float32)
    arrived_grad = (
        collect_rows(jnp.dot(hidden_one_grad, up_first.T, preferred_element_type=jnp.float32))
        + middle_grad
    ).astype(jnp.bfloat16)
    home_grad = trade_rows(arrived_grad, peer_count, capacity)
    home_grad_tok = jnp.einsum("st,sd->td", dispatch, home_grad, preferred_element_type=jnp.float32)
    up_terms = jnp.stack([up_first_grad, up_second_grad])[None]
    down_terms = jnp.stack([down_first_grad, down_second_grad])[None]
    up_grad_out, down_grad_out = (
        lax.psum_scatter(
            up_terms.astype(jnp.bfloat16), "grp", scatter_dimension=2, tiled=True
        ).astype(jnp.float32),
        lax.psum_scatter(
            down_terms.astype(jnp.bfloat16), "grp", scatter_dimension=3, tiled=True
        ).astype(jnp.float32),
    )
    residual_grad = upstream + score_grad[:, None] * picked_centroid + home_grad_tok
    residual_low = residual_grad.astype(jnp.bfloat16)
    output_term = jnp.dot(mixed_all.T, residual_low, preferred_element_type=jnp.float32)
    mixed_grad = jnp.dot(residual_low, output_full.T, preferred_element_type=jnp.float32).astype(
        jnp.bfloat16
    )
    query_grads = []
    key_grads = []
    value_grads = []
    delta_parts = []
    for section in range(sections):
        head_query = head_slice(queries, section, 0, heads_per)
        head_key = head_slice(keyvalue_all, section, 0, heads_per)
        head_value = head_slice(keyvalue_all, section, model_width, heads_per)
        head_grad = head_slice(mixed_grad, section, 0, heads_per)
        scores = (
            jnp.einsum("tgd,sgd->gts", head_query, head_key, preferred_element_type=jnp.float32)
            * score_scale
        )
        scores = jnp.where(allowed[None], scores, -1000000000.0)
        probs = jnp.exp(
            scores - logsum[section * heads_per : (section + 1) * heads_per][:, :, None]
        )
        probs_grad = jnp.einsum(
            "tgd,sgd->gts", head_grad, head_value, preferred_element_type=jnp.float32
        )
        row_delta = jnp.sum(probs_grad * probs, axis=-1)
        scores_grad = (probs * (probs_grad - row_delta[:, :, None])).astype(jnp.bfloat16)
        query_part = (
            jnp.einsum("gts,sgd->tgd", scores_grad, head_key, preferred_element_type=jnp.float32)
            * score_scale
        )
        query_grads.append(query_part.reshape(local_rows, heads_per * HDIM))
        delta_parts.append(row_delta)
        key_part = (
            jnp.einsum("gts,tgd->sgd", scores_grad, head_query, preferred_element_type=jnp.float32)
            * score_scale
        )
        value_part = jnp.einsum(
            "gts,tgd->sgd",
            probs.astype(jnp.bfloat16),
            head_grad,
            preferred_element_type=jnp.float32,
        )
        key_grads.append(key_part.reshape(total_rows, heads_per * HDIM))
        value_grads.append(value_part.reshape(total_rows, heads_per * HDIM))
    query_grad = jnp.concatenate(query_grads, axis=1).astype(jnp.bfloat16)
    keyvalue_terms = jnp.concatenate(key_grads + value_grads, axis=1)
    keyvalue_grad = lax.psum_scatter(
        keyvalue_terms.astype(jnp.bfloat16), "ctx", scatter_dimension=0, tiled=True
    )
    projected_grad = jnp.concatenate([query_grad, keyvalue_grad], axis=1)
    project_term = jnp.dot(normed_low.T, projected_grad, preferred_element_type=jnp.float32)
    normed_grad = jnp.dot(projected_grad, project_full.T, preferred_element_type=jnp.float32)
    gain_term = jnp.sum(normed_grad * normed, axis=0)
    scaled_grad = normed_grad * gain_values
    input_grad = residual_grad + inverse * (
        scaled_grad
        - jnp.mean(scaled_grad, axis=-1, keepdims=True)
        - normed * jnp.mean(scaled_grad * normed, axis=-1, keepdims=True)
    )
    project_grad, output_grad, gain_grad, centroid_grad = (
        lax.psum_scatter(project_term, ("grp", "ctx", "wsh"), scatter_dimension=0, tiled=True),
        lax.psum_scatter(output_term, ("grp", "ctx", "wsh"), scatter_dimension=0, tiled=True),
        lax.psum_scatter(gain_term, ("grp", "ctx", "wsh"), scatter_dimension=0, tiled=True),
        lax.psum_scatter(centroid_term, ("grp", "ctx", "wsh"), scatter_dimension=1, tiled=True),
    )
    return (
        output.astype(jnp.bfloat16)[None],
        input_grad[None],
        gain_grad,
        project_grad,
        output_grad,
        centroid_grad,
        up_grad_out,
        down_grad_out,
    )


VMEM_LIMIT = 61 * 2**20
CHUNKS = (384, 384, 384, 512)

IN_SPECS = (
    P(("grp", "wsh"), "ctx", None),
    P(("grp", "wsh"), "ctx", None),
    P(("grp", "ctx", "wsh")),
    P(("grp", "ctx", "wsh"), None),
    P(("grp", "ctx", "wsh"), None),
    P(None, ("grp", "ctx", "wsh")),
    P("ctx", None, "grp", "wsh"),
    P("ctx", None, "wsh", "grp"),
    P(("grp", "wsh"), None),
    P(("grp", "wsh"), None),
    P(("grp", "wsh"), "ctx", None),
)
OUT_SPECS = (
    P(("grp", "wsh"), "ctx", None),
    P(("grp", "wsh"), "ctx", None),
    P(("grp", "ctx", "wsh")),
    P(("grp", "ctx", "wsh"), None),
    P(("grp", "ctx", "wsh"), None),
    P(None, ("grp", "ctx", "wsh")),
    P("ctx", None, "grp", "wsh"),
    P("ctx", None, "wsh", "grp"),
)

BF = jnp.bfloat16
F32 = jnp.float32
NN = ((1,), (0,))
NT = ((1,), (1,))
TN = ((0,), (0,))
MESH = pl.DeviceIdType.MESH
GELU_C = 0.7978845608028654
EXTRA = 128
CAP = 80


def dot(a, b, dims=NN):
    return lax.dot_general(a, b, (dims, ((), ())), preferred_element_type=F32)


def gelu_both(h):
    sq = h * h
    t = jnp.tanh(GELU_C * h * (1.0 + 0.044715 * sq))
    half = 0.5 * (1.0 + t)
    slope = half + 0.5 * h * (1.0 - t * t) * (GELU_C * (1.0 + 3.0 * 0.044715 * sq))
    return h * half, slope


def copy_in(src, dst, sem):
    return pltpu.make_async_copy(src, dst, sem)


class Copies:
    def __init__(self, send, recv):
        self.send, self.recv, self.used = send, recv, 0

    def block(self, count):
        first = self.used
        self.used += count
        return first

    def at(self, index, src, dst, device):
        return pltpu.make_async_remote_copy(
            src_ref=src,
            dst_ref=dst,
            send_sem=self.send.at[index],
            recv_sem=self.recv.at[index],
            device_id=device,
            device_id_type=MESH,
        )

    def new(self, src, dst, device):
        return self.at(self.block(1), src, dst, device)


class Place:
    def __init__(self):
        g, y, w = lax.axis_index("grp"), lax.axis_index("ctx"), lax.axis_index("wsh")
        self.g, self.y, self.w = g, y, w
        self.x = lax.div(g, 2)
        self.c = g - 2 * self.x
        self.gx = 2 * (1 - self.x) + self.c
        self.gc = 2 * self.x + 1 - self.c
        self.gd = 2 * (1 - self.x) + 1 - self.c
        self.wb = lax.rem(w, 2)
        self.w1 = w + 1 - 2 * self.wb
        self.w2 = lax.rem(w + 2, 4)
        self.dev_x = (self.gx, y, w)
        self.dev_c = (self.gc, y, w)
        self.dev_y = (g, 1 - y, w)
        self.dev_pair = (g, y, self.w1)
        self.dev_z = lambda k: (g, y, lax.rem(w + k, 4))

    def team_places(self):
        mine = 2 * self.x + lax.div(self.w, 2)
        x_side = 2 * (1 - self.x) + lax.div(self.w, 2)
        flip = 1 - 2 * lax.div(self.w, 2)
        return mine, x_side, mine + flip, x_side + flip


def greet(devices):
    barrier = pltpu.get_barrier_semaphore()
    for device in devices:
        pl.semaphore_signal(barrier, inc=1, device_id=device, device_id_type=MESH)
    return lambda: pl.semaphore_wait(barrier, len(devices))


def one_hot(rows, columns):
    same = lax.broadcasted_iota(jnp.int32, (rows, columns), 0) == lax.broadcasted_iota(
        jnp.int32, (rows, columns), 1
    )
    return same.astype(F32).astype(BF)


def dispatch_block(route_rows, expert):
    member = (route_rows == expert.astype(F32)).astype(F32)
    earlier = lax.broadcasted_iota(jnp.int32, (128, 128), 0) < lax.broadcasted_iota(jnp.int32, (128, 128), 1)
    rank = dot(member.astype(BF), earlier.astype(F32).astype(BF))
    slot = lax.broadcasted_iota(jnp.int32, (CAP, 128), 0).astype(F32)
    hit = (jnp.broadcast_to(rank[0:1, :], (CAP, 128)) == slot) & (
        jnp.broadcast_to(member[0:1, :], (CAP, 128)) > 0.5
    )
    return hit.astype(F32).astype(BF)


def place_of(lengths, order, index):
    place = jnp.where(index < 128, order[0], order[1]) * 128 + lax.rem(index, 128)
    bound = lengths[0]
    sequence = jnp.where(place >= bound, 1, 0)
    for part in (1, 2):
        bound = bound + lengths[part]
        sequence = sequence + jnp.where(place >= bound, 1, 0)
    return place, sequence


def forward_kernel(
    lengths, order, tok, cot, rts, pw, wo_in, ext, up_in, dn_in,
    xg_out, qkv_out, pr_out, mxh_out, w0_out, w1_out, w2_out, wo_out,
    RT, OUTS, RESS, CGR, P1U, P1D, Z1U, Z1D, S2U, S2D,
    XG, QKV, PR, MXH, W0, W1, W2, WO,
    WS0, WS1, WS2, CG, XH, NRM, UP, DN, DSP, XS, GS, MS, AA,
    R1, R2, R3, R4, RB, PS, OWN, RES, GP1, A1, A2, DH, SUMS,
    GU, GD, CRU, CRD, P2U, P2D, ZSU, ZSD, ZRU, ZRD,
    send, recv, local,
):
    p = Place()
    g, y, w, x = p.g, p.y, p.w, p.x
    cp = Copies(send, recv)
    all_in = greet([p.dev_x, p.dev_c, p.dev_y, p.dev_z(1), p.dev_z(2), p.dev_z(3)])
    nlocal = [0]

    def here(src, dst):
        nlocal[0] += 1
        return copy_in(src, dst, local.at[nlocal[0] - 1])

    def go(*items):
        for item in items:
            item.start()
        return items

    def wait(*items):
        for item in items:
            item.wait()

    W, WS = (W0, W1, W2), (WS0, WS1, WS2)
    for ch in range(3):
        for t in range(4):
            for plane in (0, 1):
                first = ch * 1024 + t * 256 + plane * 128
                WS[ch][plane, :, t * 128 : (t + 1) * 128] = pw[:, first : first + 128]
    extra_rows = jnp.concatenate([ext[...], jnp.zeros((EXTRA - 8, EXTRA), F32)], axis=0).astype(BF)
    extra_cols = dot(one_hot(32, EXTRA), extra_rows, NT).astype(BF)
    WS0[0, :, 512:] = extra_cols
    WS0[1, :, 512:] = extra_cols
    RT[y] = jnp.broadcast_to(rts[...].astype(F32), (8, 128))
    mine = pl.ds(pl.multiple_of(y * 128, 128), 128)
    XG[mine, :] = tok[...]
    CG[mine, :] = cot[...]

    def row(plane):
        return pl.ds(pl.multiple_of(g * 256 + plane * 128 + w * 32, 32), 32)

    for ch in range(3):
        W[ch][row(y), :] = WS[ch][y]
    row_o = pl.ds(pl.multiple_of(g * 128 + w * 32, 32), 32)
    WO[y, row_o, :] = wo_in[...]
    all_in()

    def z_rows(ch, plane):
        return sum(
            (go(cp.new(W[ch].at[row(plane), :], W[ch].at[row(plane), :], p.dev_z(k))) for k in (2, 1, 3)), ()
        )

    yw = [go(cp.new(WS[ch].at[1 - y], W[ch].at[row(y), :], p.dev_y)) for ch in range(3)]
    zw = [z_rows(0, y), (), ()]
    ty = go(cp.new(RT.at[y], RT.at[y], p.dev_y), cp.new(tok, XG.at[mine, :], p.dev_y))

    def dq(q):
        return pl.ds(pl.multiple_of(q * 256, 256), 256)

    half = pl.ds(pl.multiple_of(x * 512, 512), 512)
    other = pl.ds(pl.multiple_of((1 - x) * 512, 512), 512)

    def e_first(s):
        return (
            cp.new(up_in.at[s, :, other], UP.at[s, 0, dq(g), :], p.dev_x),
            cp.new(dn_in.at[s, other, :], DN.at[s, 0, :, dq(g)], p.dev_x),
        )

    def e_core0(s):
        return go(
            cp.new(up_in.at[s, :, half], UP.at[s, 0, dq(g), :], p.dev_c),
            cp.new(dn_in.at[s, half, :], DN.at[s, 0, :, dq(g)], p.dev_c),
        )

    def e_local(s):
        return go(
            here(up_in.at[s, :, half], UP.at[s, 0, dq(g), :]),
            here(dn_in.at[s, half, :], DN.at[s, 0, :, dq(g)]),
        )

    def e_z(s):
        return (
            cp.new(up_in.at[s, :, half], UP.at[s, 1, dq(g), :], p.dev_pair),
            cp.new(dn_in.at[s, half, :], DN.at[s, 1, :, dq(g)], p.dev_pair),
        )

    def e_relay(s):
        return go(
            cp.new(UP.at[s, 0, dq(p.gx), :], UP.at[s, 1, dq(p.gx), :], p.dev_pair),
            cp.new(DN.at[s, 0, :, dq(p.gx)], DN.at[s, 1, :, dq(p.gx)], p.dev_pair),
        )

    def e_core(s, q, which):
        return go(
            cp.new(UP.at[s, q, dq(which), :], UP.at[s, q, dq(which), :], p.dev_c),
            cp.new(DN.at[s, q, :, dq(which)], DN.at[s, q, :, dq(which)], p.dev_c),
        )

    e1 = [e_first(0), e_first(1)]
    go(*e1[0])
    wait(*yw[0])
    zw[0] += z_rows(0, 1 - y)
    for ch in (1, 2):
        wait(*yw[ch])
        zw[ch] = z_rows(ch, y) + z_rows(ch, 1 - y)
    zo = sum((go(cp.new(wo_in, WO.at[y, row_o, :], p.dev_z(k))) for k in (2, 1, 3)), ())
    el = e_local(0) + e_local(1)
    ec0 = [e_core0(0), e_core0(1)]

    wait(*ty)
    values = XG[...].astype(F32)
    centred = values - jnp.mean(values, axis=1, keepdims=True)
    inverse = lax.rsqrt(jnp.mean(centred * centred, axis=1, keepdims=True) + 1e-05)
    XH[...] = centred * inverse
    for b in (0, 1):
        DSP[b] = dispatch_block(RT[b], y)
        XS[b * CAP : (b + 1) * CAP, :] = dot(DSP[b], XG[b * 128 : (b + 1) * 128, :])

    def quarter(d):
        return pl.ds(pl.multiple_of(d * 128, 128), 128)

    def wo_copy(plane, d, device):
        return cp.new(WO.at[plane, quarter(d), :], WO.at[plane, quarter(d), :], device)

    def w_copy(ch, d, device):
        return cp.new(W[ch].at[dq(d), :], W[ch].at[dq(d), :], device)

    xw, fw = [None] * 3, [None] * 3
    for ch in range(3):
        wait(*zw[ch])
        xw[ch] = go(w_copy(ch, g, p.dev_x), w_copy(ch, g, p.dev_c))
    wait(*zo)
    yo = go(wo_copy(y, g, p.dev_y))
    ez = [go(*e_z(0)), e_z(1)]
    cy = go(cp.new(cot, CG.at[mine, :], p.dev_y))
    wait(*xw[0])
    fw[0] = go(w_copy(0, p.gx, p.dev_c))
    wait(*fw[0])
    extra = dot(one_hot(8, EXTRA), W0[:, 512:], NT)
    gain = extra[0:1, :]
    centroid = jnp.where(y == 0, extra[1:2, :], extra[2:3, :])
    NRM[...] = (XH[...] * gain).astype(BF)

    def project(ch):
        QKV[:, ch * 512 : (ch + 1) * 512] = dot(NRM[...], W[ch][:, :512]).astype(BF)

    project(0)
    wait(*xw[1])
    fw[1] = go(w_copy(1, p.gx, p.dev_c))
    wait(*fw[1])
    project(1)
    wait(*yo)
    xo = go(
        cp.new(WO.at[:, quarter(g), :], WO.at[:, quarter(g), :], p.dev_x),
        cp.new(WO.at[:, quarter(g), :], WO.at[:, quarter(g), :], p.dev_c),
    )
    go(*e1[1])
    wait(*e1[0])
    er = [e_relay(0)]
    ec = [e_core(0, 0, p.gx)]
    go(*ez[1])
    place_q, seq_q = place_of(lengths, order, lax.broadcasted_iota(jnp.int32, (256, 256), 0))
    place_k, seq_k = place_of(lengths, order, lax.broadcasted_iota(jnp.int32, (256, 256), 1))
    allowed = (seq_q == seq_k) & (place_k <= place_q)
    low_half = lax.broadcasted_iota(jnp.int32, (256, 128), 1) < 64
    mixed_first = cp.block(4)

    def mixed_copy(t):
        cols = pl.ds(pl.multiple_of(t * 128, 128), 128)
        return cp.at(mixed_first + t, MXH.at[y, :, cols], MXH.at[y, :, cols], p.dev_y)

    def weigh(t, carry):
        q2 = QKV[:, pl.ds(pl.multiple_of(t * 128, 128), 128)]
        k2 = QKV[:, pl.ds(pl.multiple_of(512 + t * 128, 128), 128)]
        for i in (0, 1):
            keep = low_half if i == 0 else ~low_half
            scores = dot(jnp.where(keep, q2, jnp.zeros_like(q2)), k2, NT) * 0.125
            scores = jnp.where(allowed, scores, -1000000000.0)
            exponent = jnp.exp(scores - jnp.max(scores, axis=1, keepdims=True))
            PR[2 * t + i] = exponent / jnp.sum(exponent, axis=1, keepdims=True)
        return carry

    def mix(t, carry):
        v2 = QKV[:, pl.ds(pl.multiple_of(1024 + t * 128, 128), 128)]
        low_part, high_part = (dot(PR[2 * t + i].astype(BF), v2) for i in (0, 1))
        MXH[y, :, pl.ds(pl.multiple_of(t * 128, 128), 128)] = jnp.where(low_half, low_part, high_part).astype(BF)
        mixed_copy(t).start()
        return carry

    lax.fori_loop(0, 2, weigh, 0)
    wait(*xw[2])
    fw[2] = go(w_copy(2, p.gx, p.dev_c))
    lax.fori_loop(2, 4, weigh, 0)
    wait(*fw[2])
    project(2)
    lax.fori_loop(0, 4, mix, 0)

    def mixed_pick(yy):
        for b in (0, 1):
            MS[yy, b * CAP : (b + 1) * CAP, :] = dot(DSP[b], MXH[yy, b * 128 : (b + 1) * 128, :]).astype(BF)

    mixed_pick(y)
    wait(*cy)
    for b in (0, 1):
        GS[b * CAP : (b + 1) * CAP, :] = dot(DSP[b], CG[b * 128 : (b + 1) * 128, :]).astype(BF)
    wait(*xo)
    co = go(cp.new(WO.at[:, quarter(p.gx), :], WO.at[:, quarter(p.gx), :], p.dev_c))
    wait(*co)
    AA[...] = XS[...] + dot(MS[y], WO[y])
    lax.fori_loop(0, 4, lambda t, carry: (mixed_copy(t).wait(), carry)[1], 0)
    mixed_pick(1 - y)
    AA[...] += dot(MS[1 - y], WO[1 - y])
    gate = jax.nn.sigmoid(jnp.sum(AA[...] * centroid, axis=1, keepdims=True))

    early = [
        here(src, dst)
        for src, dst in (
            (XG, xg_out), (QKV, qkv_out), (PR, pr_out), (MXH, mxh_out),
            (W0, w0_out), (W1, w1_out), (W2, w2_out), (WO, wo_out),
        )
    ]
    go(*early)

    wait(*el)
    at_me, at_x, at_z, at_d = p.team_places()

    def rows_of(place):
        return pl.ds(pl.multiple_of(place * 160, 32), 160)

    def part(i, place=0):
        return pl.ds(pl.multiple_of(place * 160 + i * 32, 32), 32)

    def each(fn):
        def body(i, carry):
            fn(i)
            return carry

        lax.fori_loop(0, 5, body, 0)

    class Spread:
        def __init__(self, R):
            self.R = R
            self.zi, self.xi, self.fi = cp.block(5), cp.block(5), cp.block(5)

        def same(self, first, i, place, device):
            view = self.R.at[part(i, place), :]
            return cp.at(first + i, view, view, device)

        def z(self, i):
            return self.same(self.zi, i, at_me, p.dev_z(2))

        def x(self, i):
            return self.same(self.xi, i, at_me, p.dev_x)

        def forward(self, i):
            return self.same(self.fi, i, at_z, p.dev_x)

        def start_part(self, i):
            self.z(i).start()
            self.x(i).start()

        def relay_part(self, i):
            self.z(i).wait()
            self.forward(i).start()

    class Reduce:
        def __init__(self, staging, landing):
            self.put, self.got = PS.at[staging], RB.at[landing]
            self.xi, self.di, self.zi = cp.block(1), cp.block(5), cp.block(5)

        def x(self):
            return cp.at(self.xi, self.put.at[0], self.got.at[0], p.dev_x)

        def d(self, i):
            return cp.at(self.di + i, self.put.at[1, part(i), :], self.got.at[1, part(i), :], p.dev_x)

        def z(self, i):
            return cp.at(self.zi + i, self.put.at[2, part(i), :], self.got.at[2, part(i), :], p.dev_z(2))

        def start_x(self):
            each(lambda i: self.d(i).start())
            self.x().start()

        def relay_part(self, i, own_z):
            self.d(i).wait()
            self.put[2, part(i), :] = (own_z[part(i), :] + self.got[1, part(i), :].astype(F32)).astype(BF)
            self.z(i).start()

        def result_part(self, i, own):
            self.z(i).wait()
            return (
                own[part(i), :]
                + self.got[0, part(i), :].astype(F32)
                + self.got[2, part(i), :].astype(F32)
            )

    g1, g2, g3, g4 = Spread(R1), Spread(R2), Spread(R3), Spread(R4)
    r1, r2, r3, r4 = Reduce(0, 0), Reduce(1, 1), Reduce(0, 2), Reduce(0, 3)
    mine_r = rows_of(at_me)

    R1[mine_r, :] = AA[...].astype(BF)
    each(lambda i: g1.z(i).start())
    each(lambda i: g1.x(i).start())
    R3[mine_r, :] = (gate * GS[...].astype(F32)).astype(BF)
    each(lambda i: g3.z(i).start())
    each(lambda i: g3.x(i).start())

    wait(*ec0[0])
    wait(*ec[0])
    wait(*ez[0])
    ec1 = e_core(0, 1, g)
    wait(*er[0])
    ec2 = e_core(0, 1, p.gx)
    wait(*ec1)
    wait(*ec2)

    def cols_of(q):
        return slice(q * 512, (q + 1) * 512)

    def first_forward(place):
        at = rows_of(place)
        total = None
        for q in (0, 1):
            active, slope = gelu_both(dot(R1[at, :], UP[0, q]))
            GP1[at, cols_of(q)] = slope
            A1[at, cols_of(q)] = active.astype(BF)
            term = dot(active.astype(BF), DN[0, q])
            total = term if total is None else total + term
        return total

    OWN[0] = first_forward(at_me)
    each(g1.relay_part)
    wait(*e1[1])
    er.append(e_relay(1))
    ec.append(e_core(1, 0, p.gx))
    each(lambda i: g1.x(i).wait())
    PS[0, 0] = first_forward(at_x).astype(BF)
    OWN[3] = first_forward(at_z)
    each(lambda i: g1.forward(i).wait())
    PS[0, 1] = first_forward(at_d).astype(BF)
    r1.start_x()
    each(lambda i: r1.relay_part(i, OWN.at[3]))
    r1.x().wait()

    def middle_part(i):
        branch = r1.result_part(i, OWN.at[0])
        SUMS[0, part(i), :] = branch
        R2[part(i, at_me), :] = (AA[part(i), :].astype(BF).astype(F32) + branch).astype(BF)
        g2.start_part(i)

    each(middle_part)
    each(g3.relay_part)

    wait(*ec0[1])
    wait(*ec[1])
    wait(*ez[1])
    ec1 = e_core(1, 1, g)
    wait(*er[1])
    ec2 = e_core(1, 1, p.gx)
    wait(*ec1)
    wait(*ec2)

    def second_grad(place):
        at = rows_of(place)
        total_grad = None
        for q in (0, 1):
            active, slope = gelu_both(dot(R2[at, :], UP[1, q]))
            A2[at, cols_of(q)] = active.astype(BF)
            grad = (slope * dot(R3[at, :], DN[1, q], NT)).astype(BF)
            DH[at, cols_of(q)] = grad
            term = dot(grad, UP[1, q], NT)
            total_grad = term if total_grad is None else total_grad + term
        return total_grad

    def second_forward(place):
        at = rows_of(place)
        return dot(A2[at, :512], DN[1, 0]) + dot(A2[at, 512:], DN[1, 1])

    OWN[2] = second_grad(at_me)
    OWN[1] = second_forward(at_me)
    each(g2.relay_part)
    each(lambda i: g2.x(i).wait())
    each(lambda i: g3.x(i).wait())
    PS[0, 0] = second_grad(at_x).astype(BF)
    OWN[3] = second_grad(at_z)
    each(lambda i: g2.forward(i).wait())
    each(lambda i: g3.forward(i).wait())
    PS[0, 1] = second_grad(at_d).astype(BF)
    r3.start_x()
    PS[1, 1] = second_forward(at_d).astype(BF)
    PS[1, 0] = second_forward(at_x).astype(BF)
    OWN[4] = second_forward(at_z)
    each(lambda i: r3.relay_part(i, OWN.at[3]))
    each(lambda i: r2.d(i).start())

    def weight_grads(A, R, RG, GU, GD):
        def one(q, d):
            qcols = pl.ds(pl.multiple_of(q * 512, 512), 512)
            GU[q, d] = dot(R[:, dq(d)], DH[:, qcols], TN).astype(BF)
            GD[q, d] = dot(A[:, qcols], RG[:, dq(d)], TN).astype(BF)

        def body(t, carry):
            q, k = lax.rem(t, 2), lax.div(t, 2)
            d = lax.rem(k, 2)
            mine_c = lax.div(k, 2)
            cc = p.c * mine_c + (1 - p.c) * (1 - mine_c)
            one(q, 2 * d + cc)
            return carry

        return body

    def to_core(n):
        out = ()
        for k, theirs in enumerate((p.gc, p.gd)):
            out += go(
                cp.new(GU.at[:, theirs], CRU.at[n, :, k], p.dev_c),
                cp.new(GD.at[:, theirs], CRD.at[n, :, k], p.dev_c),
            )
        return out

    def add_core(n, own_u, own_d, far_u, far_d):
        for k, d in enumerate((g, p.gx)):
            far_u[k] = (GU[1, d].astype(F32) + CRU[n, 1, k].astype(F32)).astype(BF)
            far_d[k] = (GD[1, d].astype(F32) + CRD[n, 1, k].astype(F32)).astype(BF)
            own_u[k] = (GU[0, d].astype(F32) + CRU[n, 0, k].astype(F32)).astype(BF)
            own_d[k] = (GD[0, d].astype(F32) + CRD[n, 0, k].astype(F32)).astype(BF)

    body2 = weight_grads(A2, R2, R3, GU, GD)
    lax.fori_loop(0, 4, body2, 0)
    f0 = to_core(0)
    lax.fori_loop(4, 8, body2, 0)

    r3.x().wait()

    def middle_grad_part(i):
        total = r3.result_part(i, OWN.at[2])
        SUMS[1, part(i), :] = total
        R4[part(i, at_me), :] = (R3[part(i, at_me), :].astype(F32) + total).astype(BF)
        g4.start_part(i)

    each(middle_grad_part)
    wait(*f0)
    add_core(0, P2U, P2D, ZSU, ZSD)
    f1 = []
    for k in (0, 1):
        f1 += go(
            cp.new(ZSU.at[k], ZRU.at[k], p.dev_pair),
            cp.new(ZSD.at[k], ZRD.at[k], p.dev_pair),
        )

    each(lambda i: r2.relay_part(i, OWN.at[4]))

    def first_backward(place):
        at = rows_of(place)
        total = None
        for q in (0, 1):
            grad = (GP1[at, cols_of(q)] * dot(R4[at, :], DN[0, q], NT)).astype(BF)
            DH[at, cols_of(q)] = grad
            term = dot(grad, UP[0, q], NT)
            total = term if total is None else total + term
        return total

    OWN[0] = first_backward(at_me)
    each(g4.relay_part)
    r2.x().start()
    each(lambda i: g4.x(i).wait())
    PS[0, 0] = first_backward(at_x).astype(BF)
    OWN[3] = first_backward(at_z)
    each(lambda i: g4.forward(i).wait())
    PS[0, 1] = first_backward(at_d).astype(BF)
    r4.start_x()

    def output_part(i):
        branch_two = r2.result_part(i, OWN.at[1])
        returned = (SUMS[0, part(i), :] + branch_two).astype(BF).astype(F32)
        upstream = GS[part(i), :].astype(F32)
        after = AA[part(i), :]
        gate_part = jax.nn.sigmoid(jnp.sum(after * centroid, axis=1, keepdims=True))
        OUTS[part(i), :] = (after + gate_part * returned).astype(BF)
        score_grad = jnp.sum(upstream * returned, axis=1, keepdims=True) * gate_part * (1.0 - gate_part)
        RES[part(i), :] = upstream + score_grad * centroid
        CGR[...] += jnp.broadcast_to(jnp.sum(score_grad * after, axis=0, keepdims=True), CGR.shape)

    CGR[...] = jnp.zeros_like(CGR)

    each(lambda i: r4.relay_part(i, OWN.at[3]))
    r2.x().wait()
    each(output_part)
    body1 = weight_grads(A1, R1, R4, GU, GD)
    lax.fori_loop(0, 4, body1, 0)
    f0 = to_core(1)
    lax.fori_loop(4, 8, body1, 0)
    r4.x().wait()

    def residual_part(i):
        arrived = (r4.result_part(i, OWN.at[0]) + SUMS[1, part(i), :]).astype(BF)
        RESS[part(i), :] = (RES[part(i), :] + arrived.astype(F32)).astype(BF)

    each(residual_part)
    wait(*f0)
    add_core(1, P1U, P1D, Z1U, Z1D)
    wait(*f1)
    for k in (0, 1):
        S2U[k] = P2U[k].astype(F32) + ZRU[k].astype(F32)
        S2D[k] = P2D[k].astype(F32) + ZRD[k].astype(F32)
    wait(*early)


def backward_kernel(
    xg_in, qkv_in, pr_in, mxh_in, w0_in, w1_in, w2_in, wo_in,
    RT, OUTS, RESS, CGR, P1U, P1D, Z1U, Z1D, S2U, S2D,
    out, tgrad, pgrad, ograd, egrad, ugrad, dgrad,
    XG, QKV, PR, MXH, W0, W1, W2, WO,
    RP, OP, RL, XH, NRM, NRMT, MG, DQ, DT, NG, NGS, NGR,
    ZRU, ZRD, XSU, XSD, XRU, XRD,
    PW0, PW1, PW2, PW3, PC0, PC1, PC2, PC3, PXS0, PXS1, PXS2, PXS3, PXR0, PXR1, PXR2, PXR3,
    PYS0, PYS1, PYS2, PYS3, PK0, PK1, PK2, PK3, PZ0, PZ1, PZ2, PZ3,
    OW, OC, OXS, OXR, OK, OZR, TE,
    send, recv, local,
):
    PW, PC, PXS, PXR = (PW0, PW1, PW2, PW3), (PC0, PC1, PC2, PC3), (PXS0, PXS1, PXS2, PXS3), (PXR0, PXR1, PXR2, PXR3)
    PYS, PK, PZ = (PYS0, PYS1, PYS2, PYS3), (PK0, PK1, PK2, PK3), (PZ0, PZ1, PZ2, PZ3)
    p = Place()
    g, y, w, x = p.g, p.y, p.w, p.x
    cp = Copies(send, recv)
    all_in = greet([p.dev_x, p.dev_c, p.dev_y, p.dev_z(1), p.dev_z(2), p.dev_z(3)])

    def go(*items):
        for item in items:
            item.start()
        return items

    def wait(*items):
        for item in items:
            item.wait()

    loads = [
        copy_in(src, dst, local.at[i])
        for i, (src, dst) in enumerate(
            (
                (xg_in, XG), (w0_in, W0), (wo_in, WO), (mxh_in, MXH),
                (qkv_in, QKV), (pr_in, PR), (w1_in, W1), (w2_in, W2),
            )
        )
    ]
    go(*loads)
    XSU[1] = S2U[1].astype(BF)
    XSD[1] = S2D[1].astype(BF)
    all_in()

    own_slots = pl.ds(pl.multiple_of(y * CAP, 16), CAP)
    peer_slots = pl.ds(pl.multiple_of((1 - y) * CAP, 16), CAP)
    ry = go(cp.new(RESS, RP, p.dev_y))
    oy = go(cp.new(OUTS.at[peer_slots, :], OP, p.dev_y))

    f1 = []
    for k in (1, 0):
        f1 += go(
            cp.new(Z1U.at[k], ZRU.at[k], p.dev_pair),
            cp.new(Z1D.at[k], ZRD.at[k], p.dev_pair),
        )
    f2 = {1: go(cp.new(XSU.at[1], XRU.at[1], p.dev_x), cp.new(XSD.at[1], XRD.at[1], p.dev_x))}

    half = pl.ds(pl.multiple_of(x * 512, 512), 512)
    other = pl.ds(pl.multiple_of((1 - x) * 512, 512), 512)

    wait(loads[0], loads[1])
    values = XG[...].astype(F32)
    centred = values - jnp.mean(values, axis=1, keepdims=True)
    inverse = lax.rsqrt(jnp.mean(centred * centred, axis=1, keepdims=True) + 1e-05)
    XH[...] = centred * inverse
    pick = one_hot(8, EXTRA)
    gain = dot(pick, W0[:, 512:], NT)[0:1, :]
    NRM[...] = (XH[...] * gain).astype(BF)
    NRMT[...] = NRM[...].T
    ugrad[1, :, half] = S2U[0]
    dgrad[1, half, :] = S2D[0]

    wait(*ry)
    for b in (0, 1):
        slots = slice(b * CAP, (b + 1) * CAP)
        RL[b * 128 : (b + 1) * 128, :] = (
            dot(dispatch_block(RT[b], y), RESS[slots, :], TN)
            + dot(dispatch_block(RT[b], 1 - y), RP[slots, :], TN)
        ).astype(BF)
    wait(loads[2])
    MG[...] = dot(RL[...], WO[y], NT).astype(BF)

    def rows4(d):
        return pl.ds(pl.multiple_of(d * 128, 128), 128)

    def dq(d):
        return pl.ds(pl.multiple_of(d * 256, 256), 256)

    def row32(v):
        return pl.ds(pl.multiple_of(v * 32, 32), 32)

    def out_rows(d):
        OW[rows4(d), :] = dot(MXH[y, :, rows4(d)], RL[...], TN).astype(BF)

    low_half = lax.broadcasted_iota(jnp.int32, (256, 128), 1) < 64

    def heads(t):
        c0 = slice(t * 128, (t + 1) * 128)
        c1 = slice(512 + t * 128, 512 + (t + 1) * 128)
        c2 = slice(1024 + t * 128, 1024 + (t + 1) * 128)
        q2, k2, v2, m2 = QKV[:, c0], QKV[:, c1], QKV[:, c2], MG[:, c0]
        parts = []
        for i in (0, 1):
            keep = low_half if i == 0 else ~low_half
            probs = PR[2 * t + i]
            probs_grad = dot(jnp.where(keep, m2, jnp.zeros_like(m2)), v2, NT)
            delta = jnp.sum(probs_grad * probs, axis=1, keepdims=True)
            scores_grad = (probs * (probs_grad - delta)).astype(BF)
            parts.append(
                (
                    dot(scores_grad, k2) * 0.125,
                    dot(scores_grad, q2, TN) * 0.125,
                    dot(probs.astype(BF), m2, TN),
                )
            )
        for s, c in enumerate((c0, c1, c2)):
            grad = jnp.where(low_half, parts[0][s], parts[1][s]).astype(BF)
            DQ[:, c] = grad
            DT[t, :, s * 128 : (s + 1) * 128] = grad

    pc, px, py, pz = [None] * 4, [None] * 4, [None] * 4, [None] * 4

    def to_core(t):
        PW[t][:, :384] = dot(NRMT[...], DT[t]).astype(BF)
        pc[t] = sum(
            (go(cp.new(PW[t].at[dq(d), :], PC[t].at[k], p.dev_c)) for k, d in enumerate((p.gc, p.gd))), ()
        )

    def to_x(t):
        wait(*pc[t])
        PXS[t][...] = (PW[t][dq(p.gx), :].astype(F32) + PC[t][1].astype(F32)).astype(BF)
        px[t] = go(cp.new(PXS[t], PXR[t], p.dev_x))

    def summed(t, plane):
        rows = rows4(plane)
        full = pl.ds(pl.multiple_of(g * 256 + plane * 128, 128), 128)
        total = PW[t][full, :].astype(F32) + PC[t][0, rows, :].astype(F32) + PXR[t][rows, :].astype(F32)
        return total.astype(BF)

    def to_y(t):
        wait(*px[t])
        PYS[t][...] = summed(t, 1 - y)
        py[t] = go(cp.new(PYS[t], PK[t].at[1], p.dev_y))
        PK[t][0] = summed(t, y)

    def to_z(t):
        wait(*py[t])
        pz[t] = sum(
            (
                go(cp.new(PK[t].at[:, row32(lax.rem(w + k, 4)), :], PZ[t].at[k - 1], p.dev_z(k)))
                for k in (2, 1, 3)
            ),
            (),
        )

    wait(loads[4], loads[5])
    heads(0)
    to_core(0)
    wait(loads[3])
    out_rows(p.gc)
    out_rows(p.gd)
    oc = sum((go(cp.new(OW.at[rows4(d), :], OC.at[k], p.dev_c)) for k, d in enumerate((p.gc, p.gd))), ())
    heads(1)
    to_core(1)
    to_x(0)
    out_rows(g)
    out_rows(p.gx)
    heads(2)
    to_core(2)
    to_x(1)
    wait(*oc)
    for k, d in enumerate((g, p.gx)):
        OK[k] = (OW[rows4(d), :].astype(F32) + OC[k].astype(F32)).astype(BF)
    oz = sum(
        (go(cp.new(OK.at[:, row32(lax.rem(w + k, 4)), :], OZR.at[k - 1], p.dev_z(k))) for k in (2, 1, 3)), ()
    )
    own32 = row32(w)
    heads(3)

    wait(loads[6], loads[7])
    NG[...] = (
        dot(DQ[:, :512], W0[:, :512], NT) + dot(DQ[:, 512:1024], W1[...], NT) + dot(DQ[:, 1024:], W2[...], NT)
    )
    NGS[...] = NG[rows4(1 - y), :].astype(BF)
    ny = go(cp.new(NGS, NGR, p.dev_y))
    gain_row = jnp.sum(NG[...] * XH[...], axis=0, keepdims=True)
    line = lax.broadcasted_iota(jnp.int32, (8, 1024), 0)
    stack = jnp.where(line == 0, gain_row, jnp.where(line == 1 + y, CGR[0:1, :], 0.0)).astype(BF)
    PW3[:, 384:] = dot(stack, pick, TN).astype(BF)
    to_core(3)
    to_x(2)
    to_y(0)
    to_x(3)
    to_y(1)
    to_z(0)

    wait(*oz)

    def out_sum(k):
        return (
            OK[k, own32, :].astype(F32)
            + OZR[0, k].astype(F32)
            + OZR[1, k].astype(F32)
            + OZR[2, k].astype(F32)
        )

    OXS[...] = out_sum(1).astype(BF)
    ox = go(cp.new(OXS, OXR, p.dev_x))

    wait(*ny)
    own_rows = rows4(y)
    normed = XH[own_rows, :]
    mine = XG[own_rows, :].astype(F32)
    mine = mine - jnp.mean(mine, axis=1, keepdims=True)
    inverse = lax.rsqrt(jnp.mean(mine * mine, axis=1, keepdims=True) + 1e-05)
    scaled = (NG[own_rows, :] + NGR[...].astype(F32)) * gain
    tgrad[...] = RL[own_rows, :].astype(F32) + inverse * (
        scaled
        - jnp.mean(scaled, axis=1, keepdims=True)
        - normed * jnp.mean(scaled * normed, axis=1, keepdims=True)
    )
    to_y(2)
    to_z(1)

    wait(*f1)
    XSU[0] = (P1U[1].astype(F32) + ZRU[1].astype(F32)).astype(BF)
    XSD[0] = (P1D[1].astype(F32) + ZRD[1].astype(F32)).astype(BF)
    f2[0] = go(cp.new(XSU.at[0], XRU.at[0], p.dev_x), cp.new(XSD.at[0], XRD.at[0], p.dev_x))
    wait(*oy)
    route_own = RT[y]
    out[...] = (
        dot(dispatch_block(route_own, y), OUTS[own_slots, :], TN)
        + dot(dispatch_block(route_own, 1 - y), OP[...], TN)
    ).astype(BF)
    to_y(3)
    to_z(2)
    ugrad[0, :, half] = P1U[0].astype(F32) + ZRU[0].astype(F32)
    dgrad[0, half, :] = P1D[0].astype(F32) + ZRD[0].astype(F32)
    wait(*f2[1])
    ugrad[1, :, other] = XRU[1].astype(F32)
    dgrad[1, other, :] = XRD[1].astype(F32)
    to_z(3)

    for t in range(4):
        wait(*pz[t])
        sums = [
            PK[t][i, own32, :].astype(F32)
            + PZ[t][0, i].astype(F32)
            + PZ[t][1, i].astype(F32)
            + PZ[t][2, i].astype(F32)
            for i in (0, 1)
        ]
        for plane in (0, 1):
            kept = jnp.where(y == plane, sums[0], sums[1])
            for s in range(3):
                first = s * 1024 + t * 256 + plane * 128
                pgrad[:, first : first + 128] = kept[:, s * 128 : (s + 1) * 128]
        if t == 3:
            TE[0:32, :] = sums[0][:, 384:] + sums[1][:, 384:]
    egrad[...] = TE[...].T[0:8, :]
    wait(*f2[0])
    ugrad[0, :, other] = XRU[0].astype(F32)
    dgrad[0, other, :] = XRD[0].astype(F32)
    wait(*ox)
    ograd[...] = out_sum(0) + OXR[...].astype(F32)


def finish_kernel(
    out, tgrad, pgrad, ograd, egrad, ugrad, dgrad, out2, tgrad2, gain, pgrad2, ograd2, cent, ugrad2, dgrad2
):
    out2[0] = out[...]
    tgrad2[0] = tgrad[...]
    pgrad2[...] = pgrad[...]
    ograd2[...] = ograd[...]
    gain[...] = egrad[0:1, :32]
    cent[...] = egrad[1:3, :32]
    ugrad2[0] = ugrad[...]
    dgrad2[0] = dgrad[...]


def vmem(shape, dtype=BF):
    return pltpu.VMEM(shape, dtype)


def fast_shards(
    tokens, cotangent, norm_gain, project_weight, output_weight, centroids,
    expert_up, expert_down, sequence_lengths, block_order, routes,
):
    in_vmem = pl.BlockSpec(memory_space=pltpu.VMEM)
    in_any = pl.BlockSpec(memory_space=pl.ANY)
    in_smem = pl.BlockSpec(memory_space=pltpu.SMEM)
    shape = jax.ShapeDtypeStruct
    ext = jnp.pad(
        jnp.concatenate([norm_gain[None], centroids], axis=0).astype(F32), ((0, 5), (0, EXTRA - 32))
    )
    mid_shapes = [
        ((256, 1024), BF),
        ((256, 1536), BF),
        ((8, 256, 256), F32),
        ((2, 256, 512), BF),
        ((1024, 512 + EXTRA), BF),
        ((1024, 512), BF),
        ((1024, 512), BF),
        ((2, 512, 1024), BF),
        ((2, 8, 128), F32),
        ((160, 1024), BF),
        ((160, 1024), BF),
        ((8, 1024), F32),
        ((2, 256, 512), BF),
        ((2, 512, 256), BF),
        ((2, 256, 512), BF),
        ((2, 512, 256), BF),
        ((2, 256, 512), F32),
        ((2, 512, 256), F32),
    ]
    mid = pl.pallas_call(
        forward_kernel,
        name="forward",
        out_shape=[shape(*s) for s in mid_shapes],
        in_specs=[in_smem] * 2 + [in_vmem] * 6 + [in_any] * 2,
        out_specs=[in_any] * 8 + [in_vmem] * (len(mid_shapes) - 8),
        scratch_shapes=[vmem(*s) for s in mid_shapes[:8]]
        + [
            vmem((2, 32, 512 + EXTRA)),
            vmem((2, 32, 512)),
            vmem((2, 32, 512)),
            vmem((256, 1024)),
            vmem((256, 1024), F32),
            vmem((256, 1024)),
            vmem((2, 2, 1024, 512)),
            vmem((2, 2, 512, 1024)),
            vmem((2, CAP, 128)),
            vmem((160, 1024), F32),
            vmem((160, 1024)),
            vmem((2, 160, 512)),
            vmem((160, 1024), F32),
        ]
        + [vmem((640, 1024))] * 4
        + [
            vmem((4, 3, 160, 1024)),
            vmem((2, 3, 160, 1024)),
            vmem((5, 160, 1024), F32),
            vmem((160, 1024), F32),
            vmem((640, 1024), F32),
            vmem((640, 1024)),
            vmem((640, 1024)),
            vmem((640, 1024)),
            vmem((2, 160, 1024), F32),
            vmem((2, 4, 256, 512)),
            vmem((2, 4, 512, 256)),
            vmem((2, 2, 2, 256, 512)),
            vmem((2, 2, 2, 512, 256)),
            vmem((2, 256, 512)),
            vmem((2, 512, 256)),
            vmem((2, 256, 512)),
            vmem((2, 512, 256)),
            vmem((2, 256, 512)),
            vmem((2, 512, 256)),
            pltpu.SemaphoreType.DMA((208,)),
            pltpu.SemaphoreType.DMA((208,)),
            pltpu.SemaphoreType.DMA((24,)),
        ],
        compiler_params=pltpu.CompilerParams(
            collective_id=0, has_side_effects=True, vmem_limit_bytes=VMEM_LIMIT
        ),
    )(
        sequence_lengths[0], block_order[0], tokens[0], cotangent[0], routes.reshape(1, 128),
        project_weight, output_weight, ext, expert_up[0], expert_down[0],
    )
    out_shapes = [
        ((128, 1024), BF),
        ((128, 1024), F32),
        ((32, 3072), F32),
        ((32, 1024), F32),
        ((8, EXTRA), F32),
        ((2, 256, 1024), F32),
        ((2, 1024, 256), F32),
    ]
    out, tgrad, pgrad, ograd, egrad, ugrad, dgrad = pl.pallas_call(
        backward_kernel,
        name="backward",
        out_shape=[shape(*s) for s in out_shapes],
        in_specs=[in_any] * 8 + [in_vmem] * (len(mid_shapes) - 8),
        out_specs=[in_vmem] * len(out_shapes),
        scratch_shapes=[vmem(*s) for s in mid_shapes[:8]]
        + [
            vmem((160, 1024)),
            vmem((CAP, 1024)),
            vmem((256, 1024)),
            vmem((256, 1024), F32),
            vmem((256, 1024)),
            vmem((1024, 256)),
            vmem((256, 512)),
            vmem((256, 1536)),
            vmem((4, 256, 384)),
            vmem((256, 1024), F32),
            vmem((128, 1024)),
            vmem((128, 1024)),
            vmem((2, 256, 512)),
            vmem((2, 512, 256)),
            vmem((2, 256, 512)),
            vmem((2, 512, 256)),
            vmem((2, 256, 512)),
            vmem((2, 512, 256)),
        ]
        + [vmem((1024, c)) for c in CHUNKS]
        + [vmem((2, 256, c)) for c in CHUNKS]
        + [vmem((256, c)) for c in CHUNKS]
        + [vmem((256, c)) for c in CHUNKS]
        + [vmem((128, c)) for c in CHUNKS]
        + [vmem((2, 128, c)) for c in CHUNKS]
        + [vmem((3, 2, 32, c)) for c in CHUNKS]
        + [
            vmem((512, 1024)),
            vmem((2, 128, 1024)),
            vmem((32, 1024)),
            vmem((32, 1024)),
            vmem((2, 128, 1024)),
            vmem((3, 2, 32, 1024)),
            vmem((EXTRA, EXTRA), F32),
            pltpu.SemaphoreType.DMA((64,)),
            pltpu.SemaphoreType.DMA((64,)),
            pltpu.SemaphoreType.DMA((8,)),
        ],
        compiler_params=pltpu.CompilerParams(
            collective_id=1, has_side_effects=True, vmem_limit_bytes=VMEM_LIMIT
        ),
    )(*mid)
    out, tgrad, gain, pgrad, ograd, cent, ugrad, dgrad = pl.pallas_call(
        finish_kernel,
        name="finish",
        out_shape=[
            shape((1, 128, 1024), BF),
            shape((1, 128, 1024), F32),
            shape((1, 32), F32),
            shape((32, 3072), F32),
            shape((32, 1024), F32),
            shape((2, 32), F32),
            shape((1, 2, 256, 1024), F32),
            shape((1, 2, 1024, 256), F32),
        ],
        in_specs=[in_vmem] * 7,
        out_specs=[in_vmem] * 8,
        compiler_params=pltpu.CompilerParams(vmem_limit_bytes=VMEM_LIMIT),
    )(out, tgrad, pgrad, ograd, egrad, ugrad, dgrad)
    return out, tgrad, gain[0], pgrad, ograd, cent, ugrad, dgrad


def solution(mesh):
    sizes = dict(mesh.shape)
    fast = sizes == {"grp": 4, "ctx": 2, "wsh": 4}
    return jax.shard_map(
        fast_shards if fast else shards,
        mesh=mesh,
        in_specs=IN_SPECS,
        out_specs=OUT_SPECS,
        check_vma=False,
    )
```

```python
import math

import jax
import jax.numpy as jnp
from jax import lax
from jax.experimental import pallas as pl
from jax.experimental.pallas import tpu as pltpu
from jax.sharding import PartitionSpec as P

HEADS = 16
HDIM = 64
BLK = 128


precise = lax.Precision.HIGHEST


def place_rows(order_row, lengths_row, total_rows):
    row_index = jnp.arange(total_rows, dtype=jnp.int32)
    picked = (row_index // BLK)[:, None] == jnp.arange(order_row.shape[0], dtype=jnp.int32)[None, :]
    blocks = jnp.sum(jnp.where(picked, order_row[None, :], 0), axis=1)
    token_place = blocks * BLK + row_index % BLK
    bounds = jnp.cumsum(lengths_row)
    sequence = jnp.sum((token_place[:, None] >= bounds[None, :]).astype(jnp.int32), axis=1)
    return (token_place, sequence)


def normalize(values):
    average = jnp.mean(values, axis=-1, keepdims=True)
    centred = values - average
    inverse = lax.rsqrt(jnp.mean(centred * centred, axis=-1, keepdims=True) + 1e-05)
    return (centred * inverse, inverse)


def head_slice(matrix, section, offset, heads_per):
    width_part = heads_per * HDIM
    first_col = offset + section * width_part
    return matrix[:, first_col : first_col + width_part].reshape(matrix.shape[0], heads_per, HDIM)


def spread_rows(local_rows):
    return lax.all_gather(local_rows, "wsh", axis=0, tiled=True)


def collect_rows(partial_term):
    return lax.psum_scatter(
        partial_term.astype(jnp.bfloat16), "wsh", scatter_dimension=0, tiled=True
    ).astype(jnp.float32)


def trade_rows(slots_rows, peer_count, capacity):
    shaped = slots_rows.reshape(peer_count, capacity, slots_rows.shape[-1])
    moved = lax.all_to_all(shaped, "ctx", split_axis=0, concat_axis=0, tiled=True)
    return moved.reshape(peer_count * capacity, slots_rows.shape[-1])


def gelu_pullback(hidden, incoming):
    value_out, pullback = jax.vjp(jax.nn.gelu, hidden)
    return pullback(incoming)[0]


def shards(
    tokens,
    cotangent,
    norm_gain,
    project_weight,
    output_weight,
    centroids,
    expert_up,
    expert_down,
    sequence_lengths,
    block_order,
    routes,
):
    local_rows = tokens.shape[1]
    model_width = tokens.shape[2]
    peer_count = lax.axis_size("ctx")
    position = lax.axis_index("ctx")
    total_rows = local_rows * peer_count
    capacity = max(2, (5 * local_rows + 4 * peer_count - 1) // (4 * peer_count))
    slot_count = peer_count * capacity
    score_scale = 1.0 / math.sqrt(HDIM)
    heads_per = 4
    sections = HEADS // heads_per
    inputs_f = tokens[0].astype(jnp.float32)
    upstream = cotangent[0].astype(jnp.float32)
    project_full, output_full, gain_full, centroid_full = (
        lax.all_gather(project_weight, ("grp", "ctx", "wsh"), axis=0, tiled=True),
        lax.all_gather(output_weight, ("grp", "ctx", "wsh"), axis=0, tiled=True),
        lax.all_gather(norm_gain, ("grp", "ctx", "wsh"), axis=0, tiled=True),
        lax.all_gather(centroids, ("grp", "ctx", "wsh"), axis=1, tiled=True),
    )
    up_full, down_full = (
        lax.all_gather(expert_up, "grp", axis=2, tiled=True),
        lax.all_gather(expert_down, "grp", axis=3, tiled=True),
    )
    place_all, sequence_all = place_rows(block_order[0], sequence_lengths[0], total_rows)
    place_own = lax.dynamic_slice_in_dim(place_all, position * local_rows, local_rows)
    sequence_own = lax.dynamic_slice_in_dim(sequence_all, position * local_rows, local_rows)
    allowed = (sequence_own[:, None] == sequence_all[None, :]) & (
        place_all[None, :] <= place_own[:, None]
    )
    normed, inverse = normalize(inputs_f)
    gain_values = gain_full.astype(jnp.float32)
    normed_low = (normed * gain_values).astype(jnp.bfloat16)
    projected = jnp.dot(normed_low, project_full, preferred_element_type=jnp.float32)
    queries = projected[:, :model_width].astype(jnp.bfloat16)
    keyvalue = projected[:, model_width:].astype(jnp.bfloat16)
    keyvalue_all = lax.all_gather(keyvalue, "ctx", axis=0, tiled=True)
    mixed_parts = []
    logsum_parts = []
    for section in range(sections):
        head_query = head_slice(queries, section, 0, heads_per)
        head_key = head_slice(keyvalue_all, section, 0, heads_per)
        head_value = head_slice(keyvalue_all, section, model_width, heads_per)
        scores = (
            jnp.einsum("tgd,sgd->gts", head_query, head_key, preferred_element_type=jnp.float32)
            * score_scale
        )
        scores = jnp.where(allowed[None], scores, -1000000000.0)
        largest = jnp.max(scores, axis=-1, keepdims=True)
        exponent = jnp.exp(scores - largest)
        totals = jnp.sum(exponent, axis=-1, keepdims=True)
        weights = (exponent / totals).astype(jnp.bfloat16)
        mixed_part = jnp.einsum(
            "gts,sgd->tgd", weights, head_value, preferred_element_type=jnp.float32
        )
        mixed_parts.append(mixed_part.reshape(local_rows, heads_per * HDIM))
        logsum_parts.append((largest + jnp.log(totals))[:, :, 0])
    mixed_all = jnp.concatenate(mixed_parts, axis=1).astype(jnp.bfloat16)
    logsum = jnp.concatenate(logsum_parts, axis=0)
    after_attention = inputs_f + jnp.dot(mixed_all, output_full, preferred_element_type=jnp.float32)
    route_ids = routes[0, :, 0]
    member = route_ids[:, None] == jnp.arange(peer_count, dtype=jnp.int32)[None, :]
    member_f = member.astype(jnp.float32)
    picked_centroid = jnp.dot(member_f, centroid_full.astype(jnp.float32), precision=precise)
    gate_value = jax.nn.sigmoid(jnp.sum(after_attention * picked_centroid, axis=-1))
    member_int = member.astype(jnp.int32)
    ranking = jnp.sum((jnp.cumsum(member_int, axis=0) - 1) * member_int, axis=1)
    slot_index = route_ids * capacity + ranking
    dispatch = (slot_index[None, :] == jnp.arange(slot_count, dtype=jnp.int32)[:, None]).astype(
        jnp.bfloat16
    )
    sent_rows = jnp.dot(
        dispatch, after_attention.astype(jnp.bfloat16), preferred_element_type=jnp.float32
    ).astype(jnp.bfloat16)
    arrived = trade_rows(sent_rows, peer_count, capacity)
    up_first = up_full[0, 0]
    up_second = up_full[0, 1]
    down_first = down_full[0, 0]
    down_second = down_full[0, 1]
    gathered_one = spread_rows(arrived)
    hidden_one = jnp.dot(gathered_one, up_first, preferred_element_type=jnp.float32)
    active_one = jax.nn.gelu(hidden_one).astype(jnp.bfloat16)
    branch_one = collect_rows(jnp.dot(active_one, down_first, preferred_element_type=jnp.float32))
    middle = (arrived.astype(jnp.float32) + branch_one).astype(jnp.bfloat16)
    gathered_two = spread_rows(middle)
    hidden_two = jnp.dot(gathered_two, up_second, preferred_element_type=jnp.float32)
    active_two = jax.nn.gelu(hidden_two).astype(jnp.bfloat16)
    branch_two = collect_rows(jnp.dot(active_two, down_second, preferred_element_type=jnp.float32))
    expert_out = (branch_one + branch_two).astype(jnp.bfloat16)
    returned = trade_rows(expert_out, peer_count, capacity)
    returned_tok = jnp.einsum("st,sd->td", dispatch, returned, preferred_element_type=jnp.float32)
    output = after_attention + gate_value[:, None] * returned_tok
    gate_grad = jnp.sum(upstream * returned_tok, axis=-1)
    score_grad = gate_grad * gate_value * (1.0 - gate_value)
    centroid_term = jnp.dot(member_f.T, score_grad[:, None] * after_attention, precision=precise)
    branch_grad = (gate_value[:, None] * upstream).astype(jnp.bfloat16)
    branch_sent = jnp.dot(dispatch, branch_grad, preferred_element_type=jnp.float32).astype(
        jnp.bfloat16
    )
    branch_arrived = trade_rows(branch_sent, peer_count, capacity)
    grad_two = spread_rows(branch_arrived)
    hidden_two_grad = gelu_pullback(
        hidden_two, jnp.dot(grad_two, down_second.T, preferred_element_type=jnp.float32)
    ).astype(jnp.bfloat16)
    down_second_grad = jnp.dot(active_two.T, grad_two, preferred_element_type=jnp.float32)
    up_second_grad = jnp.dot(gathered_two.T, hidden_two_grad, preferred_element_type=jnp.float32)
    middle_grad = collect_rows(
        jnp.dot(hidden_two_grad, up_second.T, preferred_element_type=jnp.float32)
    )
    first_branch_grad = (branch_arrived.astype(jnp.float32) + middle_grad).astype(jnp.bfloat16)
    grad_one = spread_rows(first_branch_grad)
    hidden_one_grad = gelu_pullback(
        hidden_one, jnp.dot(grad_one, down_first.T, preferred_element_type=jnp.float32)
    ).astype(jnp.bfloat16)
    down_first_grad = jnp.dot(active_one.T, grad_one, preferred_element_type=jnp.float32)
    up_first_grad = jnp.dot(gathered_one.T, hidden_one_grad, preferred_element_type=jnp.float32)
    arrived_grad = (
        collect_rows(jnp.dot(hidden_one_grad, up_first.T, preferred_element_type=jnp.float32))
        + middle_grad
    ).astype(jnp.bfloat16)
    home_grad = trade_rows(arrived_grad, peer_count, capacity)
    home_grad_tok = jnp.einsum("st,sd->td", dispatch, home_grad, preferred_element_type=jnp.float32)
    up_terms = jnp.stack([up_first_grad, up_second_grad])[None]
    down_terms = jnp.stack([down_first_grad, down_second_grad])[None]
    up_grad_out, down_grad_out = (
        lax.psum_scatter(
            up_terms.astype(jnp.bfloat16), "grp", scatter_dimension=2, tiled=True
        ).astype(jnp.float32),
        lax.psum_scatter(
            down_terms.astype(jnp.bfloat16), "grp", scatter_dimension=3, tiled=True
        ).astype(jnp.float32),
    )
    residual_grad = upstream + score_grad[:, None] * picked_centroid + home_grad_tok
    residual_low = residual_grad.astype(jnp.bfloat16)
    output_term = jnp.dot(mixed_all.T, residual_low, preferred_element_type=jnp.float32)
    mixed_grad = jnp.dot(residual_low, output_full.T, preferred_element_type=jnp.float32).astype(
        jnp.bfloat16
    )
    query_grads = []
    key_grads = []
    value_grads = []
    delta_parts = []
    for section in range(sections):
        head_query = head_slice(queries, section, 0, heads_per)
        head_key = head_slice(keyvalue_all, section, 0, heads_per)
        head_value = head_slice(keyvalue_all, section, model_width, heads_per)
        head_grad = head_slice(mixed_grad, section, 0, heads_per)
        scores = (
            jnp.einsum("tgd,sgd->gts", head_query, head_key, preferred_element_type=jnp.float32)
            * score_scale
        )
        scores = jnp.where(allowed[None], scores, -1000000000.0)
        probs = jnp.exp(
            scores - logsum[section * heads_per : (section + 1) * heads_per][:, :, None]
        )
        probs_grad = jnp.einsum(
            "tgd,sgd->gts", head_grad, head_value, preferred_element_type=jnp.float32
        )
        row_delta = jnp.sum(probs_grad * probs, axis=-1)
        scores_grad = (probs * (probs_grad - row_delta[:, :, None])).astype(jnp.bfloat16)
        query_part = (
            jnp.einsum("gts,sgd->tgd", scores_grad, head_key, preferred_element_type=jnp.float32)
            * score_scale
        )
        query_grads.append(query_part.reshape(local_rows, heads_per * HDIM))
        delta_parts.append(row_delta)
        key_part = (
            jnp.einsum("gts,tgd->sgd", scores_grad, head_query, preferred_element_type=jnp.float32)
            * score_scale
        )
        value_part = jnp.einsum(
            "gts,tgd->sgd",
            probs.astype(jnp.bfloat16),
            head_grad,
            preferred_element_type=jnp.float32,
        )
        key_grads.append(key_part.reshape(total_rows, heads_per * HDIM))
        value_grads.append(value_part.reshape(total_rows, heads_per * HDIM))
    query_grad = jnp.concatenate(query_grads, axis=1).astype(jnp.bfloat16)
    keyvalue_terms = jnp.concatenate(key_grads + value_grads, axis=1)
    keyvalue_grad = lax.psum_scatter(
        keyvalue_terms.astype(jnp.bfloat16), "ctx", scatter_dimension=0, tiled=True
    )
    projected_grad = jnp.concatenate([query_grad, keyvalue_grad], axis=1)
    project_term = jnp.dot(normed_low.T, projected_grad, preferred_element_type=jnp.float32)
    normed_grad = jnp.dot(projected_grad, project_full.T, preferred_element_type=jnp.float32)
    gain_term = jnp.sum(normed_grad * normed, axis=0)
    scaled_grad = normed_grad * gain_values
    input_grad = residual_grad + inverse * (
        scaled_grad
        - jnp.mean(scaled_grad, axis=-1, keepdims=True)
        - normed * jnp.mean(scaled_grad * normed, axis=-1, keepdims=True)
    )
    project_grad, output_grad, gain_grad, centroid_grad = (
        lax.psum_scatter(project_term, ("grp", "ctx", "wsh"), scatter_dimension=0, tiled=True),
        lax.psum_scatter(output_term, ("grp", "ctx", "wsh"), scatter_dimension=0, tiled=True),
        lax.psum_scatter(gain_term, ("grp", "ctx", "wsh"), scatter_dimension=0, tiled=True),
        lax.psum_scatter(centroid_term, ("grp", "ctx", "wsh"), scatter_dimension=1, tiled=True),
    )
    return (
        output.astype(jnp.bfloat16)[None],
        input_grad[None],
        gain_grad,
        project_grad,
        output_grad,
        centroid_grad,
        up_grad_out,
        down_grad_out,
    )


VMEM_LIMIT = 61 * 2**20
CHUNKS = (384, 384, 384, 512)

IN_SPECS = (
    P(("grp", "wsh"), "ctx", None),
    P(("grp", "wsh"), "ctx", None),
    P(("grp", "ctx", "wsh")),
    P(("grp", "ctx", "wsh"), None),
    P(("grp", "ctx", "wsh"), None),
    P(None, ("grp", "ctx", "wsh")),
    P("ctx", None, "grp", "wsh"),
    P("ctx", None, "wsh", "grp"),
    P(("grp", "wsh"), None),
    P(("grp", "wsh"), None),
    P(("grp", "wsh"), "ctx", None),
)
OUT_SPECS = (
    P(("grp", "wsh"), "ctx", None),
    P(("grp", "wsh"), "ctx", None),
    P(("grp", "ctx", "wsh")),
    P(("grp", "ctx", "wsh"), None),
    P(("grp", "ctx", "wsh"), None),
    P(None, ("grp", "ctx", "wsh")),
    P("ctx", None, "grp", "wsh"),
    P("ctx", None, "wsh", "grp"),
)

BF = jnp.bfloat16
F32 = jnp.float32
NN = ((1,), (0,))
NT = ((1,), (1,))
TN = ((0,), (0,))
MESH = pl.DeviceIdType.MESH
GELU_C = 0.7978845608028654
EXTRA = 128
CAP = 80


def dot(a, b, dims=NN):
    return lax.dot_general(a, b, (dims, ((), ())), preferred_element_type=F32)


def gelu_both(h):
    sq = h * h
    t = jnp.tanh(GELU_C * h * (1.0 + 0.044715 * sq))
    half = 0.5 * (1.0 + t)
    slope = half + 0.5 * h * (1.0 - t * t) * (GELU_C * (1.0 + 3.0 * 0.044715 * sq))
    return h * half, slope


def copy_in(src, dst, sem):
    return pltpu.make_async_copy(src, dst, sem)


class Copies:
    def __init__(self, send, recv):
        self.send, self.recv, self.used = send, recv, 0

    def block(self, count):
        first = self.used
        self.used += count
        return first

    def at(self, index, src, dst, device):
        return pltpu.make_async_remote_copy(
            src_ref=src,
            dst_ref=dst,
            send_sem=self.send.at[index],
            recv_sem=self.recv.at[index],
            device_id=device,
            device_id_type=MESH,
        )

    def new(self, src, dst, device):
        return self.at(self.block(1), src, dst, device)


class Place:
    def __init__(self):
        g, y, w = lax.axis_index("grp"), lax.axis_index("ctx"), lax.axis_index("wsh")
        self.g, self.y, self.w = g, y, w
        self.x = lax.div(g, 2)
        self.c = g - 2 * self.x
        self.gx = 2 * (1 - self.x) + self.c
        self.gc = 2 * self.x + 1 - self.c
        self.gd = 2 * (1 - self.x) + 1 - self.c
        self.wb = lax.rem(w, 2)
        self.w1 = w + 1 - 2 * self.wb
        self.w2 = lax.rem(w + 2, 4)
        self.dev_x = (self.gx, y, w)
        self.dev_c = (self.gc, y, w)
        self.dev_y = (g, 1 - y, w)
        self.dev_pair = (g, y, self.w1)
        self.dev_z = lambda k: (g, y, lax.rem(w + k, 4))

    def team_places(self):
        mine = 2 * self.x + lax.div(self.w, 2)
        x_side = 2 * (1 - self.x) + lax.div(self.w, 2)
        flip = 1 - 2 * lax.div(self.w, 2)
        return mine, x_side, mine + flip, x_side + flip


def greet(devices):
    barrier = pltpu.get_barrier_semaphore()
    for device in devices:
        pl.semaphore_signal(barrier, inc=1, device_id=device, device_id_type=MESH)
    return lambda: pl.semaphore_wait(barrier, len(devices))


def one_hot(rows, columns):
    same = lax.broadcasted_iota(jnp.int32, (rows, columns), 0) == lax.broadcasted_iota(
        jnp.int32, (rows, columns), 1
    )
    return same.astype(F32).astype(BF)


def dispatch_block(route_rows, expert):
    member = (route_rows == expert.astype(F32)).astype(F32)
    earlier = lax.broadcasted_iota(jnp.int32, (128, 128), 0) < lax.broadcasted_iota(jnp.int32, (128, 128), 1)
    rank = dot(member.astype(BF), earlier.astype(F32).astype(BF))
    slot = lax.broadcasted_iota(jnp.int32, (CAP, 128), 0).astype(F32)
    hit = (jnp.broadcast_to(rank[0:1, :], (CAP, 128)) == slot) & (
        jnp.broadcast_to(member[0:1, :], (CAP, 128)) > 0.5
    )
    return hit.astype(F32).astype(BF)


def place_of(lengths, order, index):
    place = jnp.where(index < 128, order[0], order[1]) * 128 + lax.rem(index, 128)
    bound = lengths[0]
    sequence = jnp.where(place >= bound, 1, 0)
    for part in (1, 2):
        bound = bound + lengths[part]
        sequence = sequence + jnp.where(place >= bound, 1, 0)
    return place, sequence


def forward_kernel(
    lengths, order, tok, cot, rts, pw, wo_in, ext, up_in, dn_in,
    xg_out, qkv_out, pr_out, mxh_out, w0_out, w1_out, w2_out, wo_out,
    RT, OUTS, RESS, CGR, P1U, P1D, Z1U, Z1D, S2U, S2D,
    XG, QKV, PR, MXH, W0, W1, W2, WO,
    WS0, WS1, WS2, CG, XH, NRM, UP, DN, DSP, XS, GS, MS, AA,
    R1, R2, R3, R4, RB, PS, OWN, RES, GP1, A1, A2, DH, SUMS,
    GU, GD, CRU, CRD, P2U, P2D, ZSU, ZSD, ZRU, ZRD,
    send, recv, local,
):
    p = Place()
    g, y, w, x = p.g, p.y, p.w, p.x
    cp = Copies(send, recv)
    all_in = greet([p.dev_x, p.dev_c, p.dev_y, p.dev_z(1), p.dev_z(2), p.dev_z(3)])
    nlocal = [0]

    def here(src, dst):
        nlocal[0] += 1
        return copy_in(src, dst, local.at[nlocal[0] - 1])

    def go(*items):
        for item in items:
            item.start()
        return items

    def wait(*items):
        for item in items:
            item.wait()

    W, WS = (W0, W1, W2), (WS0, WS1, WS2)
    for ch in range(3):
        for t in range(4):
            for plane in (0, 1):
                first = ch * 1024 + t * 256 + plane * 128
                WS[ch][plane, :, t * 128 : (t + 1) * 128] = pw[:, first : first + 128]
    extra_rows = jnp.concatenate([ext[...], jnp.zeros((EXTRA - 8, EXTRA), F32)], axis=0).astype(BF)
    extra_cols = dot(one_hot(32, EXTRA), extra_rows, NT).astype(BF)
    WS0[0, :, 512:] = extra_cols
    WS0[1, :, 512:] = extra_cols
    RT[y] = jnp.broadcast_to(rts[...].astype(F32), (8, 128))
    mine = pl.ds(pl.multiple_of(y * 128, 128), 128)
    XG[mine, :] = tok[...]
    CG[mine, :] = cot[...]

    def row(plane):
        return pl.ds(pl.multiple_of(g * 256 + plane * 128 + w * 32, 32), 32)

    for ch in range(3):
        W[ch][row(y), :] = WS[ch][y]
    row_o = pl.ds(pl.multiple_of(g * 128 + w * 32, 32), 32)
    WO[y, row_o, :] = wo_in[...]
    all_in()

    def z_rows(ch, plane):
        return sum(
            (go(cp.new(W[ch].at[row(plane), :], W[ch].at[row(plane), :], p.dev_z(k))) for k in (2, 1, 3)), ()
        )

    yw = [go(cp.new(WS[ch].at[1 - y], W[ch].at[row(y), :], p.dev_y)) for ch in range(3)]
    zw = [z_rows(0, y), (), ()]
    ty = go(cp.new(RT.at[y], RT.at[y], p.dev_y), cp.new(tok, XG.at[mine, :], p.dev_y))

    def dq(q):
        return pl.ds(pl.multiple_of(q * 256, 256), 256)

    half = pl.ds(pl.multiple_of(x * 512, 512), 512)
    other = pl.ds(pl.multiple_of((1 - x) * 512, 512), 512)

    def e_first(s):
        return (
            cp.new(up_in.at[s, :, other], UP.at[s, 0, dq(g), :], p.dev_x),
            cp.new(dn_in.at[s, other, :], DN.at[s, 0, :, dq(g)], p.dev_x),
        )

    def e_core0(s):
        return go(
            cp.new(up_in.at[s, :, half], UP.at[s, 0, dq(g), :], p.dev_c),
            cp.new(dn_in.at[s, half, :], DN.at[s, 0, :, dq(g)], p.dev_c),
        )

    def e_local(s):
        return go(
            here(up_in.at[s, :, half], UP.at[s, 0, dq(g), :]),
            here(dn_in.at[s, half, :], DN.at[s, 0, :, dq(g)]),
        )

    def e_z(s):
        return (
            cp.new(up_in.at[s, :, half], UP.at[s, 1, dq(g), :], p.dev_pair),
            cp.new(dn_in.at[s, half, :], DN.at[s, 1, :, dq(g)], p.dev_pair),
        )

    def e_relay(s):
        return go(
            cp.new(UP.at[s, 0, dq(p.gx), :], UP.at[s, 1, dq(p.gx), :], p.dev_pair),
            cp.new(DN.at[s, 0, :, dq(p.gx)], DN.at[s, 1, :, dq(p.gx)], p.dev_pair),
        )

    def e_core(s, q, which):
        return go(
            cp.new(UP.at[s, q, dq(which), :], UP.at[s, q, dq(which), :], p.dev_c),
            cp.new(DN.at[s, q, :, dq(which)], DN.at[s, q, :, dq(which)], p.dev_c),
        )

    e1 = [e_first(0), e_first(1)]
    go(*e1[0])
    wait(*yw[0])
    zw[0] += z_rows(0, 1 - y)
    for ch in (1, 2):
        wait(*yw[ch])
        zw[ch] = z_rows(ch, y) + z_rows(ch, 1 - y)
    zo = sum((go(cp.new(wo_in, WO.at[y, row_o, :], p.dev_z(k))) for k in (2, 1, 3)), ())
    el = e_local(0) + e_local(1)
    ec0 = [e_core0(0), e_core0(1)]

    wait(*ty)
    values = XG[...].astype(F32)
    centred = values - jnp.mean(values, axis=1, keepdims=True)
    inverse = lax.rsqrt(jnp.mean(centred * centred, axis=1, keepdims=True) + 1e-05)
    XH[...] = centred * inverse
    for b in (0, 1):
        DSP[b] = dispatch_block(RT[b], y)
        XS[b * CAP : (b + 1) * CAP, :] = dot(DSP[b], XG[b * 128 : (b + 1) * 128, :])

    def quarter(d):
        return pl.ds(pl.multiple_of(d * 128, 128), 128)

    def wo_copy(plane, d, device):
        return cp.new(WO.at[plane, quarter(d), :], WO.at[plane, quarter(d), :], device)

    def w_copy(ch, d, device):
        return cp.new(W[ch].at[dq(d), :], W[ch].at[dq(d), :], device)

    xw, fw = [None] * 3, [None] * 3
    for ch in range(3):
        wait(*zw[ch])
        xw[ch] = go(w_copy(ch, g, p.dev_x), w_copy(ch, g, p.dev_c))
    wait(*zo)
    yo = go(wo_copy(y, g, p.dev_y))
    ez = [go(*e_z(0)), e_z(1)]
    wait(*e1[0])
    er = [e_relay(0)]
    ec = [e_core(0, 0, p.gx)]
    cy = go(cp.new(cot, CG.at[mine, :], p.dev_y))
    wait(*xw[0])
    fw[0] = go(w_copy(0, p.gx, p.dev_c))
    wait(*fw[0])
    extra = dot(one_hot(8, EXTRA), W0[:, 512:], NT)
    gain = extra[0:1, :]
    centroid = jnp.where(y == 0, extra[1:2, :], extra[2:3, :])
    NRM[...] = (XH[...] * gain).astype(BF)

    def project(ch):
        QKV[:, ch * 512 : (ch + 1) * 512] = dot(NRM[...], W[ch][:, :512]).astype(BF)

    project(0)
    wait(*xw[1])
    fw[1] = go(w_copy(1, p.gx, p.dev_c))
    wait(*fw[1])
    project(1)
    wait(*yo)
    xo = go(
        cp.new(WO.at[:, quarter(g), :], WO.at[:, quarter(g), :], p.dev_x),
        cp.new(WO.at[:, quarter(g), :], WO.at[:, quarter(g), :], p.dev_c),
    )
    go(*e1[1])
    go(*ez[1])
    place_q, seq_q = place_of(lengths, order, lax.broadcasted_iota(jnp.int32, (256, 256), 0))
    place_k, seq_k = place_of(lengths, order, lax.broadcasted_iota(jnp.int32, (256, 256), 1))
    allowed = (seq_q == seq_k) & (place_k <= place_q)
    low_half = lax.broadcasted_iota(jnp.int32, (256, 128), 1) < 64
    mixed_first = cp.block(4)

    def mixed_copy(t):
        cols = pl.ds(pl.multiple_of(t * 128, 128), 128)
        return cp.at(mixed_first + t, MXH.at[y, :, cols], MXH.at[y, :, cols], p.dev_y)

    def weigh(t, carry):
        q2 = QKV[:, pl.ds(pl.multiple_of(t * 128, 128), 128)]
        k2 = QKV[:, pl.ds(pl.multiple_of(512 + t * 128, 128), 128)]
        for i in (0, 1):
            keep = low_half if i == 0 else ~low_half
            scores = dot(jnp.where(keep, q2, jnp.zeros_like(q2)), k2, NT) * 0.125
            scores = jnp.where(allowed, scores, -1000000000.0)
            exponent = jnp.exp(scores - jnp.max(scores, axis=1, keepdims=True))
            PR[2 * t + i] = exponent / jnp.sum(exponent, axis=1, keepdims=True)
        return carry

    def mix(t, carry):
        v2 = QKV[:, pl.ds(pl.multiple_of(1024 + t * 128, 128), 128)]
        low_part, high_part = (dot(PR[2 * t + i].astype(BF), v2) for i in (0, 1))
        MXH[y, :, pl.ds(pl.multiple_of(t * 128, 128), 128)] = jnp.where(low_half, low_part, high_part).astype(BF)
        mixed_copy(t).start()
        return carry

    lax.fori_loop(0, 2, weigh, 0)
    wait(*xw[2])
    fw[2] = go(w_copy(2, p.gx, p.dev_c))
    lax.fori_loop(2, 4, weigh, 0)
    wait(*fw[2])
    project(2)
    lax.fori_loop(0, 4, mix, 0)

    def mixed_pick(yy):
        for b in (0, 1):
            MS[yy, b * CAP : (b + 1) * CAP, :] = dot(DSP[b], MXH[yy, b * 128 : (b + 1) * 128, :]).astype(BF)

    mixed_pick(y)
    wait(*cy)
    for b in (0, 1):
        GS[b * CAP : (b + 1) * CAP, :] = dot(DSP[b], CG[b * 128 : (b + 1) * 128, :]).astype(BF)
    wait(*xo)
    co = go(cp.new(WO.at[:, quarter(p.gx), :], WO.at[:, quarter(p.gx), :], p.dev_c))
    wait(*co)
    AA[...] = XS[...] + dot(MS[y], WO[y])
    lax.fori_loop(0, 4, lambda t, carry: (mixed_copy(t).wait(), carry)[1], 0)
    mixed_pick(1 - y)
    AA[...] += dot(MS[1 - y], WO[1 - y])
    gate = jax.nn.sigmoid(jnp.sum(AA[...] * centroid, axis=1, keepdims=True))

    early = [
        here(src, dst)
        for src, dst in (
            (XG, xg_out), (QKV, qkv_out), (PR, pr_out), (MXH, mxh_out),
            (W0, w0_out), (W1, w1_out), (W2, w2_out), (WO, wo_out),
        )
    ]
    go(*early)

    wait(*el)
    at_me, at_x, at_z, at_d = p.team_places()

    def rows_of(place):
        return pl.ds(pl.multiple_of(place * 160, 32), 160)

    def part(i, place=0):
        return pl.ds(pl.multiple_of(place * 160 + i * 32, 32), 32)

    def each(fn):
        def body(i, carry):
            fn(i)
            return carry

        lax.fori_loop(0, 5, body, 0)

    class Spread:
        def __init__(self, R):
            self.R = R
            self.zi, self.xi, self.fi = cp.block(5), cp.block(5), cp.block(5)

        def same(self, first, i, place, device):
            view = self.R.at[part(i, place), :]
            return cp.at(first + i, view, view, device)

        def z(self, i):
            return self.same(self.zi, i, at_me, p.dev_z(2))

        def x(self, i):
            return self.same(self.xi, i, at_me, p.dev_x)

        def forward(self, i):
            return self.same(self.fi, i, at_z, p.dev_x)

        def start_part(self, i):
            self.z(i).start()
            self.x(i).start()

        def relay_part(self, i):
            self.z(i).wait()
            self.forward(i).start()

    class Reduce:
        def __init__(self, staging, landing):
            self.put, self.got = PS.at[staging], RB.at[landing]
            self.xi, self.di, self.zi = cp.block(1), cp.block(5), cp.block(5)

        def x(self):
            return cp.at(self.xi, self.put.at[0], self.got.at[0], p.dev_x)

        def d(self, i):
            return cp.at(self.di + i, self.put.at[1, part(i), :], self.got.at[1, part(i), :], p.dev_x)

        def z(self, i):
            return cp.at(self.zi + i, self.put.at[2, part(i), :], self.got.at[2, part(i), :], p.dev_z(2))

        def start_x(self):
            each(lambda i: self.d(i).start())
            self.x().start()

        def relay_part(self, i, own_z):
            self.d(i).wait()
            self.put[2, part(i), :] = (own_z[part(i), :] + self.got[1, part(i), :].astype(F32)).astype(BF)
            self.z(i).start()

        def result_part(self, i, own):
            self.z(i).wait()
            return (
                own[part(i), :]
                + self.got[0, part(i), :].astype(F32)
                + self.got[2, part(i), :].astype(F32)
            )

    g1, g2, g3, g4 = Spread(R1), Spread(R2), Spread(R3), Spread(R4)
    r1, r2, r3, r4 = Reduce(0, 0), Reduce(1, 1), Reduce(0, 2), Reduce(0, 3)
    mine_r = rows_of(at_me)

    R1[mine_r, :] = AA[...].astype(BF)
    each(lambda i: g1.z(i).start())
    each(lambda i: g1.x(i).start())
    R3[mine_r, :] = (gate * GS[...].astype(F32)).astype(BF)
    each(lambda i: g3.z(i).start())
    each(lambda i: g3.x(i).start())

    wait(*ec0[0])
    wait(*ec[0])
    wait(*ez[0])
    ec1 = e_core(0, 1, g)
    wait(*er[0])
    ec2 = e_core(0, 1, p.gx)
    wait(*ec1)
    wait(*ec2)

    def cols_of(q):
        return slice(q * 512, (q + 1) * 512)

    def first_forward(place):
        at = rows_of(place)
        total = None
        for q in (0, 1):
            active, slope = gelu_both(dot(R1[at, :], UP[0, q]))
            GP1[at, cols_of(q)] = slope
            A1[at, cols_of(q)] = active.astype(BF)
            term = dot(active.astype(BF), DN[0, q])
            total = term if total is None else total + term
        return total

    OWN[0] = first_forward(at_me)
    each(g1.relay_part)
    wait(*e1[1])
    er.append(e_relay(1))
    ec.append(e_core(1, 0, p.gx))
    each(lambda i: g1.x(i).wait())
    PS[0, 0] = first_forward(at_x).astype(BF)
    OWN[3] = first_forward(at_z)
    each(lambda i: g1.forward(i).wait())
    PS[0, 1] = first_forward(at_d).astype(BF)
    r1.start_x()
    each(lambda i: r1.relay_part(i, OWN.at[3]))
    r1.x().wait()

    def middle_part(i):
        branch = r1.result_part(i, OWN.at[0])
        SUMS[0, part(i), :] = branch
        R2[part(i, at_me), :] = (AA[part(i), :].astype(BF).astype(F32) + branch).astype(BF)
        g2.start_part(i)

    each(middle_part)
    each(g3.relay_part)

    wait(*ec0[1])
    wait(*ec[1])
    wait(*ez[1])
    ec1 = e_core(1, 1, g)
    wait(*er[1])
    ec2 = e_core(1, 1, p.gx)
    wait(*ec1)
    wait(*ec2)

    def second_grad(place):
        at = rows_of(place)
        total_grad = None
        for q in (0, 1):
            active, slope = gelu_both(dot(R2[at, :], UP[1, q]))
            A2[at, cols_of(q)] = active.astype(BF)
            grad = (slope * dot(R3[at, :], DN[1, q], NT)).astype(BF)
            DH[at, cols_of(q)] = grad
            term = dot(grad, UP[1, q], NT)
            total_grad = term if total_grad is None else total_grad + term
        return total_grad

    def second_forward(place):
        at = rows_of(place)
        return dot(A2[at, :512], DN[1, 0]) + dot(A2[at, 512:], DN[1, 1])

    OWN[2] = second_grad(at_me)
    OWN[1] = second_forward(at_me)
    each(g2.relay_part)
    each(lambda i: g2.x(i).wait())
    each(lambda i: g3.x(i).wait())
    PS[0, 0] = second_grad(at_x).astype(BF)
    OWN[3] = second_grad(at_z)
    each(lambda i: g2.forward(i).wait())
    each(lambda i: g3.forward(i).wait())
    PS[0, 1] = second_grad(at_d).astype(BF)
    r3.start_x()
    PS[1, 1] = second_forward(at_d).astype(BF)
    PS[1, 0] = second_forward(at_x).astype(BF)
    OWN[4] = second_forward(at_z)
    each(lambda i: r3.relay_part(i, OWN.at[3]))
    each(lambda i: r2.d(i).start())

    def weight_grads(A, R, RG, GU, GD):
        def one(q, d):
            qcols = pl.ds(pl.multiple_of(q * 512, 512), 512)
            GU[q, d] = dot(R[:, dq(d)], DH[:, qcols], TN).astype(BF)
            GD[q, d] = dot(A[:, qcols], RG[:, dq(d)], TN).astype(BF)

        def body(t, carry):
            q, k = lax.rem(t, 2), lax.div(t, 2)
            d = lax.rem(k, 2)
            mine_c = lax.div(k, 2)
            cc = p.c * mine_c + (1 - p.c) * (1 - mine_c)
            one(q, 2 * d + cc)
            return carry

        return body

    def to_core(n):
        out = ()
        for k, theirs in enumerate((p.gc, p.gd)):
            out += go(
                cp.new(GU.at[:, theirs], CRU.at[n, :, k], p.dev_c),
                cp.new(GD.at[:, theirs], CRD.at[n, :, k], p.dev_c),
            )
        return out

    def add_core(n, own_u, own_d, far_u, far_d):
        for k, d in enumerate((g, p.gx)):
            far_u[k] = (GU[1, d].astype(F32) + CRU[n, 1, k].astype(F32)).astype(BF)
            far_d[k] = (GD[1, d].astype(F32) + CRD[n, 1, k].astype(F32)).astype(BF)
            own_u[k] = (GU[0, d].astype(F32) + CRU[n, 0, k].astype(F32)).astype(BF)
            own_d[k] = (GD[0, d].astype(F32) + CRD[n, 0, k].astype(F32)).astype(BF)

    body2 = weight_grads(A2, R2, R3, GU, GD)
    lax.fori_loop(0, 4, body2, 0)
    f0 = to_core(0)
    lax.fori_loop(4, 8, body2, 0)

    r3.x().wait()

    def middle_grad_part(i):
        total = r3.result_part(i, OWN.at[2])
        SUMS[1, part(i), :] = total
        R4[part(i, at_me), :] = (R3[part(i, at_me), :].astype(F32) + total).astype(BF)
        g4.start_part(i)

    each(middle_grad_part)
    wait(*f0)
    add_core(0, P2U, P2D, ZSU, ZSD)
    f1 = []
    for k in (0, 1):
        f1 += go(
            cp.new(ZSU.at[k], ZRU.at[k], p.dev_pair),
            cp.new(ZSD.at[k], ZRD.at[k], p.dev_pair),
        )

    each(lambda i: r2.relay_part(i, OWN.at[4]))

    def first_backward(place):
        at = rows_of(place)
        total = None
        for q in (0, 1):
            grad = (GP1[at, cols_of(q)] * dot(R4[at, :], DN[0, q], NT)).astype(BF)
            DH[at, cols_of(q)] = grad
            term = dot(grad, UP[0, q], NT)
            total = term if total is None else total + term
        return total

    OWN[0] = first_backward(at_me)
    each(g4.relay_part)
    r2.x().start()
    each(lambda i: g4.x(i).wait())
    PS[0, 0] = first_backward(at_x).astype(BF)
    OWN[3] = first_backward(at_z)
    each(lambda i: g4.forward(i).wait())
    PS[0, 1] = first_backward(at_d).astype(BF)
    r4.start_x()

    def output_part(i):
        branch_two = r2.result_part(i, OWN.at[1])
        returned = (SUMS[0, part(i), :] + branch_two).astype(BF).astype(F32)
        upstream = GS[part(i), :].astype(F32)
        after = AA[part(i), :]
        gate_part = jax.nn.sigmoid(jnp.sum(after * centroid, axis=1, keepdims=True))
        OUTS[part(i), :] = (after + gate_part * returned).astype(BF)
        score_grad = jnp.sum(upstream * returned, axis=1, keepdims=True) * gate_part * (1.0 - gate_part)
        RES[part(i), :] = upstream + score_grad * centroid
        CGR[...] += jnp.broadcast_to(jnp.sum(score_grad * after, axis=0, keepdims=True), CGR.shape)

    CGR[...] = jnp.zeros_like(CGR)

    each(lambda i: r4.relay_part(i, OWN.at[3]))
    r2.x().wait()
    each(output_part)
    body1 = weight_grads(A1, R1, R4, GU, GD)
    lax.fori_loop(0, 4, body1, 0)
    f0 = to_core(1)
    lax.fori_loop(4, 8, body1, 0)
    r4.x().wait()

    def residual_part(i):
        arrived = (r4.result_part(i, OWN.at[0]) + SUMS[1, part(i), :]).astype(BF)
        RESS[part(i), :] = (RES[part(i), :] + arrived.astype(F32)).astype(BF)

    each(residual_part)
    wait(*f0)
    add_core(1, P1U, P1D, Z1U, Z1D)
    wait(*f1)
    for k in (0, 1):
        S2U[k] = P2U[k].astype(F32) + ZRU[k].astype(F32)
        S2D[k] = P2D[k].astype(F32) + ZRD[k].astype(F32)
    wait(*early)


def backward_kernel(
    xg_in, qkv_in, pr_in, mxh_in, w0_in, w1_in, w2_in, wo_in,
    RT, OUTS, RESS, CGR, P1U, P1D, Z1U, Z1D, S2U, S2D,
    out, tgrad, pgrad, ograd, egrad, ugrad, dgrad,
    XG, QKV, PR, MXH, W0, W1, W2, WO,
    RP, OP, RL, XH, NRM, NRMT, MG, DQ, DT, NG, NGS, NGR,
    ZRU, ZRD, XSU, XSD, XRU, XRD,
    PW0, PW1, PW2, PW3, PC0, PC1, PC2, PC3, PXS0, PXS1, PXS2, PXS3, PXR0, PXR1, PXR2, PXR3,
    PYS0, PYS1, PYS2, PYS3, PK0, PK1, PK2, PK3, PZ0, PZ1, PZ2, PZ3,
    OW, OC, OXS, OXR, OK, OZR, TE,
    send, recv, local,
):
    PW, PC, PXS, PXR = (PW0, PW1, PW2, PW3), (PC0, PC1, PC2, PC3), (PXS0, PXS1, PXS2, PXS3), (PXR0, PXR1, PXR2, PXR3)
    PYS, PK, PZ = (PYS0, PYS1, PYS2, PYS3), (PK0, PK1, PK2, PK3), (PZ0, PZ1, PZ2, PZ3)
    p = Place()
    g, y, w, x = p.g, p.y, p.w, p.x
    cp = Copies(send, recv)
    all_in = greet([p.dev_x, p.dev_c, p.dev_y, p.dev_z(1), p.dev_z(2), p.dev_z(3)])

    def go(*items):
        for item in items:
            item.start()
        return items

    def wait(*items):
        for item in items:
            item.wait()

    loads = [
        copy_in(src, dst, local.at[i])
        for i, (src, dst) in enumerate(
            (
                (xg_in, XG), (w0_in, W0), (wo_in, WO), (mxh_in, MXH),
                (qkv_in, QKV), (pr_in, PR), (w1_in, W1), (w2_in, W2),
            )
        )
    ]
    go(*loads)
    XSU[1] = S2U[1].astype(BF)
    XSD[1] = S2D[1].astype(BF)
    all_in()

    own_slots = pl.ds(pl.multiple_of(y * CAP, 16), CAP)
    peer_slots = pl.ds(pl.multiple_of((1 - y) * CAP, 16), CAP)
    ry = go(cp.new(RESS, RP, p.dev_y))
    oy = go(cp.new(OUTS.at[peer_slots, :], OP, p.dev_y))

    f1 = []
    for k in (1, 0):
        f1 += go(
            cp.new(Z1U.at[k], ZRU.at[k], p.dev_pair),
            cp.new(Z1D.at[k], ZRD.at[k], p.dev_pair),
        )
    f2 = {1: go(cp.new(XSU.at[1], XRU.at[1], p.dev_x), cp.new(XSD.at[1], XRD.at[1], p.dev_x))}

    half = pl.ds(pl.multiple_of(x * 512, 512), 512)
    other = pl.ds(pl.multiple_of((1 - x) * 512, 512), 512)

    wait(loads[0], loads[1])
    values = XG[...].astype(F32)
    centred = values - jnp.mean(values, axis=1, keepdims=True)
    inverse = lax.rsqrt(jnp.mean(centred * centred, axis=1, keepdims=True) + 1e-05)
    XH[...] = centred * inverse
    pick = one_hot(8, EXTRA)
    gain = dot(pick, W0[:, 512:], NT)[0:1, :]
    NRM[...] = (XH[...] * gain).astype(BF)
    NRMT[...] = NRM[...].T
    ugrad[1, :, half] = S2U[0]
    dgrad[1, half, :] = S2D[0]

    wait(*ry)
    for b in (0, 1):
        slots = slice(b * CAP, (b + 1) * CAP)
        RL[b * 128 : (b + 1) * 128, :] = (
            dot(dispatch_block(RT[b], y), RESS[slots, :], TN)
            + dot(dispatch_block(RT[b], 1 - y), RP[slots, :], TN)
        ).astype(BF)
    wait(loads[2])
    MG[...] = dot(RL[...], WO[y], NT).astype(BF)

    def rows4(d):
        return pl.ds(pl.multiple_of(d * 128, 128), 128)

    def dq(d):
        return pl.ds(pl.multiple_of(d * 256, 256), 256)

    def row32(v):
        return pl.ds(pl.multiple_of(v * 32, 32), 32)

    def out_rows(d):
        OW[rows4(d), :] = dot(MXH[y, :, rows4(d)], RL[...], TN).astype(BF)

    low_half = lax.broadcasted_iota(jnp.int32, (256, 128), 1) < 64

    def heads(t):
        c0 = slice(t * 128, (t + 1) * 128)
        c1 = slice(512 + t * 128, 512 + (t + 1) * 128)
        c2 = slice(1024 + t * 128, 1024 + (t + 1) * 128)
        q2, k2, v2, m2 = QKV[:, c0], QKV[:, c1], QKV[:, c2], MG[:, c0]
        parts = []
        for i in (0, 1):
            keep = low_half if i == 0 else ~low_half
            probs = PR[2 * t + i]
            probs_grad = dot(jnp.where(keep, m2, jnp.zeros_like(m2)), v2, NT)
            delta = jnp.sum(probs_grad * probs, axis=1, keepdims=True)
            scores_grad = (probs * (probs_grad - delta)).astype(BF)
            parts.append(
                (
                    dot(scores_grad, k2) * 0.125,
                    dot(scores_grad, q2, TN) * 0.125,
                    dot(probs.astype(BF), m2, TN),
                )
            )
        for s, c in enumerate((c0, c1, c2)):
            grad = jnp.where(low_half, parts[0][s], parts[1][s]).astype(BF)
            DQ[:, c] = grad
            DT[t, :, s * 128 : (s + 1) * 128] = grad

    pc, px, py, pz = [None] * 4, [None] * 4, [None] * 4, [None] * 4

    def to_core(t):
        PW[t][:, :384] = dot(NRMT[...], DT[t]).astype(BF)
        pc[t] = sum(
            (go(cp.new(PW[t].at[dq(d), :], PC[t].at[k], p.dev_c)) for k, d in enumerate((p.gc, p.gd))), ()
        )

    def to_x(t):
        wait(*pc[t])
        PXS[t][...] = (PW[t][dq(p.gx), :].astype(F32) + PC[t][1].astype(F32)).astype(BF)
        px[t] = go(cp.new(PXS[t], PXR[t], p.dev_x))

    def summed(t, plane):
        rows = rows4(plane)
        full = pl.ds(pl.multiple_of(g * 256 + plane * 128, 128), 128)
        total = PW[t][full, :].astype(F32) + PC[t][0, rows, :].astype(F32) + PXR[t][rows, :].astype(F32)
        return total.astype(BF)

    def to_y(t):
        wait(*px[t])
        PYS[t][...] = summed(t, 1 - y)
        py[t] = go(cp.new(PYS[t], PK[t].at[1], p.dev_y))
        PK[t][0] = summed(t, y)

    def to_z(t):
        wait(*py[t])
        pz[t] = sum(
            (
                go(cp.new(PK[t].at[:, row32(lax.rem(w + k, 4)), :], PZ[t].at[k - 1], p.dev_z(k)))
                for k in (2, 1, 3)
            ),
            (),
        )

    wait(loads[4], loads[5])
    heads(0)
    to_core(0)
    wait(loads[3])
    out_rows(p.gc)
    out_rows(p.gd)
    oc = sum((go(cp.new(OW.at[rows4(d), :], OC.at[k], p.dev_c)) for k, d in enumerate((p.gc, p.gd))), ())
    heads(1)
    to_core(1)
    to_x(0)
    out_rows(g)
    out_rows(p.gx)
    heads(2)
    to_core(2)
    to_x(1)
    wait(*oc)
    for k, d in enumerate((g, p.gx)):
        OK[k] = (OW[rows4(d), :].astype(F32) + OC[k].astype(F32)).astype(BF)
    oz = sum(
        (go(cp.new(OK.at[:, row32(lax.rem(w + k, 4)), :], OZR.at[k - 1], p.dev_z(k))) for k in (2, 1, 3)), ()
    )
    own32 = row32(w)
    heads(3)

    wait(loads[6], loads[7])
    NG[...] = (
        dot(DQ[:, :512], W0[:, :512], NT) + dot(DQ[:, 512:1024], W1[...], NT) + dot(DQ[:, 1024:], W2[...], NT)
    )
    NGS[...] = NG[rows4(1 - y), :].astype(BF)
    ny = go(cp.new(NGS, NGR, p.dev_y))
    gain_row = jnp.sum(NG[...] * XH[...], axis=0, keepdims=True)
    line = lax.broadcasted_iota(jnp.int32, (8, 1024), 0)
    stack = jnp.where(line == 0, gain_row, jnp.where(line == 1 + y, CGR[0:1, :], 0.0)).astype(BF)
    PW3[:, 384:] = dot(stack, pick, TN).astype(BF)
    to_core(3)
    to_x(2)
    to_y(0)
    to_x(3)
    to_y(1)
    to_z(0)

    wait(*oz)

    def out_sum(k):
        return (
            OK[k, own32, :].astype(F32)
            + OZR[0, k].astype(F32)
            + OZR[1, k].astype(F32)
            + OZR[2, k].astype(F32)
        )

    OXS[...] = out_sum(1).astype(BF)
    ox = go(cp.new(OXS, OXR, p.dev_x))

    wait(*ny)
    own_rows = rows4(y)
    normed = XH[own_rows, :]
    mine = XG[own_rows, :].astype(F32)
    mine = mine - jnp.mean(mine, axis=1, keepdims=True)
    inverse = lax.rsqrt(jnp.mean(mine * mine, axis=1, keepdims=True) + 1e-05)
    scaled = (NG[own_rows, :] + NGR[...].astype(F32)) * gain
    tgrad[...] = RL[own_rows, :].astype(F32) + inverse * (
        scaled
        - jnp.mean(scaled, axis=1, keepdims=True)
        - normed * jnp.mean(scaled * normed, axis=1, keepdims=True)
    )
    to_y(2)
    to_z(1)

    wait(*f1)
    XSU[0] = (P1U[1].astype(F32) + ZRU[1].astype(F32)).astype(BF)
    XSD[0] = (P1D[1].astype(F32) + ZRD[1].astype(F32)).astype(BF)
    f2[0] = go(cp.new(XSU.at[0], XRU.at[0], p.dev_x), cp.new(XSD.at[0], XRD.at[0], p.dev_x))
    wait(*oy)
    route_own = RT[y]
    out[...] = (
        dot(dispatch_block(route_own, y), OUTS[own_slots, :], TN)
        + dot(dispatch_block(route_own, 1 - y), OP[...], TN)
    ).astype(BF)
    to_y(3)
    to_z(2)
    ugrad[0, :, half] = P1U[0].astype(F32) + ZRU[0].astype(F32)
    dgrad[0, half, :] = P1D[0].astype(F32) + ZRD[0].astype(F32)
    wait(*f2[1])
    ugrad[1, :, other] = XRU[1].astype(F32)
    dgrad[1, other, :] = XRD[1].astype(F32)
    to_z(3)

    for t in range(4):
        wait(*pz[t])
        sums = [
            PK[t][i, own32, :].astype(F32)
            + PZ[t][0, i].astype(F32)
            + PZ[t][1, i].astype(F32)
            + PZ[t][2, i].astype(F32)
            for i in (0, 1)
        ]
        for plane in (0, 1):
            kept = jnp.where(y == plane, sums[0], sums[1])
            for s in range(3):
                first = s * 1024 + t * 256 + plane * 128
                pgrad[:, first : first + 128] = kept[:, s * 128 : (s + 1) * 128]
        if t == 3:
            TE[0:32, :] = sums[0][:, 384:] + sums[1][:, 384:]
    egrad[...] = TE[...].T[0:8, :]
    wait(*f2[0])
    ugrad[0, :, other] = XRU[0].astype(F32)
    dgrad[0, other, :] = XRD[0].astype(F32)
    wait(*ox)
    ograd[...] = out_sum(0) + OXR[...].astype(F32)


def finish_kernel(
    out, tgrad, pgrad, ograd, egrad, ugrad, dgrad, out2, tgrad2, gain, pgrad2, ograd2, cent, ugrad2, dgrad2
):
    out2[0] = out[...]
    tgrad2[0] = tgrad[...]
    pgrad2[...] = pgrad[...]
    ograd2[...] = ograd[...]
    gain[...] = egrad[0:1, :32]
    cent[...] = egrad[1:3, :32]
    ugrad2[0] = ugrad[...]
    dgrad2[0] = dgrad[...]


def vmem(shape, dtype=BF):
    return pltpu.VMEM(shape, dtype)


def fast_shards(
    tokens, cotangent, norm_gain, project_weight, output_weight, centroids,
    expert_up, expert_down, sequence_lengths, block_order, routes,
):
    in_vmem = pl.BlockSpec(memory_space=pltpu.VMEM)
    in_any = pl.BlockSpec(memory_space=pl.ANY)
    in_smem = pl.BlockSpec(memory_space=pltpu.SMEM)
    shape = jax.ShapeDtypeStruct
    ext = jnp.pad(
        jnp.concatenate([norm_gain[None], centroids], axis=0).astype(F32), ((0, 5), (0, EXTRA - 32))
    )
    mid_shapes = [
        ((256, 1024), BF),
        ((256, 1536), BF),
        ((8, 256, 256), F32),
        ((2, 256, 512), BF),
        ((1024, 512 + EXTRA), BF),
        ((1024, 512), BF),
        ((1024, 512), BF),
        ((2, 512, 1024), BF),
        ((2, 8, 128), F32),
        ((160, 1024), BF),
        ((160, 1024), BF),
        ((8, 1024), F32),
        ((2, 256, 512), BF),
        ((2, 512, 256), BF),
        ((2, 256, 512), BF),
        ((2, 512, 256), BF),
        ((2, 256, 512), F32),
        ((2, 512, 256), F32),
    ]
    mid = pl.pallas_call(
        forward_kernel,
        name="forward",
        out_shape=[shape(*s) for s in mid_shapes],
        in_specs=[in_smem] * 2 + [in_vmem] * 6 + [in_any] * 2,
        out_specs=[in_any] * 8 + [in_vmem] * (len(mid_shapes) - 8),
        scratch_shapes=[vmem(*s) for s in mid_shapes[:8]]
        + [
            vmem((2, 32, 512 + EXTRA)),
            vmem((2, 32, 512)),
            vmem((2, 32, 512)),
            vmem((256, 1024)),
            vmem((256, 1024), F32),
            vmem((256, 1024)),
            vmem((2, 2, 1024, 512)),
            vmem((2, 2, 512, 1024)),
            vmem((2, CAP, 128)),
            vmem((160, 1024), F32),
            vmem((160, 1024)),
            vmem((2, 160, 512)),
            vmem((160, 1024), F32),
        ]
        + [vmem((640, 1024))] * 4
        + [
            vmem((4, 3, 160, 1024)),
            vmem((2, 3, 160, 1024)),
            vmem((5, 160, 1024), F32),
            vmem((160, 1024), F32),
            vmem((640, 1024), F32),
            vmem((640, 1024)),
            vmem((640, 1024)),
            vmem((640, 1024)),
            vmem((2, 160, 1024), F32),
            vmem((2, 4, 256, 512)),
            vmem((2, 4, 512, 256)),
            vmem((2, 2, 2, 256, 512)),
            vmem((2, 2, 2, 512, 256)),
            vmem((2, 256, 512)),
            vmem((2, 512, 256)),
            vmem((2, 256, 512)),
            vmem((2, 512, 256)),
            vmem((2, 256, 512)),
            vmem((2, 512, 256)),
            pltpu.SemaphoreType.DMA((208,)),
            pltpu.SemaphoreType.DMA((208,)),
            pltpu.SemaphoreType.DMA((24,)),
        ],
        compiler_params=pltpu.CompilerParams(
            collective_id=0, has_side_effects=True, vmem_limit_bytes=VMEM_LIMIT
        ),
    )(
        sequence_lengths[0], block_order[0], tokens[0], cotangent[0], routes.reshape(1, 128),
        project_weight, output_weight, ext, expert_up[0], expert_down[0],
    )
    out_shapes = [
        ((128, 1024), BF),
        ((128, 1024), F32),
        ((32, 3072), F32),
        ((32, 1024), F32),
        ((8, EXTRA), F32),
        ((2, 256, 1024), F32),
        ((2, 1024, 256), F32),
    ]
    out, tgrad, pgrad, ograd, egrad, ugrad, dgrad = pl.pallas_call(
        backward_kernel,
        name="backward",
        out_shape=[shape(*s) for s in out_shapes],
        in_specs=[in_any] * 8 + [in_vmem] * (len(mid_shapes) - 8),
        out_specs=[in_vmem] * len(out_shapes),
        scratch_shapes=[vmem(*s) for s in mid_shapes[:8]]
        + [
            vmem((160, 1024)),
            vmem((CAP, 1024)),
            vmem((256, 1024)),
            vmem((256, 1024), F32),
            vmem((256, 1024)),
            vmem((1024, 256)),
            vmem((256, 512)),
            vmem((256, 1536)),
            vmem((4, 256, 384)),
            vmem((256, 1024), F32),
            vmem((128, 1024)),
            vmem((128, 1024)),
            vmem((2, 256, 512)),
            vmem((2, 512, 256)),
            vmem((2, 256, 512)),
            vmem((2, 512, 256)),
            vmem((2, 256, 512)),
            vmem((2, 512, 256)),
        ]
        + [vmem((1024, c)) for c in CHUNKS]
        + [vmem((2, 256, c)) for c in CHUNKS]
        + [vmem((256, c)) for c in CHUNKS]
        + [vmem((256, c)) for c in CHUNKS]
        + [vmem((128, c)) for c in CHUNKS]
        + [vmem((2, 128, c)) for c in CHUNKS]
        + [vmem((3, 2, 32, c)) for c in CHUNKS]
        + [
            vmem((512, 1024)),
            vmem((2, 128, 1024)),
            vmem((32, 1024)),
            vmem((32, 1024)),
            vmem((2, 128, 1024)),
            vmem((3, 2, 32, 1024)),
            vmem((EXTRA, EXTRA), F32),
            pltpu.SemaphoreType.DMA((64,)),
            pltpu.SemaphoreType.DMA((64,)),
            pltpu.SemaphoreType.DMA((8,)),
        ],
        compiler_params=pltpu.CompilerParams(
            collective_id=1, has_side_effects=True, vmem_limit_bytes=VMEM_LIMIT
        ),
    )(*mid)
    out, tgrad, gain, pgrad, ograd, cent, ugrad, dgrad = pl.pallas_call(
        finish_kernel,
        name="finish",
        out_shape=[
            shape((1, 128, 1024), BF),
            shape((1, 128, 1024), F32),
            shape((1, 32), F32),
            shape((32, 3072), F32),
            shape((32, 1024), F32),
            shape((2, 32), F32),
            shape((1, 2, 256, 1024), F32),
            shape((1, 2, 1024, 256), F32),
        ],
        in_specs=[in_vmem] * 7,
        out_specs=[in_vmem] * 8,
        compiler_params=pltpu.CompilerParams(vmem_limit_bytes=VMEM_LIMIT),
    )(out, tgrad, pgrad, ograd, egrad, ugrad, dgrad)
    return out, tgrad, gain[0], pgrad, ograd, cent, ugrad, dgrad


def solution(mesh):
    sizes = dict(mesh.shape)
    fast = sizes == {"grp": 4, "ctx": 2, "wsh": 4}
    return jax.shard_map(
        fast_shards if fast else shards,
        mesh=mesh,
        in_specs=IN_SPECS,
        out_specs=OUT_SPECS,
        check_vma=False,
    )
```
